32 devices in a mesh: dp: 8 (over y, x, core), tensor: 4 (over z).
Axes of the slice: x: 2, y: 2, z: 4, core: 2. Of those that a mesh axis runs over, the one named last changes fastest.
Arguments:
- inputs: bfloat16 [16, 1024, 1024], P('dp', 'tensor'), may hold values from -6 to 6
- query_weight: bfloat16 [1024, 1024], P(None, 'tensor'), may hold values from -0.1875 to 0.1875
- key_weight: bfloat16 [1024, 512], P(None, 'tensor'), may hold values from -0.1875 to 0.1875
- value_weight: bfloat16 [1024, 512], P(None, 'tensor'), may hold values from -0.1875 to 0.1875
- out_weight: bfloat16 [1024, 1024], P('tensor'), may hold values from -1.5 to 1.5
- gate_weight: bfloat16 [1024, 4608], P(None, 'tensor'), may hold values from -0.1875 to 0.1875
- up_weight: bfloat16 [1024, 4608], P(None, 'tensor'), may hold values from -0.1875 to 0.1875
- down_weight: bfloat16 [4608, 1024], P('tensor'), may hold values from -0.1875 to 0.1875
- attn_gain: float32 [1024], replicated, may hold values from 0.5 to 1.5
- ffn_gain: float32 [1024], replicated, may hold values from 0.5 to 1.5
- query_gain: float32 [64], replicated, may hold values from 0.5 to 1.5
- key_gain: float32 [64], replicated, may hold values from 0.5 to 1.5
- cotangent: bfloat16 [16, 1024, 1024], P('dp', 'tensor'), may hold values from -6 to 6
- segment_ids: int32 [16, 1024], P('dp'), may hold values from 0 to 1023, as said below
- padding: int32 [16, 1024], P('dp'), may hold values from 0 to 1, as said below
- row_count: int32 [8], P('dp'), may hold values from 1 to 2, as said below
Outputs:
- outputs: bfloat16 [16, 1024, 1024], P('dp', 'tensor')
- input_grad: float32 [16, 1024, 1024], P('dp', 'tensor')
- query_grad: float32 [1024, 1024], P('dp', 'tensor')
- key_grad: float32 [1024, 512], P('dp', 'tensor')
- value_grad: float32 [1024, 512], P('dp', 'tensor')
- out_grad: float32 [1024, 1024], P(('tensor', 'dp'))
- gate_grad: float32 [1024, 4608], P('dp', 'tensor')
- up_grad: float32 [1024, 4608], P('dp', 'tensor')
- down_grad: float32 [4608, 1024], P(('tensor', 'dp'))
- attn_gain_grad: float32 [1024], replicated
- ffn_gain_grad: float32 [1024], replicated
- query_gain_grad: float32 [64], replicated
- key_gain_grad: float32 [64], replicated
The draws below stay inside these ranges and needn't reach their ends.
Inputs may be any that keep to these rules, and one draw needn't show every extreme that they name: `segment_ids`: within each row the ids start at 0 and never fall; a document is a run of equal ids. The last position of each row is a document of its own, numbered 1024 - 1. `padding`: each row is 1 on a prefix and 0 after it. `row_count`: some device holds 2 rows and some other device 1 in every draw.
All inputs are finite; a program needn't handle non-finite values.
Results may differ from the reference program's by a relative error of at most 0.02.
Values may be sent and summed in bfloat16 or wider, within the bound.
A program may use at most 256 MiB of HBM per device.

```python
import jax
import jax.numpy as jnp
from jax import lax

D = 1024
HQ = 16
KV = 8
HD = 64
FF = 4608
SEQ = 1024
SLOTS = 2
ROWS = 16
N_DP = 8


def draw_segment_ids(key, part):
    key = jax.random.fold_in(key, 37)
    rate_key, flag_key = jax.random.split(key)
    rate_pick = jax.random.randint(rate_key, (ROWS, 1), 0, 4)
    spans = jnp.power(4, rate_pick + 1)
    raw_draws = jax.random.randint(flag_key, (ROWS, SEQ), 0, 1 << 20)
    places = jnp.arange(SEQ, dtype=jnp.int32)[None, :]
    row_index = jnp.arange(ROWS, dtype=jnp.int32)[:, None]
    starts = raw_draws % spans == 0
    long_row = row_index % SLOTS == 0
    starts = jnp.where(long_row & (places < SEQ * 7 // 8), False, starts)
    starts = starts | (places == 0) | (places == SEQ - 1)
    numbered = (jnp.cumsum(starts.astype(jnp.int32), axis=1) - 1).astype(jnp.int32)
    final_id = numbered[:, SEQ - 1:SEQ]
    return jnp.where(numbered == final_id, SEQ - 1, numbered).astype(jnp.int32)


def draw_padding(key, part):
    key = jax.random.fold_in(key, 23)
    cut_count = jax.random.randint(key, (ROWS, 1), 0, SEQ // 8 + 1)
    places = jnp.arange(SEQ, dtype=jnp.int32)[None, :]
    return (places < SEQ - cut_count).astype(jnp.int32)


def draw_row_count(key, part):
    key = jax.random.fold_in(key, 11)
    count_key, busy_key, other_key = jax.random.split(key, 3)
    counts = jax.random.randint(count_key, (N_DP,), 1, SLOTS + 1)
    busiest = jax.random.randint(busy_key, (), 0, N_DP)
    lightest = (busiest + 1 + jax.random.randint(other_key, (), 0, N_DP - 1)) % N_DP
    places = jnp.arange(N_DP, dtype=jnp.int32)
    counts = jnp.where(places == busiest, SLOTS, counts)
    counts = jnp.where(places == lightest, 1, counts)
    return counts.astype(jnp.int32)


def block_levels(own_key, shape, cuts, least, high):
    factor_of = 1.0
    for position, parts in cuts:
        heights = jax.random.uniform(jax.random.fold_in(jax.random.fold_in(own_key, 6), position), (parts,), jnp.float32, least / len(cuts), high / len(cuts))
        factor_of = factor_of * jnp.repeat(jnp.exp(heights), shape[position] // parts).reshape((-1,) + (1,) * (len(shape) - 1 - position))
    return factor_of


def noise(key, dims, deviation, reach, cuts=(), kind=jnp.bfloat16):
    drawn = deviation * jax.random.normal(key, dims, jnp.float32)
    if cuts:
        drawn = drawn * block_levels(key, dims, cuts, -0.22, 0.18)
    return jnp.clip(drawn, -reach, reach).astype(kind)


def setup_inputs(seed: int = 0) -> dict:
    streams_of = jax.random.split(jax.random.key(seed), 17)
    inputs = noise(streams_of[0], (ROWS, SEQ, D), 1.0, 6.0, ((0, 8), (1, 4)))
    query_weight = noise(streams_of[1], (D, HQ * HD), D ** -0.5, 0.1875, ((1, 4),))
    key_weight = noise(streams_of[2], (D, KV * HD), D ** -0.5, 0.1875, ((1, 4),))
    value_weight = noise(streams_of[3], (D, KV * HD), D ** -0.5, 0.1875, ((1, 4),))
    out_weight = noise(streams_of[4], (HQ * HD, D), (HQ * HD // 64) ** -0.5, 1.5, ((0, 4),))
    gate_weight = noise(streams_of[5], (D, FF), D ** -0.5, 0.1875, ((1, 4),))
    up_weight = noise(streams_of[6], (D, FF), D ** -0.5, 0.1875, ((1, 4),))
    down_weight = noise(streams_of[7], (FF, D), (FF // 4) ** -0.5, 0.1875, ((0, 4),))
    attn_gain = jnp.clip(1.0 + 0.1 * jax.random.normal(streams_of[8], (D,), jnp.float32), 0.5, 1.5)
    ffn_gain = jnp.clip(1.0 + 0.1 * jax.random.normal(streams_of[9], (D,), jnp.float32), 0.5, 1.5)
    query_gain = jnp.clip(1.0 + 0.1 * jax.random.normal(streams_of[10], (HD,), jnp.float32), 0.5, 1.5)
    key_gain = jnp.clip(1.0 + 0.1 * jax.random.normal(streams_of[11], (HD,), jnp.float32), 0.5, 1.5)
    cotangent = noise(streams_of[12], (ROWS, SEQ, D), 1.0, 6.0, ((0, 8), (1, 4)))
    segment_ids = draw_segment_ids(jax.random.fold_in(streams_of[16], 71), 0)
    padding = draw_padding(jax.random.fold_in(streams_of[16], 71), 0)
    row_count = draw_row_count(jax.random.fold_in(streams_of[16], 71), 0)
    return dict(inputs=inputs, query_weight=query_weight, key_weight=key_weight, value_weight=value_weight, out_weight=out_weight, gate_weight=gate_weight, up_weight=up_weight, down_weight=down_weight, attn_gain=attn_gain, ffn_gain=ffn_gain, query_gain=query_gain, key_gain=key_gain, cotangent=cotangent, segment_ids=segment_ids, padding=padding, row_count=row_count)


EPS = 1e-05
THETA = 1000000.0
MASKED = -1e+30
HIGH = lax.Precision.HIGHEST

@jax.custom_vjp
def low(v):
    return lax.optimization_barrier(v.astype(jnp.bfloat16)).astype(jnp.float32)

@jax.custom_vjp
def low_back(v):
    return v

def low_keep(v):
    return (low(v), None)

def low_pass(kept, grad):
    return (grad,)

def back_keep(v):
    return (v, None)

def back_low(kept, grad):
    return (low(grad),)
low.defvjp(low_keep, low_pass)
low_back.defvjp(back_keep, back_low)

def norm_rows(values, gain):
    return values * lax.rsqrt(lax.optimization_barrier(jnp.mean(values * values, axis=-1, keepdims=True)) + EPS) * gain

def rope_tables(length, width):
    half_width = width // 2
    frequency = THETA ** (-(2.0 * jnp.arange(half_width, dtype=jnp.float32)) / width)
    angles = jnp.arange(length, dtype=jnp.float32)[:, None] * frequency[None, :]
    return (jnp.cos(angles), jnp.sin(angles))

def rotate(values, cos_table, sin_table):
    half_width = values.shape[-1] // 2
    leading = values[..., :half_width]
    trailing = values[..., half_width:]
    cos_part = cos_table[:, None, :]
    sin_part = sin_table[:, None, :]
    return jnp.concatenate([leading * cos_part - trailing * sin_part, trailing * cos_part + leading * sin_part], axis=-1)

def forward(weights, rows_in, alive_mask, segment):
    query_weight, key_weight, value_weight, out_weight, gate_weight, up_weight, down_weight, attn_gain, ffn_gain, query_gain, key_gain = weights
    batch_size = rows_in.shape[0]
    normed = low(norm_rows(rows_in, attn_gain))
    query_proj = low_back(jnp.einsum('bsd,de->bse', normed, query_weight, precision=HIGH)).reshape(batch_size, SEQ, HQ, HD)
    key_proj = low_back(jnp.einsum('bsd,de->bse', normed, key_weight, precision=HIGH)).reshape(batch_size, SEQ, KV, HD)
    values = low_back(low(jnp.einsum('bsd,de->bse', normed, value_weight, precision=HIGH))).reshape(batch_size, SEQ, KV, HD)
    cos_table, sin_table = rope_tables(SEQ, HD)
    queries = low_back(low(rotate(norm_rows(query_proj, query_gain), cos_table, sin_table)))
    keys_all = low_back(low(rotate(norm_rows(key_proj, key_gain), cos_table, sin_table)))
    grouped = queries.reshape(batch_size, SEQ, KV, HQ // KV, HD)
    scores = low_back(jnp.einsum('bigrd,bjgd->bgrij', grouped, keys_all, precision=HIGH) * HD ** (-0.5))
    places = jnp.arange(SEQ, dtype=jnp.int32)
    itself = places[:, None] == places[None, :]
    earlier = places[None, :] < places[:, None]
    same_doc = segment[:, :, None] == segment[:, None, :]
    allowed = itself[None] | earlier[None] & same_doc & (alive_mask[:, None, :] > 0)
    scores = jnp.where(allowed[:, None, None], scores, MASKED)
    attention = low(jax.nn.softmax(scores, axis=-1))
    attended = jnp.einsum('bgrij,bjgd->bigrd', attention, values, precision=HIGH).reshape(batch_size, SEQ, HQ * HD)
    attended = low_back(low(attended))
    branch = low_back(jnp.einsum('bse,ed->bsd', attended, out_weight, precision=HIGH))
    hidden = rows_in + branch
    normed_two = low(norm_rows(hidden, ffn_gain))
    gate_value = low_back(jnp.einsum('bsd,df->bsf', normed_two, gate_weight, precision=HIGH))
    upward = low_back(jnp.einsum('bsd,df->bsf', normed_two, up_weight, precision=HIGH))
    active = low(jax.nn.silu(gate_value) * upward)
    return hidden + low_back(jnp.einsum('bsf,fd->bsd', active, down_weight, precision=HIGH))

def reference(inputs, query_weight, key_weight, value_weight, out_weight, gate_weight, up_weight, down_weight, attn_gain, ffn_gain, query_gain, key_gain, cotangent, segment_ids, padding, row_count):
    weights = tuple((matrix.astype(jnp.float32) for matrix in (query_weight, key_weight, value_weight, out_weight, gate_weight, up_weight, down_weight, attn_gain, ffn_gain, query_gain, key_gain)))
    row_used = (jnp.arange(SLOTS, dtype=jnp.int32)[None, :] < row_count[:, None]).astype(jnp.int32).reshape(ROWS)
    alive_mask = padding * row_used[:, None]
    groups = ROWS // SLOTS
    stacked = (inputs.astype(jnp.float32).reshape(groups, SLOTS, SEQ, D), cotangent.astype(jnp.float32).reshape(groups, SLOTS, SEQ, D), alive_mask.reshape(groups, SLOTS, SEQ), segment_ids.reshape(groups, SLOTS, SEQ))

    def one_group(totals, pieces):
        rows_in, grads_in, alive_group, segment_group = pieces

        def layer(params, tokens):
            return forward(params, tokens, alive_group, segment_group)
        result, pullback = jax.vjp(layer, weights, rows_in)
        weight_grads, row_grads = pullback(grads_in * alive_group[..., None].astype(jnp.float32))
        totals = jax.tree.map(jnp.add, totals, weight_grads)
        return (totals, (result.astype(jnp.bfloat16), row_grads))
    zeros = jax.tree.map(jnp.zeros_like, weights)
    totals, (outputs, input_grads) = lax.scan(one_group, zeros, stacked)
    return (outputs.reshape(ROWS, SEQ, D), input_grads.reshape(ROWS, SEQ, D), totals[0], totals[1], totals[2], totals[3], totals[4], totals[5], totals[6], totals[7], totals[8], totals[9], totals[10])
```

```python
import functools

import jax
import jax.numpy as jnp
from jax import lax
from jax.experimental import pallas as pl
from jax.experimental.pallas import tpu as pltpu
from jax.sharding import PartitionSpec as P

EPS = 1e-05
THETA = 1000000.0
MASKED = -1e30
row_block = 512
ALIVE = 4096
MESH = pl.DeviceIdType.MESH
BF16 = jnp.bfloat16
F32 = jnp.float32


class Place:
    def __init__(self):
        self.dp = lax.axis_index("dp")
        self.z = lax.axis_index("tensor")
        self.c = lax.rem(self.dp, 2)
        self.j = lax.rem(self.dp // 2, 4)
        self.half = self.z // 2
        self.par = lax.rem(self.z, 2)
        self.near = self.half == self.c

    def plane(self, k):
        j = self.j
        bit = lax.rem(j // k, 2)
        return (self.dp + (1 - 2 * bit) * 2 * k, self.z)

    def column(self, c, z):
        return (self.dp - self.c + c, z)

    def quarter(self, k):
        j = self.j
        low, high = lax.rem(j, 2), j // 2
        if k & 1:
            low = 1 - low
        if k & 2:
            high = 1 - high
        return 2 * high + low


def greet(place):
    barrier = pltpu.get_barrier_semaphore()
    for k in (1, 2):
        pl.semaphore_signal(barrier, inc=1, device_id=place.plane(k), device_id_type=MESH)
    for dc in range(2):
        for dz in range(4):
            if dc or dz:
                c = lax.rem(place.c + dc, 2)
                z = lax.rem(place.z + dz, 4)
                pl.semaphore_signal(barrier, inc=1, device_id=place.column(c, z), device_id_type=MESH)
    pl.semaphore_wait(barrier, 9)


def remote(src, dst, send, recv, device):
    return pltpu.make_async_remote_copy(
        src_ref=src, dst_ref=dst, send_sem=send, recv_sem=recv, device_id=device, device_id_type=MESH
    )


def gather_kernel(nw, x_ref, ct_ref, *refs):
    shards = refs[:nw]
    xo, co = refs[nw : nw + 2]
    full = refs[nw + 2 : 2 * nw + 2]
    tok_s, tok_r, tok_l, own_l, zs, zr, fs, fr = refs[2 * nw + 2 :]
    place = Place()
    z, c, par, near, j = place.z, place.c, place.par, place.near, place.j
    seg = x_ref.shape[1]
    greet(place)

    def token_copies(a, src, dst, go):
        for b in range(2):
            slot = par if b == 0 else 1 - par
            target = place.column(place.half, 2 * c + slot)
            here = dst.at[pl.ds(pl.multiple_of(par * seg, seg), seg)]
            if b == 0:
                @pl.when(near)
                def _():
                    cp = pltpu.make_async_copy(src.at[slot], here, tok_l.at[a])
                    cp.start() if go else cp.wait()

                @pl.when(jnp.logical_not(near))
                def _():
                    cp = remote(src.at[slot], here, tok_s.at[a, b], tok_r.at[a, par], target)
                    cp.start() if go else cp.wait_send()
            else:
                cp = remote(src.at[slot], here, tok_s.at[a, b], tok_r.at[a, par], target)
                cp.start() if go else cp.wait_send()

    def token_arrivals(a, src, dst):
        for h in range(2):
            @pl.when(jnp.logical_not(near & (par == h)))
            def _():
                remote(src.at[0], dst.at[pl.ds(h * seg, seg)], tok_s.at[a, 0], tok_r.at[a, h], place.plane(1)).wait_recv()

    def z_copies(w, go):
        q = shards[w].shape[0] // 4
        rows = pl.ds(pl.multiple_of(j * q, q), q)

        @pl.when(near)
        def _():
            cp = pltpu.make_async_copy(shards[w], full[w].at[par], own_l.at[w])
            cp.start() if go else cp.wait()
            far = 2 - 2 * place.half
            for i, to in enumerate((2 * place.half + 1 - par, far + par, far + 1 - par)):
                cp = remote(shards[w].at[rows], full[w].at[par, rows], zs.at[w, i], zr.at[w, par], place.column(c, to))
                cp.start() if go else cp.wait_send()

    def part(w, p, k, half=None):
        q = shards[w].shape[0] // 4
        start, size = pl.multiple_of(place.quarter(k) * q, q), q
        if half is not None:
            size = q // 2
            start = pl.multiple_of(start + half * size, size)
        return full[w].at[p, pl.ds(start, size)]

    def missing(p, body):
        pl.when(jnp.logical_or(jnp.logical_not(near), par != p))(body)

    def step_copy(w, p, i):
        k, half, to = ((0, None, 1), (0, None, 2), (1, 0, 2), (2, 1, 1))[i]
        return remote(part(w, p, k, half), part(w, p, k, half), fs.at[w, p, i], fr.at[w, p, i], place.plane(to))

    token_copies(0, x_ref, xo, True)
    for w in range(nw):
        z_copies(w, True)
        if w == 1:
            token_copies(1, ct_ref, co, True)

    def first(w):
        for p in range(2):
            @functools.partial(missing, p)
            def _():
                remote(part(w, p, 0), part(w, p, 0), zs.at[w, 0], zr.at[w, p], place.plane(1)).wait_recv()
                step_copy(w, p, 0).start()
                step_copy(w, p, 1).start()

    def second(w):
        for p in range(2):
            @functools.partial(missing, p)
            def _():
                step_copy(w, p, 0).wait_recv()
                step_copy(w, p, 2).start()
                step_copy(w, p, 1).wait_recv()
                step_copy(w, p, 3).start()

    for w in range(nw + 1):
        if w < nw:
            first(w)
        if w:
            second(w - 1)
    for w in range(nw):
        for p in range(2):
            @functools.partial(missing, p)
            def _():
                step_copy(w, p, 2).wait_recv()
                step_copy(w, p, 3).wait_recv()
                for i in range(4):
                    step_copy(w, p, i).wait_send()
    for w in range(nw):
        z_copies(w, False)
    for a, (src, dst) in enumerate(((x_ref, xo), (ct_ref, co))):
        token_copies(a, src, dst, False)
        token_arrivals(a, src, dst)


def gather(x, ct, shards):
    nw = len(shards)
    tokens = x.shape[0] * x.shape[1]
    anywhere = pl.BlockSpec(memory_space=pl.ANY)
    dma = pltpu.SemaphoreType.DMA
    out = pl.pallas_call(
        functools.partial(gather_kernel, nw),
        out_shape=[jax.ShapeDtypeStruct((tokens, x.shape[2]), x.dtype)] * 2
        + [jax.ShapeDtypeStruct((2,) + s.shape, s.dtype) for s in shards],
        in_specs=[anywhere] * (2 + nw),
        out_specs=[anywhere] * (2 + nw),
        scratch_shapes=[
            dma((2, 2)), dma((2, 2)), dma((2,)), dma((nw,)), dma((nw, 3)), dma((nw, 2)), dma((nw, 2, 4)), dma((nw, 2, 4)),
        ],
        compiler_params=pltpu.CompilerParams(collective_id=0, has_side_effects=True),
        name="gather",
    )(x, ct, *shards)
    return out[0], out[1], out[2:]


def scatter_kernel(nw, o_ref, i_ref, gain_ref, *refs):
    grads = refs[:nw]
    oo, io, gain_out = refs[nw : nw + 3]
    sums = refs[nw + 3 : 2 * nw + 3]
    scr = refs[2 * nw + 3 :]
    diag, plane_in, col_in, mate = scr[:nw], scr[nw : 2 * nw], scr[2 * nw : 3 * nw], scr[3 * nw : 4 * nw]
    gain_in, tok_s, tok_r, tok_l, ps, pr, cs, cr, ms, mr, gs, gr = scr[4 * nw :]
    place = Place()
    z, c, par, near, j = place.z, place.c, place.par, place.near, place.j
    seg = o_ref.shape[0] // 2
    greet(place)

    def token_copies(a, src, dst, go):
        for b in range(2):
            h = par if b == 0 else 1 - par
            piece = src.at[pl.ds(pl.multiple_of(h * seg, seg), seg)]
            target = place.column(place.half, 2 * c + h)
            there = dst.at[par]

            def far_copy():
                cp = remote(piece, there, tok_s.at[a, b], tok_r.at[a, par], target)
                cp.start() if go else cp.wait_send()

            if b == 0:
                @pl.when(near)
                def _():
                    cp = pltpu.make_async_copy(piece, there, tok_l.at[a])
                    cp.start() if go else cp.wait()

                pl.when(jnp.logical_not(near))(far_copy)
            else:
                far_copy()

    def token_arrivals(a, src, dst):
        for s in range(2):
            @pl.when(jnp.logical_not(near & (par == s)))
            def _():
                remote(src.at[pl.ds(0, seg)], dst.at[s], tok_s.at[a, 0], tok_r.at[a, s], place.plane(1)).wait_recv()

    def rows_of(w, k, half=None):
        q = grads[w].shape[1] // 4
        start, size = pl.multiple_of(place.quarter(k) * q, q), q
        if half is not None:
            size = q // 2
            start = pl.multiple_of(start + half * size, size)
        return pl.ds(start, size)

    def diag_copy(w, half):
        return remote(grads[w].at[:, rows_of(w, 3, half)], diag[w].at[half], ps.at[w, half], pr.at[w, half], place.plane(1 + half))

    def plane_copy(w, i, half):
        e = grads[w].shape[1] // 8
        src = grads[w].at[:, rows_of(w, 1 + i, half)] if half == i else diag[w].at[half]
        n = 2 + 2 * i + half
        return remote(src, plane_in[w].at[i, :, pl.ds(half * e, e)], ps.at[w, n], pr.at[w, n], place.plane(1 + i))

    token_copies(0, o_ref, oo, True)
    token_copies(1, i_ref, io, True)
    for w in range(nw):
        diag_copy(w, 0).start()
        diag_copy(w, 1).start()
        plane_copy(w, 0, 0).start()
        plane_copy(w, 1, 1).start()

    def gain_copy(i):
        to = (place.column(1 - c, z), place.plane(1), place.plane(2), place.column(c, 2 * place.half + 1 - par),
              place.column(c, 2 - 2 * place.half + par))[i]
        return remote(gain_out, gain_in.at[i], gs.at[i], gr.at[i], to)

    gain_out[...] = gain_ref[...]

    def add_diag(w):
        for half in (0, 1):
            diag_copy(w, half).wait()
            rows = rows_of(w, 2 - half, half)
            for p in range(2):
                diag[w][half, p] = (grads[w][p, rows, :].astype(F32) + diag[w][half, p].astype(F32)).astype(BF16)
            plane_copy(w, 1 - half, half).start()

    outer = jnp.where(c == 0, z == 3, z == 0)
    inner = jnp.where(c == 0, z == 2, z == 1)

    def outer_copy(w):
        return remote(plane_in[w].at[0], col_in[w], cs.at[w, 0], cr.at[w, 0], place.column(c, z - 1 + 2 * c))

    def inner_copy(w, p):
        return remote(plane_in[w].at[0, p], col_in[w].at[1], cs.at[w, p], cr.at[w, 1], place.column(c, 2 * c + p))

    def near_copy(w):
        to = place.column(c, 2 * place.half + 1 - par)
        return remote(plane_in[w].at[0, 1 - par], col_in[w].at[0], cs.at[w, 0], cr.at[w, 0], to)

    def mate_copy(w):
        return remote(mate[w].at[0], mate[w].at[1], ms.at[w], mr.at[w], place.column(1 - c, z))

    def add_plane(w):
        mine = rows_of(w, 0)
        for i in range(2):
            for half in range(2):
                plane_copy(w, i, half).wait()
        for p in range(2):
            total = grads[w][p, mine, :].astype(F32) + plane_in[w][0, p].astype(F32) + plane_in[w][1, p].astype(F32)
            plane_in[w][0, p] = total.astype(BF16)
        pl.when(outer)(lambda: outer_copy(w).start())
        pl.when(near)(lambda: near_copy(w).start())

    def add_outer(w):
        @pl.when(inner)
        def _():
            outer_copy(w).wait_recv()
            for p in range(2):
                plane_in[w][0, p] = (plane_in[w][0, p].astype(F32) + col_in[w][p].astype(F32)).astype(BF16)
                inner_copy(w, p).start()

    def add_column(w):
        @pl.when(near)
        def _():
            e = grads[w].shape[1] // 8
            near_copy(w).wait_recv()
            inner_copy(w, 0).wait_recv()
            for hc in range(2):
                here = pl.ds(hc * e, e)
                total = (
                    plane_in[w][0, par, here, :].astype(F32)
                    + col_in[w][0, here, :].astype(F32)
                    + col_in[w][1, here, :].astype(F32)
                )

                @pl.when(c == hc)
                def _():
                    sums[w][...] = total

                @pl.when(c != hc)
                def _():
                    mate[w][0] = total

            mate_copy(w).start()

    def finish(w):
        @pl.when(near)
        def _():
            mate_copy(w).wait_send()
            near_copy(w).wait_send()

        @pl.when(jnp.logical_not(near))
        def _():
            mate_copy(w).wait_recv()
            sums[w][...] = mate[w][1]

        pl.when(outer)(lambda: outer_copy(w).wait_send())

        @pl.when(inner)
        def _():
            inner_copy(w, 0).wait_send()
            inner_copy(w, 1).wait_send()

    for w in range(nw + 3):
        if w < nw:
            add_diag(w)
        if 0 <= w - 1 < nw:
            add_plane(w - 1)
        if 0 <= w - 2 < nw:
            add_outer(w - 2)
        if 0 <= w - 3 < nw:
            add_column(w - 3)
        if w < 5:
            gain_copy(w).start()
            gain_copy(w).wait()
            gain_out[...] += gain_in[w]
    for w in range(nw):
        finish(w)
    for a, (src, dst) in enumerate(((o_ref, oo), (i_ref, io))):
        token_copies(a, src, dst, False)
        token_arrivals(a, src, dst)


def scatter(o, i, gains, grads):
    nw = len(grads)
    assert nw + 3 >= 5
    seg = o.shape[0] // 2
    anywhere = pl.BlockSpec(memory_space=pl.ANY)
    vmem = pl.BlockSpec(memory_space=pltpu.VMEM)
    dma = pltpu.SemaphoreType.DMA
    shapes = [g.shape for g in grads]
    out = pl.pallas_call(
        functools.partial(scatter_kernel, nw),
        out_shape=[jax.ShapeDtypeStruct((2, seg, o.shape[1]), BF16)] * 2
        + [jax.ShapeDtypeStruct(gains.shape, F32)]
        + [jax.ShapeDtypeStruct((r // 8, n), F32) for _, r, n in shapes],
        in_specs=[anywhere] * 2 + [vmem] * (1 + nw),
        out_specs=[anywhere] * 2 + [vmem] * (1 + nw),
        scratch_shapes=[pltpu.VMEM((2, 2, r // 8, n), BF16) for _, r, n in shapes]
        + [pltpu.VMEM((2, 2, r // 4, n), BF16) for _, r, n in shapes]
        + [pltpu.VMEM((2, r // 4, n), BF16) for _, r, n in shapes]
        + [pltpu.VMEM((2, r // 8, n), F32) for _, r, n in shapes]
        + [pltpu.VMEM((5,) + gains.shape, F32)]
        + [
            dma((2, 2)), dma((2, 2)), dma((2,)), dma((nw, 6)), dma((nw, 6)), dma((nw, 2)), dma((nw, 2)), dma((nw,)),
            dma((nw,)), dma((5,)), dma((5,)),
        ],
        compiler_params=pltpu.CompilerParams(collective_id=1, has_side_effects=True, vmem_limit_bytes=60 * 1024 * 1024),
        name="scatter",
    )(o, i, gains, *grads)
    return out[0], out[1], out[2], out[3:]


def rms_scale(values):
    return lax.rsqrt(jnp.mean(values * values, axis=-1, keepdims=True) + EPS)


def rope_tables(length, width):
    half_width = width // 2
    frequency = THETA ** (-(2.0 * jnp.arange(half_width, dtype=F32)) / width)
    angles = jnp.arange(length, dtype=F32)[:, None] * frequency[None, :]
    return (jnp.cos(angles), jnp.sin(angles))


def rotate(values, cos_table, sin_table):
    half_width = values.shape[-1] // 2
    leading = values[..., :half_width]
    trailing = values[..., half_width:]
    cos_part = cos_table[:, None, :]
    sin_part = sin_table[:, None, :]
    return jnp.concatenate(
        [leading * cos_part - trailing * sin_part, trailing * cos_part + leading * sin_part], axis=-1
    )


def norm_back(grads, unit, scale, gain):
    scaled = grads * gain
    return scale * (scaled - unit * jnp.mean(scaled * unit, axis=-1, keepdims=True))


def allowed_block(segment, alive_row, start_row, count_rows, count_keys):
    query_pos = start_row + lax.iota(jnp.int32, count_rows)
    key_pos = lax.iota(jnp.int32, count_keys)
    same_doc = segment[start_row : start_row + count_rows][:, None] == segment[:count_keys][None, :]
    earlier = key_pos[None, :] < query_pos[:, None]
    itself = key_pos[None, :] == query_pos[:, None]
    return itself | earlier & same_doc & (alive_row[:count_keys][None, :] > 0)


def block_scores(query_block, key_block, allowed, scale):
    raw_scores = jnp.einsum("igrd,jgd->grij", query_block, key_block, preferred_element_type=F32) * scale
    return jnp.where(allowed[None, None], raw_scores, MASKED)


def dot(spec, a, b):
    return jnp.einsum(spec, a, b, preferred_element_type=F32)


def per_device(n_dp, inputs, query_weight, key_weight, value_weight, out_weight, gate_weight, up_weight, down_weight,
               attn_gain, ffn_gain, query_gain, key_gain, cotangent, segment_ids, padding, row_count):
    slots, _, width = inputs.shape
    seq_len = segment_ids.shape[1]
    head_dim = query_gain.shape[0]
    hq, hk = query_weight.shape[1] // head_dim, key_weight.shape[1] // head_dim
    per_group = hq // hk
    nq, nk = hq * head_dim, hk * head_dim
    scale = head_dim ** (-0.5)
    z = lax.axis_index("tensor")
    c = lax.axis_index("dp") % 2
    groups = n_dp // 8
    mate = [(i, i ^ 1) for i in range(n_dp)]

    def swap(v):
        return lax.ppermute(v, "dp", mate)

    def both(own):
        other = swap(own)
        return jnp.where(c == 0, jnp.concatenate([own, other], 0), jnp.concatenate([other, own], 0))

    half = seq_len // 2

    def own_sum(partial):
        partial = partial.astype(BF16)
        keep = lax.dynamic_slice_in_dim(partial, c * half, half)
        give = lax.dynamic_slice_in_dim(partial, (1 - c) * half, half)
        return keep.astype(F32) + swap(give).astype(F32)

    alive_all = padding * (jnp.arange(slots)[:, None] < row_count[0]).astype(jnp.int32)
    code = (segment_ids + ALIVE * alive_all)[z % 2]
    code = jnp.where(c == z // 2, code, swap(code))
    segment, alive_row = code % ALIVE, code // ALIVE

    qkv_shard = jnp.concatenate([query_weight, key_weight, value_weight], axis=1)
    x, ct, (wqkv, wo, wg, wu, wd) = gather(
        inputs, cotangent, [qkv_shard, out_weight, gate_weight, up_weight, down_weight]
    )
    cos_table, sin_table = rope_tables(seq_len, head_dim)
    rows_in = x.astype(F32)
    scale_one = rms_scale(rows_in)
    unit_one = rows_in * scale_one
    normed = both((unit_one * attn_gain).astype(BF16))
    proj = dot("sd,pde->spe", normed, wqkv)
    query_proj = proj[:, :, :nq].reshape(seq_len, 2 * hq, head_dim)
    key_proj = proj[:, :, nq : nq + nk].reshape(seq_len, 2 * hk, head_dim)
    values = proj[:, :, nq + nk :].astype(BF16).reshape(seq_len, 2 * hk, head_dim)
    query_scale = rms_scale(query_proj)
    query_unit = query_proj * query_scale
    queries = (
        rotate(query_unit * query_gain, cos_table, sin_table).astype(BF16).reshape(seq_len, 2 * hk, per_group, head_dim)
    )
    key_scale = rms_scale(key_proj)
    key_unit = key_proj * key_scale
    keys_all = rotate(key_unit * key_gain, cos_table, sin_table).astype(BF16)
    block = min(row_block, seq_len)
    blocks = seq_len // block
    attended_parts, log_totals = [], []
    for b in range(blocks):
        start_row, count_keys = b * block, b * block + block
        allowed = allowed_block(segment, alive_row, start_row, block, count_keys)
        scores = block_scores(queries[start_row : start_row + block], keys_all[:count_keys], allowed, scale)
        row_peak = jnp.max(scores, axis=-1, keepdims=True)
        exponent = jnp.exp(scores - row_peak)
        row_total = jnp.sum(exponent, axis=-1, keepdims=True)
        weights_soft = (exponent / row_total).astype(BF16)
        attended_parts.append(dot("grij,jgd->igrd", weights_soft, values[:count_keys]))
        log_totals.append(row_peak + jnp.log(row_total))
    attended = jnp.concatenate(attended_parts, axis=0).reshape(seq_len, 2, nq).astype(BF16)
    hidden = rows_in + own_sum(dot("spe,ped->sd", attended, wo))
    scale_two = rms_scale(hidden)
    unit_two = hidden * scale_two
    normed_two = both((unit_two * ffn_gain).astype(BF16))
    gate_value = dot("sd,pdf->spf", normed_two, wg)
    upward = dot("sd,pdf->spf", normed_two, wu)
    active = (jax.nn.silu(gate_value) * upward).astype(BF16)
    outputs = (hidden + own_sum(dot("spf,pfd->sd", active, wd))).astype(BF16)
    alive_own = lax.dynamic_slice_in_dim(alive_row, c * half, half).astype(F32)
    out_cot = ct.astype(F32) * alive_own[:, None]
    down_in = both(out_cot.astype(BF16))
    active_grad = dot("sd,pfd->spf", down_in, wd)
    sigma = jax.nn.sigmoid(gate_value)
    gate_rows = (active_grad * upward * sigma * (1.0 + gate_value * (1.0 - sigma))).astype(BF16)
    up_rows = (active_grad * gate_value * sigma).astype(BF16)
    grad_down = dot("spf,sd->pfd", active, down_in).astype(BF16)
    grad_gate = dot("sd,spf->pdf", normed_two, gate_rows).astype(BF16)
    grad_up = dot("sd,spf->pdf", normed_two, up_rows).astype(BF16)
    normed_two_grad = own_sum(dot("spf,pdf->sd", gate_rows, wg) + dot("spf,pdf->sd", up_rows, wu))
    grad_ffn_gain = jnp.sum(normed_two_grad * unit_two, axis=0)
    hidden_grad = out_cot + norm_back(normed_two_grad, unit_two, scale_two, ffn_gain)
    attn_in = both(hidden_grad.astype(BF16))
    grad_out = dot("spe,sd->ped", attended, attn_in).astype(BF16)
    attended_grad = dot("sd,ped->spe", attn_in, wo).astype(BF16).reshape(seq_len, 2 * hk, per_group, head_dim)
    value_acc = jnp.zeros((seq_len, 2 * hk, head_dim), F32)
    key_acc = jnp.zeros((seq_len, 2 * hk, head_dim), F32)
    query_parts = []
    for b in range(blocks):
        start_row, count_keys = b * block, b * block + block
        allowed = allowed_block(segment, alive_row, start_row, block, count_keys)
        query_block = queries[start_row : start_row + block]
        scores = block_scores(query_block, keys_all[:count_keys], allowed, scale)
        soft_rows = jnp.exp(scores - log_totals[b])
        soft_low = soft_rows.astype(BF16)
        grad_block = attended_grad[start_row : start_row + block]
        value_acc = value_acc.at[:count_keys].add(dot("grij,igrd->jgd", soft_low, grad_block))
        prob_grad = dot("igrd,jgd->grij", grad_block, values[:count_keys])
        row_inner = jnp.sum(prob_grad * soft_rows, axis=-1, keepdims=True)
        score_grad = (soft_rows * (prob_grad - row_inner)).astype(BF16)
        query_parts.append(dot("grij,jgd->igrd", score_grad, keys_all[:count_keys]) * scale)
        key_acc = key_acc.at[:count_keys].add(dot("grij,igrd->jgd", score_grad, query_block) * scale)
    value_rows = value_acc.astype(BF16).reshape(seq_len, 2, nk)
    query_rot = jnp.concatenate(query_parts, axis=0).astype(BF16).astype(F32).reshape(seq_len, 2 * hq, head_dim)
    key_rot = key_acc.astype(BF16).astype(F32)
    query_norm_grad = rotate(query_rot, cos_table, -sin_table)
    key_norm_grad = rotate(key_rot, cos_table, -sin_table)
    grad_query_gain = jnp.sum(query_norm_grad * query_unit, axis=(0, 1))
    grad_key_gain = jnp.sum(key_norm_grad * key_unit, axis=(0, 1))
    query_rows = norm_back(query_norm_grad, query_unit, query_scale, query_gain).astype(BF16).reshape(seq_len, 2, nq)
    key_rows = norm_back(key_norm_grad, key_unit, key_scale, key_gain).astype(BF16).reshape(seq_len, 2, nk)
    qkv_rows = jnp.concatenate([query_rows, key_rows, value_rows], axis=-1)
    grad_qkv = dot("sd,spe->pde", normed, qkv_rows).astype(BF16)
    normed_grad = own_sum(dot("spe,pde->sd", qkv_rows, wqkv))
    grad_attn_gain = jnp.sum(normed_grad * unit_one, axis=0)
    input_grad = hidden_grad + norm_back(normed_grad, unit_one, scale_one, attn_gain)

    gains = jnp.concatenate([grad_attn_gain, grad_ffn_gain, grad_query_gain, grad_key_gain])
    n_gain = gains.shape[0]
    gains = jnp.pad(gains, (0, -n_gain % 1024)).reshape(-1, 128)

    def spread(g):
        if groups == 1:
            return g
        p, r, n = g.shape
        rr = r // n_dp
        return g.reshape(p, groups, 4, 2, rr, n).transpose(0, 2, 3, 1, 4, 5).reshape(p, r, n)

    outs, in_grad, gains, sums = scatter(
        outputs, input_grad.astype(BF16), gains, [spread(g) for g in (grad_down, grad_gate, grad_up, grad_out, grad_qkv)]
    )
    if groups > 1:
        same = [[g * 8 + k for g in range(groups)] for k in range(8)]
        sums = [lax.psum_scatter(s, "dp", scatter_dimension=0, axis_index_groups=same, tiled=True) for s in sums]
        gains = lax.psum(gains, "dp", axis_index_groups=same)
    down_sum, gate_sum, up_sum, out_sum, qkv_sum = sums
    gains = gains.reshape(-1)
    return (
        outs,
        in_grad.astype(F32),
        qkv_sum[:, :nq],
        qkv_sum[:, nq : nq + nk],
        qkv_sum[:, nq + nk :],
        out_sum,
        gate_sum,
        up_sum,
        down_sum,
        gains[:width],
        gains[width : 2 * width],
        gains[2 * width : 2 * width + head_dim],
        gains[2 * width + head_dim : 2 * width + 2 * head_dim],
    )


def solution(mesh):
    return jax.shard_map(
        functools.partial(per_device, mesh.shape["dp"]),
        mesh=mesh,
        in_specs=(
            P("dp", "tensor", None),
            P(None, "tensor"),
            P(None, "tensor"),
            P(None, "tensor"),
            P("tensor", None),
            P(None, "tensor"),
            P(None, "tensor"),
            P("tensor", None),
            P(),
            P(),
            P(),
            P(),
            P("dp", "tensor", None),
            P("dp", None),
            P("dp", None),
            P("dp"),
        ),
        out_specs=(
            P("dp", "tensor", None),
            P("dp", "tensor", None),
            P("dp", "tensor"),
            P("dp", "tensor"),
            P("dp", "tensor"),
            P(("tensor", "dp"), None),
            P("dp", "tensor"),
            P("dp", "tensor"),
            P(("tensor", "dp"), None),
            P(),
            P(),
            P(),
            P(),
        ),
        check_vma=False,
    )
```

```python
import functools

import jax
import jax.numpy as jnp
import numpy as np
from jax import lax
from jax.experimental import pallas as pl
from jax.experimental.pallas import tpu as pltpu
from jax.sharding import PartitionSpec as P

EPS = 1e-05
THETA = 1000000.0
ALIVE = 4096
MESH = pl.DeviceIdType.MESH
BF16 = jnp.bfloat16
F32 = jnp.float32


class Place:
    def __init__(self):
        self.dp = lax.axis_index("dp")
        self.z = lax.axis_index("tensor")
        self.c = lax.rem(self.dp, 2)
        self.j = lax.rem(self.dp // 2, 4)
        self.half = self.z // 2
        self.par = lax.rem(self.z, 2)
        self.near = self.half == self.c

    def plane(self, k):
        j = self.j
        bit = lax.rem(j // k, 2)
        return (self.dp + (1 - 2 * bit) * 2 * k, self.z)

    def column(self, c, z):
        return (self.dp - self.c + c, z)

    def quarter(self, k):
        j = self.j
        low, high = lax.rem(j, 2), j // 2
        if k & 1:
            low = 1 - low
        if k & 2:
            high = 1 - high
        return 2 * high + low


def greet(place):
    barrier = pltpu.get_barrier_semaphore()
    for k in (1, 2):
        pl.semaphore_signal(barrier, inc=1, device_id=place.plane(k), device_id_type=MESH)
    for dc in range(2):
        for dz in range(4):
            if dc or dz:
                c = lax.rem(place.c + dc, 2)
                z = lax.rem(place.z + dz, 4)
                pl.semaphore_signal(barrier, inc=1, device_id=place.column(c, z), device_id_type=MESH)
    pl.semaphore_wait(barrier, 9)


def remote(src, dst, send, recv, device):
    return pltpu.make_async_remote_copy(
        src_ref=src, dst_ref=dst, send_sem=send, recv_sem=recv, device_id=device, device_id_type=MESH
    )


def lane_swap(v):
    lane = lax.broadcasted_iota(jnp.int32, v.shape, 1)
    return jnp.where(lane % 64 < 32, pltpu.roll(v, 96, 1), pltpu.roll(v, 32, 1))


def head_mean(v, ones_ref, n):
    high = v.astype(BF16)
    low = (v - high.astype(F32)).astype(BF16)
    ones = ones_ref[:n, :n]
    return jnp.dot(high, ones, preferred_element_type=F32) + jnp.dot(low, ones, preferred_element_type=F32)


def mm(a, b):
    return jnp.dot(a, b, preferred_element_type=F32)


def mm_nt(a, b):
    return lax.dot_general(a, b, (((1,), (1,)), ((), ())), preferred_element_type=F32)


def mm_tn(a, b):
    return lax.dot_general(a, b, (((0,), (0,)), ((), ())), preferred_element_type=F32)


BLK = 256


def rows_at(start, size):
    return pl.ds(pl.multiple_of(start, size), size)


def first_kernel(x_ref, ct_ref, wqkv_ref, wo_ref, wg_ref, wu_ref, wd_ref, qcode_ref, kcode_ref, alive_ref, gain1_ref,
                 gain2_ref, gainqk_ref, cos_ref, sin_ref, ones_ref,
                 gg, gu, gd, o_wqkv, o_wo, o_x, o_din, o_normed, o_n2, o_hidden, o_qk, o_q, o_k, o_v, o_att, o_linv,
                 wqkv, wo, xbuf, cbuf, normed, n2, din, hidden, qk, qs, k2, v2, mask, att, linv, give, take,
                 tok_s, tok_r, tok_l, own_l, zs, zr, fs, fr, ms, mr, outs):
    shards = (wqkv_ref, wo_ref, wg_ref, wu_ref, wd_ref)
    full = (wqkv, wo, gg, gu, gd)
    nw = 5
    place = Place()
    z, c, par, near, j = place.z, place.c, place.par, place.near, place.j
    inner = jnp.where(c == 0, z == 2, z == 1)
    outer = jnp.where(c == 0, z == 3, z == 0)
    seg = x_ref.shape[1]
    half = 2 * seg
    seq = 2 * half
    mate = place.column(1 - c, z)
    greet(place)

    def token_copies(a, src, dst, go):
        for b in range(2):
            slot = par if b == 0 else 1 - par
            target = place.column(place.half, 2 * c + slot)
            here = dst.at[rows_at(par * seg, seg)]

            def far_copy():
                cp = remote(src.at[slot], here, tok_s.at[a, b], tok_r.at[a, par], target)
                cp.start() if go else cp.wait_send()

            if b == 0:
                @pl.when(near)
                def _():
                    cp = pltpu.make_async_copy(src.at[slot], here, tok_l.at[a])
                    cp.start() if go else cp.wait()

                pl.when(jnp.logical_not(near))(far_copy)
            else:
                far_copy()

    def token_arrivals(a, src, dst):
        @pl.when(near)
        def _():
            pltpu.make_async_copy(src.at[par], dst.at[rows_at(par * seg, seg)], tok_l.at[a]).wait()

        for h in range(2):
            @pl.when(jnp.logical_not(near & (par == h)))
            def _():
                remote(src.at[0], dst.at[pl.ds(h * seg, seg)], tok_s.at[a, 0], tok_r.at[a, h], place.plane(1)).wait_recv()

    def token_sent(a, src, dst):
        for b in range(2):
            slot = par if b == 0 else 1 - par

            def wait():
                remote(src.at[slot], dst.at[pl.ds(0, seg)], tok_s.at[a, b], tok_r.at[a, 0], place.plane(1)).wait_send()

            if b == 0:
                pl.when(jnp.logical_not(near))(wait)
            else:
                wait()

    def part(w, p, k, side=None):
        q = shards[w].shape[0] // 4
        start, size = pl.multiple_of(place.quarter(k) * q, q), q
        if side is not None:
            size = q // 2
            start = pl.multiple_of(start + side * size, size)
        return full[w].at[p, pl.ds(start, size)]

    def z_copies(w, go):
        q = shards[w].shape[0] // 4

        @pl.when(near)
        def _():
            for i, to in enumerate((2 * place.half + 1 - par, 2 - c)):
                cp = remote(shards[w].at[rows_at(j * q, q)], part(w, par, 0), zs.at[w, i], zr.at[w, par], place.column(c, to))
                cp.start() if go else cp.wait_send()

    def z_onward(w, p):
        return remote(part(w, p, 0), part(w, p, 0), zs.at[w, p], zr.at[w, p], place.column(c, 3 - 3 * c))

    def missing(p, body):
        pl.when(jnp.logical_or(jnp.logical_not(near), par != p))(body)

    def step_copy(w, p, i):
        k, side, to = ((0, None, 1), (0, None, 2), (1, 0, 2), (2, 1, 1))[i]
        return remote(part(w, p, k, side), part(w, p, k, side), fs.at[w, p, i], fr.at[w, p, i], place.plane(to))

    def first(w):
        for p in range(2):
            @functools.partial(missing, p)
            def _():
                z_onward(w, p).wait_recv()
                pl.when(inner)(lambda: z_onward(w, p).start())
                step_copy(w, p, 0).start()
                step_copy(w, p, 1).start()

    def second(w):
        for p in range(2):
            @functools.partial(missing, p)
            def _():
                step_copy(w, p, 0).wait_recv()
                step_copy(w, p, 2).start()
                step_copy(w, p, 1).wait_recv()
                step_copy(w, p, 3).start()

    def third(w):
        for p in range(2):
            @functools.partial(missing, p)
            def _():
                step_copy(w, p, 2).wait_recv()
                step_copy(w, p, 3).wait_recv()

    def sent(w):
        z_copies(w, False)
        for p in range(2):
            @functools.partial(missing, p)
            def _():
                pl.when(inner)(lambda: z_onward(w, p).wait_send())
                for i in range(4):
                    step_copy(w, p, i).wait_send()

    def own_load(w):
        return pltpu.make_async_copy(shards[w], full[w].at[par], own_l.at[w])

    def save(n, src, dst):
        cp = pltpu.make_async_copy(src, dst, outs.at[n])
        saves.append(cp)
        cp.start()

    saves = []

    token_copies(0, x_ref, xbuf, True)
    for w in range(nw):
        z_copies(w, True)
        if w < 2:
            pl.when(near)(lambda: own_load(w).start())
    token_copies(1, ct_ref, cbuf, True)

    for i in range(seq // BLK):
        for jb in range(i + 1):
            same = qcode_ref[i * BLK : (i + 1) * BLK, :] == kcode_ref[:, jb * BLK : (jb + 1) * BLK]
            if i == jb:
                ri = lax.broadcasted_iota(jnp.int32, (BLK, BLK), 0)
                ci = lax.broadcasted_iota(jnp.int32, (BLK, BLK), 1)
                same = jnp.logical_or(ri == ci, jnp.logical_and(ci < ri, same))
            mask[i * BLK : (i + 1) * BLK, jb * BLK : (jb + 1) * BLK] = jnp.where(same, 1.0, 0.0).astype(F32)
    v2[:, :, 128:] = jnp.ones((v2.shape[0], v2.shape[1], 128), BF16)

    token_arrivals(0, x_ref, xbuf)
    step = 128

    @pl.loop(0, half // step)
    def _(r):
        xs = xbuf[rows_at(r * step, step), :].astype(F32)
        sc = lax.rsqrt(jnp.mean(xs * xs, axis=-1, keepdims=True) + EPS)
        normed[rows_at(c * half + r * step, step), :] = (xs * sc * gain1_ref[...]).astype(BF16)

    def swap_rows(buf, n):
        own = rows_at(c * half, half)
        return remote(buf.at[own], buf.at[own], ms.at[n], mr.at[n], mate)

    def swap_wait(buf, n):
        remote(buf.at[rows_at((1 - c) * half, half)], buf.at[rows_at((1 - c) * half, half)], ms.at[n], mr.at[n], mate).wait_recv()

    swap_rows(normed, 0).start()
    first(0)
    first(1)
    second(0)
    second(1)
    save(0, xbuf, o_x)
    swap_wait(normed, 0)
    save(1, normed, o_normed)
    pl.when(near)(lambda: own_load(0).wait())
    third(0)

    @pl.loop(0, seq // BLK)
    def _(r):
        rows = rows_at(r * BLK, BLK)
        cos, sin = cos_ref[rows, :], sin_ref[rows, :]
        lane = lax.broadcasted_iota(jnp.int32, (BLK, 128), 1)
        left = lane < 64
        for p in range(2):
            proj = mm(normed[rows, :], wqkv[p])
            pq = proj[:, :384]
            qk[p, rows, :] = pq
            sc = lax.rsqrt(head_mean(pq * pq, ones_ref, 384) + EPS)
            n = pq * sc * gainqk_ref[...]
            for s in range(3):
                v = n[:, s * 128 : (s + 1) * 128]
                rot = v * cos + lane_swap(v) * sin
                if s < 2:
                    qr = rot.astype(BF16).astype(F32) * 0.125
                    qs[2 * p + s, 0, rows, :] = jnp.where(left, qr, 0.0).astype(BF16)
                    qs[2 * p + s, 1, rows, :] = jnp.where(left, 0.0, qr).astype(BF16)
                else:
                    kr = pltpu.roll(rot, 64, 1)
                    k2[2 * p, rows, :] = jnp.where(left, rot, kr).astype(BF16)
                    k2[2 * p + 1, rows, :] = jnp.where(left, kr, rot).astype(BF16)
            v = proj[:, 384:]
            vr = pltpu.roll(v, 64, 1)
            v2[2 * p, rows, :128] = jnp.where(left, v, vr).astype(BF16)
            v2[2 * p + 1, rows, :128] = jnp.where(left, vr, v).astype(BF16)

    save(2, wqkv, o_wqkv)
    save(3, qk, o_qk)
    save(4, qs, o_q)
    save(5, k2, o_k)
    save(6, v2.at[:, :, pl.ds(0, 128)], o_v)
    first(2)
    for i in range(seq // BLK):
        n = (i + 1) * BLK
        rows = pl.ds(i * BLK, BLK)

        @pl.loop(0, k2.shape[0])
        def _(g):
            s = mm_nt(qs[g, :, rows, :].reshape(2 * BLK, 128), k2[g, :n, :])
            e = jnp.exp(s).reshape(2, BLK, n) * mask[rows, :n][None]
            acc = mm(e.astype(BF16).reshape(2 * BLK, n), v2[g, :n, :])
            inv = 1.0 / acc[:, 128:]
            o = acc[:, :128] * inv
            left = lax.broadcasted_iota(jnp.int32, (BLK, 128), 1) < 64
            cols = pl.ds(pl.multiple_of(g * 128, 128), 128)
            att[rows, cols] = jnp.where(left, o[:BLK], o[BLK:]).astype(BF16)
            linv[rows, cols] = jnp.where(left, inv[:BLK], inv[BLK:])

        if i == 1:
            second(2)
            first(3)
    save(7, att, o_att)
    save(8, linv, o_linv)
    second(3)
    pl.when(near)(lambda: own_load(1).wait())
    third(1)
    save(9, wo, o_wo)

    def out_rows(start):
        return mm(att[rows_at(start, BLK), :], wo[...].reshape(2 * wo.shape[1], wo.shape[2]))

    @pl.loop(0, half // BLK)
    def _(r):
        give[rows_at(r * BLK, BLK), :] = out_rows((1 - c) * half + r * BLK).astype(BF16)

    swap_give = remote(give, take, ms.at[1], mr.at[1], mate)
    swap_give.start()

    @pl.loop(0, half // BLK)
    def _(r):
        hidden[rows_at(r * BLK, BLK), :] = out_rows(c * half + r * BLK) + xbuf[rows_at(r * BLK, BLK), :].astype(F32)

    first(4)
    swap_give.wait_recv()

    @pl.loop(0, half // step)
    def _(r):
        h = hidden[rows_at(r * step, step), :] + take[rows_at(r * step, step), :].astype(F32)
        hidden[rows_at(r * step, step), :] = h
        sc = lax.rsqrt(jnp.mean(h * h, axis=-1, keepdims=True) + EPS)
        n2[rows_at(c * half + r * step, step), :] = (h * sc * gain2_ref[...]).astype(BF16)

    swap_rows(n2, 2).start()
    save(10, hidden, o_hidden)
    second(4)
    token_arrivals(1, ct_ref, cbuf)

    @pl.loop(0, half // step)
    def _(r):
        v = cbuf[rows_at(r * step, step), :].astype(F32) * alive_ref[rows_at(r * step, step), :]
        din[rows_at(c * half + r * step, step), :] = v.astype(BF16)

    swap_rows(din, 3).start()
    swap_wait(n2, 2)
    save(11, n2, o_n2)
    swap_wait(din, 3)
    save(12, din, o_din)
    for w in range(2, nw):
        third(w)
    for w in range(nw):
        sent(w)
    token_sent(0, x_ref, xbuf)
    token_sent(1, ct_ref, cbuf)
    swap_rows(normed, 0).wait_send()
    swap_give.wait_send()
    swap_rows(n2, 2).wait_send()
    swap_rows(din, 3).wait_send()
    for cp in saves:
        cp.wait()


def first_part(x, ct, shards, qcode, kcode, alive, gain1, gain2, gainqk, cos, sin, ones):
    anywhere = pl.BlockSpec(memory_space=pl.ANY)
    vmem = pl.BlockSpec(memory_space=pltpu.VMEM)
    dma = pltpu.SemaphoreType.DMA
    seg, width = x.shape[1], x.shape[2]
    half, seq = 2 * seg, 4 * seg
    wqkv, wo, wg, wu, wd = shards
    groups = 4
    SDS = jax.ShapeDtypeStruct
    kept = dict(
        wqkv=((2,) + wqkv.shape, BF16), wo=((2,) + wo.shape, BF16), x=((half, width), BF16), din=((seq, width), BF16),
        normed=((seq, width), BF16), n2=((seq, width), BF16), hidden=((half, width), F32), qk=((2, seq, 384), F32),
        q=((groups, 2, seq, 128), BF16), k=((groups, seq, 128), BF16), v=((groups, seq, 128), BF16), att=((seq, 512), BF16),
        linv=((seq, 512), F32),
    )
    order = ("wqkv", "wo", "x", "din", "normed", "n2", "hidden", "qk", "q", "k", "v", "att", "linv")
    out_shape = [SDS((2,) + w.shape, BF16) for w in (wg, wu, wd)] + [SDS(*kept[k]) for k in order]

    def vm(k):
        return pltpu.VMEM(*kept[k])

    nw = 5
    out = pl.pallas_call(
        first_kernel,
        out_shape=out_shape,
        in_specs=[anywhere] * 7 + [vmem] * 9,
        out_specs=[anywhere] * len(out_shape),
        scratch_shapes=[
            vm("wqkv"), vm("wo"), vm("x"), pltpu.VMEM((half, width), BF16), vm("normed"), vm("n2"), vm("din"), vm("hidden"), vm("qk"),
            vm("q"), vm("k"), pltpu.VMEM((groups, seq, 256), BF16), pltpu.VMEM((seq, seq), F32), vm("att"), vm("linv"), pltpu.VMEM((half, width), BF16),
            pltpu.VMEM((half, width), BF16),
            dma((2, 2)), dma((2, 2)), dma((2,)), dma((nw,)), dma((nw, 2)), dma((nw, 2)), dma((nw, 2, 4)), dma((nw, 2, 4)),
            dma((4,)), dma((4,)), dma((13,)),
        ],
        compiler_params=pltpu.CompilerParams(collective_id=0, has_side_effects=True, vmem_limit_bytes=60 * 1024 * 1024),
        name="gather_attention",
    )(x, ct, *shards, qcode, kcode, alive, gain1, gain2, gainqk, cos, sin, ones)
    gathered, rest = out[:3], dict(zip(order, out[3:]))
    return gathered, rest


TILE = 384
PIECES = 3


def second_kernel(gg, gu, gd, wg_ref, wu_ref, wd_ref, wqkv_ref, wo_ref, x_ref, din_ref, normed_ref, n2_ref, hidden_ref, qk_ref,
                  q_ref, k_ref, v_ref, att_ref, linv_ref, qrow_ref, kcol_ref, gain1_ref, gain2_ref, gainqk_ref, cos_ref, sin_ref,
                  ones_ref,
                  oo, io, gain_out, s_gu0, s_gu1, s_gu2, s_d, s_o, s_qkv,
                  p_gu0, p_gu1, p_gu2, p_d, p_o, p_qkv, c_gu0, c_gu1, c_gu2, c_d, c_o, c_qkv,
                  g_a, g_b, g_d, g_o, g_qkv, d_gu0, d_gu1, d_gu2, d_d, d_o, d_qkv, stage, last, give, take, obuf, hgrad,
                  gain_in, attn_in,
                  tok_s, tok_r, tok_l, ps, pr, cs, cr, ls, lr, ll, gs, gr, ms, mr, ld, wl, st_sem):
    grads = (g_a, g_b, g_a, g_d, g_o, g_qkv)
    diag = (d_gu0, d_gu1, d_gu2, d_d, d_o, d_qkv)
    plane_in = (p_gu0, p_gu1, p_gu2, p_d, p_o, p_qkv)
    col_in = (c_gu0, c_gu1, c_gu2, c_d, c_o, c_qkv)
    sums = (s_gu0, s_gu1, s_gu2, s_d, s_o, s_qkv)
    nw = 6
    D_, O_, QKV_ = 3, 4, 5
    place = Place()
    z, c, par, near, j = place.z, place.c, place.par, place.near, place.j
    inner = jnp.where(c == 0, z == 2, z == 1)
    outer = jnp.where(c == 0, z == 3, z == 0)
    half = obuf.shape[0]
    seq = 2 * half
    seg = half // 2
    width = obuf.shape[1]
    mate = place.column(1 - c, z)
    own_at = c * half
    other_at = (1 - c) * half
    step = 128
    greet(place)

    def token_copies(a, src, dst, go):
        for b in range(2):
            h = par if b == 0 else 1 - par
            piece = src.at[rows_at(h * seg, seg)]
            target = place.column(place.half, 2 * c + h)
            there = dst.at[par]

            def far_copy():
                cp = remote(piece, there, tok_s.at[a, b], tok_r.at[a, par], target)
                cp.start() if go else cp.wait_send()

            if b == 0:
                @pl.when(near)
                def _():
                    cp = pltpu.make_async_copy(piece, there, tok_l.at[a])
                    cp.start() if go else cp.wait()

                pl.when(jnp.logical_not(near))(far_copy)
            else:
                far_copy()

    def token_arrivals(a, src, dst):
        for s in range(2):
            @pl.when(jnp.logical_not(near & (par == s)))
            def _():
                remote(src.at[pl.ds(0, seg)], dst.at[s], tok_s.at[a, 0], tok_r.at[a, s], place.plane(1)).wait_recv()

    def rows_of(w, k, side=None):
        q = grads[w].shape[1] // 4
        start, size = pl.multiple_of(place.quarter(k) * q, q), q
        if side is not None:
            size = q // 2
            start = pl.multiple_of(start + side * size, size)
        return pl.ds(start, size)

    def diag_copy(w, side):
        return remote(grads[w].at[:, rows_of(w, 3, side)], diag[w].at[side], ps.at[w, side], pr.at[w, side], place.plane(1 + side))

    def plane_copy(w, i, side):
        src = grads[w].at[:, rows_of(w, 1 + i, side)] if side == i else diag[w].at[side]
        n = 2 + 2 * i + side
        return remote(src, plane_in[w].at[i, side], ps.at[w, n], pr.at[w, n], place.plane(1 + i))

    def begin(w):
        diag_copy(w, 0).start()
        diag_copy(w, 1).start()
        plane_copy(w, 0, 0).start()
        plane_copy(w, 1, 1).start()

    def add_diag(w):
        for side in (0, 1):
            diag_copy(w, side).wait()
            rows = rows_of(w, 2 - side, side)
            for p in range(2):
                diag[w][side, p] = (grads[w][p, rows, :].astype(F32) + diag[w][side, p].astype(F32)).astype(BF16)
            plane_copy(w, 1 - side, side).start()

    def outer_copy(w):
        return remote(diag[w], col_in[w], cs.at[w, 0], cr.at[w, 0], place.column(c, z - 1 + 2 * c))

    def inner_copy(w, p):
        return remote(diag[w].at[:, p], col_in[w].at[:, 1], cs.at[w, p], cr.at[w, 1], place.column(c, 2 * c + p))

    def near_copy(w):
        to = place.column(c, 2 * place.half + 1 - par)
        return remote(diag[w].at[:, 1 - par], col_in[w].at[:, 0], cs.at[w, 0], cr.at[w, 0], to)

    def staged(w, n):
        e = grads[w].shape[1] // 8
        return stage.at[pl.ds(0, n), :, :, pl.ds(0, e), pl.ds(0, grads[w].shape[2])]

    def add_plane(w):
        for i in range(2):
            for side in range(2):
                plane_copy(w, i, side).wait()
        cp = pltpu.make_async_copy(plane_in[w], staged(w, 2), st_sem.at[0])
        cp.start()
        cp.wait()
        e, n = grads[w].shape[1] // 8, grads[w].shape[2]
        for side in range(2):
            rows = rows_of(w, 0, side)
            for p in range(2):
                total = (
                    grads[w][p, rows, :].astype(F32)
                    + stage[0, side, p, :e, :n].astype(F32)
                    + stage[1, side, p, :e, :n].astype(F32)
                )
                diag[w][side, p] = total.astype(BF16)
        pl.when(outer)(lambda: outer_copy(w).start())
        pl.when(near)(lambda: near_copy(w).start())

    def load_column(w):
        cp = pltpu.make_async_copy(col_in[w], staged(w, 1).at[0], st_sem.at[1])
        cp.start()
        cp.wait()

    def add_outer(w):
        @pl.when(inner)
        def _():
            outer_copy(w).wait_recv()
            load_column(w)
            e, n = grads[w].shape[1] // 8, grads[w].shape[2]
            for p in range(2):
                for side in range(2):
                    diag[w][side, p] = (diag[w][side, p].astype(F32) + stage[0, side, p, :e, :n].astype(F32)).astype(BF16)
                inner_copy(w, p).start()

    def last_view(w, k):
        return last.at[w % 2, k, pl.ds(0, grads[w].shape[1] // 8), pl.ds(0, grads[w].shape[2])]

    def last_remote(w):
        return remote(last_view(w, 1), sums[w], ls.at[w], lr.at[w], mate)

    def last_local(w):
        return pltpu.make_async_copy(last_view(w, 0), sums[w], ll.at[w])

    def release_last(w):
        @pl.when(near)
        def _():
            last_remote(w).wait_send()
            last_local(w).wait()

    def add_column(w):
        if w >= 2:
            release_last(w - 2)

        @pl.when(near)
        def _():
            e, n = grads[w].shape[1] // 8, grads[w].shape[2]
            near_copy(w).wait_recv()
            inner_copy(w, 0).wait_recv()
            load_column(w)
            for hc in range(2):
                total = (
                    diag[w][hc, par].astype(F32) + stage[0, hc, 0, :e, :n].astype(F32) + stage[0, hc, 1, :e, :n].astype(F32)
                )

                @pl.when(c == hc)
                def _():
                    last[w % 2, 0, :e, :n] = total

                @pl.when(c != hc)
                def _():
                    last[w % 2, 1, :e, :n] = total

            last_remote(w).start()
            last_local(w).start()

    def finish(w):
        pl.when(near)(lambda: near_copy(w).wait_send())
        pl.when(jnp.logical_not(near))(lambda: last_remote(w).wait_recv())
        pl.when(outer)(lambda: outer_copy(w).wait_send())

        @pl.when(inner)
        def _():
            inner_copy(w, 0).wait_send()
            inner_copy(w, 1).wait_send()

    def trade(n):
        return remote(give.at[n % 2], take.at[n], ms.at[n], mr.at[n], mate)

    def load(n, src, dst):
        return pltpu.make_async_copy(src, dst, ld.at[n])

    def ffn(n2, din, n2t, wg, wu, wd, acc_o, acc_n, act, gr, ur):
        loads = [load(0, n2_ref, n2), load(1, din_ref, din)]
        for cp in loads:
            cp.start()

        def tile_loads(i, go):
            t, p = i // 2, i % 2
            b = i % 2
            cols = pl.ds(t * TILE, TILE)
            mine = near & (par == p)

            def run(g, u, d):
                for k, (src, dst) in enumerate(((g.at[:, cols], wg.at[b]), (u.at[:, cols], wu.at[b]), (d.at[cols], wd.at[b]))):
                    cp = pltpu.make_async_copy(src, dst, wl.at[b, k])
                    cp.start() if go else cp.wait()

            if go:
                pl.when(mine)(lambda: run(wg_ref, wu_ref, wd_ref))
                pl.when(jnp.logical_not(mine))(lambda: run(gg.at[p], gu.at[p], gd.at[p]))
            else:
                run(gg.at[p], gu.at[p], gd.at[p])

        tile_loads(0, True)
        for cp in loads:
            cp.wait()

        @pl.loop(0, seq // BLK)
        def _(r):
            cols = pl.ds(pl.multiple_of(r * BLK, BLK), BLK)
            n2t[:, cols] = n2[cols, :].T

        for i in range(2 * PIECES):
            t, p = i // 2, i % 2
            b = i % 2
            if i + 1 < 2 * PIECES:
                tile_loads(i + 1, True)
            tile_loads(i, False)

            @pl.loop(0, seq // BLK)
            def _(r):
                rows = rows_at(r * BLK, BLK)
                a = n2[rows, :]
                g = mm(a, wg[b])
                u = mm(a, wu[b])
                ag = mm_nt(din[rows, :], wd[b])
                sig = jax.nn.sigmoid(g)
                gs_ = g * sig
                av = (gs_ * u).astype(BF16)
                act[p, rows, t * TILE : (t + 1) * TILE] = av
                gv = (ag * u * sig * (1.0 + g * (1.0 - sig))).astype(BF16)
                uv = (ag * gs_).astype(BF16)
                gr[rows, :] = gv
                ur[rows, :] = uv
                dn = mm_nt(gv, wg[b]) + mm_nt(uv, wu[b])
                do = mm(av, wd[b])
                if i == 0:
                    acc_n[rows, :] = dn
                    acc_o[rows, :] = do
                else:
                    acc_n[rows, :] += dn
                    acc_o[rows, :] += do

            @pl.loop(0, width // BLK)
            def _(r):
                rows = rows_at(r * BLK, BLK)
                grads[t][p, rows, :TILE] = mm(n2t[rows, :], gr[...]).astype(BF16)
                grads[t][p, rows, TILE:] = mm(n2t[rows, :], ur[...]).astype(BF16)

            if p == 1:
                begin(t)
                if t == 1:
                    add_diag(0)
                    add_plane(0)

        @pl.loop(0, half // BLK)
        def _(r):
            rows = rows_at(r * BLK, BLK)
            give[0, rows, :] = acc_n[rows_at(other_at + r * BLK, BLK), :].astype(BF16)
            give[1, rows, :] = acc_o[rows_at(other_at + r * BLK, BLK), :].astype(BF16)

        trade(0).start()
        trade(1).start()
        hid_load = load(2, hidden_ref, hgrad)
        hid_load.start()
        for p in range(2):
            @pl.loop(0, width // BLK)
            def _(r):
                cols = pl.ds(pl.multiple_of(r * BLK, BLK), BLK)
                for k in range(PIECES):
                    rows = pl.ds(k * TILE, TILE)
                    grads[D_][p, rows, cols] = mm_tn(act[p, :, rows], din[:, cols]).astype(BF16)

        begin(D_)
        hid_load.wait()
        trade(0).wait_recv()
        trade(1).wait_recv()
        gain_out[8:16, :] = jnp.zeros((8, 128), F32)

        @pl.loop(0, half // step)
        def _(r):
            rows = rows_at(r * step, step)
            own = rows_at(own_at + r * step, step)
            h = hgrad[rows, :]
            obuf[rows, :] = (h + acc_o[own, :] + take[1, rows, :].astype(F32)).astype(BF16)
            ng = acc_n[own, :] + take[0, rows, :].astype(F32)
            sc = lax.rsqrt(jnp.mean(h * h, axis=-1, keepdims=True) + EPS)
            unit = h * sc
            acc_gain(8, ng * unit)
            e = ng * gain2_ref[...]
            hg = din[own, :].astype(F32) + sc * (e - unit * jnp.mean(e * unit, axis=-1, keepdims=True))
            hgrad[rows, :] = hg
            attn_in[own, :] = hg.astype(BF16)

        token_copies(0, obuf, oo, True)

    def acc_gain(at, v):
        s = jnp.sum(v, axis=0, keepdims=True)
        for k in range(width // 128):
            gain_out[at + k : at + k + 1, :] += s[:, k * 128 : (k + 1) * 128]

    gain_out[...] = jnp.zeros(gain_out.shape, F32)
    pl.run_scoped(
        ffn,
        pltpu.VMEM((seq, width), BF16), pltpu.VMEM((seq, width), BF16), pltpu.VMEM((width, seq), BF16),
        pltpu.VMEM((2, width, TILE), BF16), pltpu.VMEM((2, width, TILE), BF16), pltpu.VMEM((2, TILE, width), BF16),
        pltpu.VMEM((seq, width), F32), pltpu.VMEM((seq, width), F32), pltpu.VMEM((2, seq, PIECES * TILE), BF16),
        pltpu.VMEM((seq, TILE), BF16), pltpu.VMEM((seq, TILE), BF16),
    )

    def attn_swap():
        own = rows_at(own_at, half)
        return remote(attn_in.at[own], attn_in.at[own], ms.at[3], mr.at[3], mate)

    attn_swap().start()

    def attention(dos, dq, dk, dv, drow):
        def front(wo, att, linv):
            loads = [load(3, wo_ref, wo), load(4, att_ref, att), load(5, linv_ref, linv)]
            for cp in loads:
                cp.start()
            add_diag(1)
            for cp in loads:
                cp.wait()
            other = rows_at(other_at, half)
            remote(attn_in.at[other], attn_in.at[other], ms.at[3], mr.at[3], mate).wait_recv()

            @pl.loop(0, seq // BLK)
            def _(r):
                rows = rows_at(r * BLK, BLK)
                left = lax.broadcasted_iota(jnp.int32, (BLK, 128), 1) < 64
                for p in range(2):
                    ag = mm_nt(attn_in[rows, :], wo[p]).astype(BF16).astype(F32)
                    for s in range(2):
                        g = 2 * p + s
                        cols = slice(g * 128, (g + 1) * 128)
                        d = ag[:, s * 128 : (s + 1) * 128] * linv[rows, cols]
                        d0, d1 = jnp.where(left, d, 0.0).astype(BF16), jnp.where(left, 0.0, d).astype(BF16)
                        dos[g, 0, rows, :] = d0
                        dos[g, 1, rows, :] = d1
                        o = att[rows, cols].astype(F32)
                        one = jnp.ones((8, 128), BF16)
                        for k, dd in enumerate((d0, d1)):
                            prod = dd.astype(F32) * o
                            high = prod.astype(BF16)
                            low = (prod - high.astype(F32)).astype(BF16)
                            drow[g, k, :, rows] = mm_nt(one, high) + mm_nt(one, low)

            @pl.loop(0, width // BLK)
            def _(r):
                cols = pl.ds(pl.multiple_of(r * BLK, BLK), BLK)
                for p in range(2):
                    grads[O_][p, :, cols] = mm_tn(att[:, p * 256 : (p + 1) * 256], attn_in[:, cols]).astype(BF16)

            begin(O_)

        pl.run_scoped(
            front, pltpu.VMEM(wo_ref.shape, BF16), pltpu.VMEM(att_ref.shape, BF16), pltpu.VMEM(linv_ref.shape, F32),
        )
        add_plane(1)
        add_diag(2)

        def rest(q, k, v, mt, qk, rows_, wqkv, normed, x):
            loads = [load(6, q_ref, q), load(7, k_ref, k), load(8, v_ref, v)]
            later = [load(9, qk_ref, qk), load(10, wqkv_ref, wqkv), load(11, normed_ref, normed), load(12, x_ref, x)]
            for cp in loads + later:
                cp.start()
            for cp in loads:
                cp.wait()
            dq[...] = jnp.zeros(dq.shape, F32)
            todo = {
                0: [lambda: add_outer(0), lambda: add_plane(2)],
                1: [lambda: add_diag(D_), lambda: add_column(0), lambda: add_outer(1)],
                2: [lambda: add_plane(D_), lambda: add_diag(O_), lambda: add_column(1), lambda: add_outer(2)],
                3: [lambda: add_plane(O_), lambda: add_column(2), lambda: add_outer(D_)],
            }
            for jb in range(seq // BLK):
                at = jb * BLK
                ni = seq - at
                keys = pl.ds(at, BLK)
                cols = pl.ds(at, ni)
                ki = lax.broadcasted_iota(jnp.int32, (BLK, ni), 0)
                qi = lax.broadcasted_iota(jnp.int32, (BLK, ni), 1)
                same = jnp.logical_and(ki < qi, kcol_ref[keys, :] == qrow_ref[:, cols])
                mt[:, :ni] = jnp.where(jnp.logical_or(ki == qi, same), 1.0, 0.0).astype(F32)

                @pl.loop(0, 4)
                def _(g):
                    kb = k[g, keys, :]
                    qb = q[g, :, cols, :].reshape(2 * ni, 128)
                    db = dos[g, :, cols, :].reshape(2 * ni, 128)
                    m = mt[:, :ni]
                    e = jnp.exp(mm_nt(kb, qb)) * jnp.concatenate([m, m], axis=1)
                    dv[g, keys, :] = mm(e.astype(BF16), db)
                    dp = mm_nt(v[g, keys, :], db)
                    dr = jnp.concatenate([drow[g, 0, :1, cols], drow[g, 1, :1, cols]], axis=1)
                    ds = (e * (dp - dr)).astype(BF16)
                    dk[g, keys, :] = mm(ds, qb)
                    dqs = mm_tn(ds, kb)
                    left = lax.broadcasted_iota(jnp.int32, (ni, 128), 1) < 64
                    lanes = pl.ds(pl.multiple_of(g * 128, 128), 128)
                    dq[cols, lanes] += jnp.where(left, dqs[:ni], dqs[ni:])

                for f in todo[jb]:
                    f()
            for cp in later:
                cp.wait()

            @pl.loop(0, seq // BLK)
            def _(r):
                rows = rows_at(r * BLK, BLK)
                cos, sin = cos_ref[rows, :], sin_ref[rows, :]
                left = lax.broadcasted_iota(jnp.int32, (BLK, 128), 1) < 64

                def fold(ref, p):
                    a, b = ref[2 * p, rows, :], ref[2 * p + 1, rows, :]
                    return jnp.where(left, a + pltpu.roll(a, 64, 1), b + pltpu.roll(b, 64, 1))

                for p in range(2):
                    raw = qk[p, rows, :]
                    sc = lax.rsqrt(head_mean(raw * raw, ones_ref, 384) + EPS)
                    unit = raw * sc
                    parts = []
                    for s in range(3):
                        if s < 2:
                            v_ = dq[rows, (2 * p + s) * 128 : (2 * p + s + 1) * 128] * 0.125
                        else:
                            v_ = fold(dk, p)
                        v_ = v_.astype(BF16).astype(F32)
                        parts.append(v_ * cos - lane_swap(v_) * sin)
                    ng = jnp.concatenate(parts, axis=1)
                    gsum = jnp.sum(ng * unit, axis=0, keepdims=True)
                    qsum = gsum[:, :128] + gsum[:, 128:256]
                    ksum = gsum[:, 256:]
                    gain_out[16:17, :] += qsum
                    gain_out[17:18, :] += ksum
                    e = ng * gainqk_ref[...]
                    back = sc * (e - unit * head_mean(e * unit, ones_ref, 384))
                    rows_[p, rows, :384] = back.astype(BF16)
                    rows_[p, rows, 384:] = fold(dv, p).astype(BF16)

            def back_rows(start):
                at = rows_at(start, BLK)
                return mm_nt(rows_[0, at, :], wqkv[0]) + mm_nt(rows_[1, at, :], wqkv[1])

            trade(0).wait_send()

            @pl.loop(0, half // BLK)
            def _(r):
                give[0, rows_at(r * BLK, BLK), :] = back_rows(other_at + r * BLK).astype(BF16)

            trade(2).start()
            for p in range(2):
                @pl.loop(0, width // BLK)
                def _(r):
                    cols = pl.ds(pl.multiple_of(r * BLK, BLK), BLK)
                    grads[QKV_][p, cols, :] = mm_tn(normed[:, cols], rows_[p]).astype(BF16)

            begin(QKV_)
            add_column(D_)
            add_outer(O_)
            trade(2).wait_recv()
            token_copies(0, obuf, oo, False)

            @pl.loop(0, half // BLK)
            def _(r):
                rows = rows_at(r * BLK, BLK)
                ng = back_rows(own_at + r * BLK) + take[2, rows, :].astype(F32)
                xs = x[rows, :].astype(F32)
                sc = lax.rsqrt(jnp.mean(xs * xs, axis=-1, keepdims=True) + EPS)
                unit = xs * sc
                acc_gain(0, ng * unit)
                e = ng * gain1_ref[...]
                ig = hgrad[rows, :] + sc * (e - unit * jnp.mean(e * unit, axis=-1, keepdims=True))
                obuf[rows, :] = ig.astype(BF16)

        V = pltpu.VMEM
        pl.run_scoped(
            rest, V(q_ref.shape, BF16), V(k_ref.shape, BF16), V(v_ref.shape, BF16), V((BLK, seq), F32), V(qk_ref.shape, F32),
            V((2, seq, 512), BF16), V(wqkv_ref.shape, BF16), V(normed_ref.shape, BF16), V(x_ref.shape, BF16),
        )

    pl.run_scoped(
        attention, pltpu.VMEM(q_ref.shape, BF16), pltpu.VMEM((seq, 512), F32), pltpu.VMEM((4, seq, 128), F32),
        pltpu.VMEM((4, seq, 128), F32), pltpu.VMEM((4, 2, 8, seq), F32),
    )
    token_copies(1, obuf, io, True)

    def gain_copy(i):
        to = (mate, place.plane(1), place.plane(2), place.column(c, 2 * place.half + 1 - par),
              place.column(c, 2 - 2 * place.half + par))[i]
        return remote(gain_out, gain_in.at[i], gs.at[i], gr.at[i], to)

    for i in range(5):
        gain_copy(i).start()
        if i == 0:
            add_diag(QKV_)
        if i == 1:
            add_column(O_)
        if i == 2:
            add_plane(QKV_)
        if i == 3:
            add_outer(QKV_)
        gain_copy(i).wait()
        gain_out[...] += gain_in[i]
    add_column(QKV_)
    release_last(nw - 2)
    release_last(nw - 1)
    for w in range(nw):
        finish(w)
    trade(1).wait_send()
    trade(2).wait_send()
    attn_swap().wait_send()
    token_copies(1, obuf, io, False)
    token_arrivals(0, obuf, oo)
    token_arrivals(1, obuf, io)


def second_part(gathered, shards, kept, qrow, kcol, gain1, gain2, gainqk, cos, sin, ones):
    anywhere = pl.BlockSpec(memory_space=pl.ANY)
    vmem = pl.BlockSpec(memory_space=pltpu.VMEM)
    dma = pltpu.SemaphoreType.DMA
    half, width = kept["x"].shape
    SDS = jax.ShapeDtypeStruct
    wg, wu, wd = shards
    r_d = wd.shape[0]
    sizes = [(width, 2 * TILE)] * 3 + [(r_d, width), (kept["wo"].shape[1], width), (width, kept["wqkv"].shape[2])]
    held = [sizes[0], sizes[1]] + sizes[3:]
    nw = 6
    order = ("wqkv", "wo", "x", "din", "normed", "n2", "hidden", "qk", "q", "k", "v", "att", "linv")
    gains = (24, 128)
    out_shape = (
        [SDS((2, half // 2, width), BF16)] * 2
        + [SDS(gains, F32)]
        + [SDS((r // 8, n), F32) for r, n in sizes]
        + [SDS((2, 2, 2, r // 8, n), BF16) for r, n in sizes]
        + [SDS((2, 2, r // 8, n), BF16) for r, n in sizes]
    )
    V = pltpu.VMEM
    e_max, n_max = max(r // 8 for r, _ in sizes), max(n for _, n in sizes)
    out = pl.pallas_call(
        second_kernel,
        out_shape=out_shape,
        in_specs=[anywhere] * (6 + len(order)) + [vmem] * 8,
        out_specs=[anywhere] * 2 + [vmem] + [anywhere] * 18,
        scratch_shapes=[V((2, r, n), BF16) for r, n in held]
        + [V((2, 2, r // 8, n), BF16) for r, n in sizes]
        + [
            V((2, 2, 2, e_max, n_max), BF16), V((2, 2, e_max, n_max), F32), V((2, half, width), BF16), V((3, half, width), BF16),
            V((half, width), BF16), V((half, width), F32), V((5,) + gains, F32), V((2 * half, width), BF16),
        ]
        + [
            dma((2, 2)), dma((2, 2)), dma((2,)), dma((nw, 6)), dma((nw, 6)), dma((nw, 2)), dma((nw, 2)), dma((nw,)), dma((nw,)),
            dma((nw,)), dma((5,)), dma((5,)), dma((4,)), dma((4,)), dma((13,)), dma((2, 3)), dma((2,)),
        ],
        compiler_params=pltpu.CompilerParams(collective_id=1, has_side_effects=True, vmem_limit_bytes=60 * 1024 * 1024),
        name="backward_scatter",
    )(*gathered, *shards, *[kept[k] for k in order], qrow, kcol, gain1, gain2, gainqk, cos, sin, ones)
    return out[0], out[1], out[2], out[3:9]


def rope_tables(length, width):
    k = np.arange(width // 2)
    angles = np.arange(length)[:, None] * (THETA ** (-2.0 * k / width))[None]
    cos, sin = np.cos(angles), np.sin(angles)
    return (
        jnp.asarray(np.concatenate([cos] * 4, axis=1), F32),
        jnp.asarray(np.concatenate([-sin, sin] * 2, axis=1), F32),
    )


def per_device(n_dp, inputs, query_weight, key_weight, value_weight, out_weight, gate_weight, up_weight, down_weight,
               attn_gain, ffn_gain, query_gain, key_gain, cotangent, segment_ids, padding, row_count):
    slots, _, width = inputs.shape
    seq_len = segment_ids.shape[1]
    head_dim = query_gain.shape[0]
    nq, nk = query_weight.shape[1], key_weight.shape[1]
    z = lax.axis_index("tensor")
    c = lax.axis_index("dp") % 2
    groups = n_dp // 8
    half = seq_len // 2

    alive_all = padding * (jnp.arange(slots)[:, None] < row_count[0]).astype(jnp.int32)
    code = (segment_ids + ALIVE * alive_all)[z % 2]
    code = jnp.where(c == z // 2, code, lax.ppermute(code, "dp", [(i, i ^ 1) for i in range(n_dp)]))
    segment, alive_row = code % ALIVE, code // ALIVE
    key_code = jnp.where(alive_row > 0, segment, -1)
    alive_own = lax.dynamic_slice_in_dim(alive_row, c * half, half).astype(F32)

    qkv_shard = jnp.concatenate([query_weight, key_weight, value_weight], axis=1)
    cos, sin = rope_tables(seq_len, head_dim)
    gain_qk = jnp.concatenate([query_gain] * (nq // head_dim) + [key_gain] * (nk // head_dim))[None]
    lanes = np.arange(nq + nk) // head_dim
    ones = jnp.asarray(np.where(lanes[:, None] == lanes[None], 1.0 / head_dim, 0.0), BF16)
    gain1, gain2 = attn_gain[None], ffn_gain[None]
    ffn_shards = (gate_weight, up_weight, down_weight)
    gathered, kept = first_part(
        inputs, cotangent, (qkv_shard, out_weight) + ffn_shards, segment[:, None], key_code[None], alive_own[:, None],
        gain1, gain2, gain_qk, cos, sin, ones,
    )
    outs, in_grad, gains, sums = second_part(
        gathered, ffn_shards, kept, segment[None], key_code[:, None], gain1, gain2, gain_qk, cos, sin, ones
    )
    if groups > 1:
        same = [[g * 8 + k for g in range(groups)] for k in range(8)]
        sums = [lax.psum_scatter(s, "dp", scatter_dimension=0, axis_index_groups=same, tiled=True) for s in sums]
        gains = lax.psum(gains, "dp", axis_index_groups=same)
    down_sum, out_sum, qkv_sum = sums[3:]
    pair = gains[16:18, :head_dim] + gains[16:18, head_dim:]
    return (
        outs,
        in_grad.astype(F32),
        qkv_sum[:, :nq],
        qkv_sum[:, nq : nq + nk],
        qkv_sum[:, nq + nk :],
        out_sum,
        jnp.concatenate([s[:, :TILE] for s in sums[:3]], axis=1),
        jnp.concatenate([s[:, TILE:] for s in sums[:3]], axis=1),
        down_sum,
        gains[:8].reshape(-1),
        gains[8:16].reshape(-1),
        pair[0],
        pair[1],
    )


def solution(mesh):
    return jax.shard_map(
        functools.partial(per_device, mesh.shape["dp"]),
        mesh=mesh,
        in_specs=(
            P("dp", "tensor", None),
            P(None, "tensor"),
            P(None, "tensor"),
            P(None, "tensor"),
            P("tensor", None),
            P(None, "tensor"),
            P(None, "tensor"),
            P("tensor", None),
            P(),
            P(),
            P(),
            P(),
            P("dp", "tensor", None),
            P("dp", None),
            P("dp", None),
            P("dp"),
        ),
        out_specs=(
            P("dp", "tensor", None),
            P("dp", "tensor", None),
            P("dp", "tensor"),
            P("dp", "tensor"),
            P("dp", "tensor"),
            P(("tensor", "dp"), None),
            P("dp", "tensor"),
            P("dp", "tensor"),
            P(("tensor", "dp"), None),
            P(),
            P(),
            P(),
            P(),
        ),
        check_vma=False,
    )
```

```python
import functools

import jax
import jax.numpy as jnp
import numpy as np
from jax import lax
from jax.experimental import pallas as pl
from jax.experimental.pallas import tpu as pltpu
from jax.sharding import PartitionSpec as P

EPS = 1e-05
THETA = 1000000.0
ALIVE = 4096
MESH = pl.DeviceIdType.MESH
BF16 = jnp.bfloat16
F32 = jnp.float32


class Place:
    def __init__(self):
        self.dp = lax.axis_index("dp")
        self.z = lax.axis_index("tensor")
        self.c = lax.rem(self.dp, 2)
        self.j = lax.rem(self.dp // 2, 4)
        self.half = self.z // 2
        self.par = lax.rem(self.z, 2)
        self.near = self.half == self.c

    def plane(self, k):
        j = self.j
        bit = lax.rem(j // k, 2)
        return (self.dp + (1 - 2 * bit) * 2 * k, self.z)

    def column(self, c, z):
        return (self.dp - self.c + c, z)

    def quarter(self, k):
        j = self.j
        low, high = lax.rem(j, 2), j // 2
        if k & 1:
            low = 1 - low
        if k & 2:
            high = 1 - high
        return 2 * high + low


def greet(place):
    barrier = pltpu.get_barrier_semaphore()
    for k in (1, 2):
        pl.semaphore_signal(barrier, inc=1, device_id=place.plane(k), device_id_type=MESH)
    for dc in range(2):
        for dz in range(4):
            if dc or dz:
                c = lax.rem(place.c + dc, 2)
                z = lax.rem(place.z + dz, 4)
                pl.semaphore_signal(barrier, inc=1, device_id=place.column(c, z), device_id_type=MESH)
    pl.semaphore_wait(barrier, 9)


def remote(src, dst, send, recv, device):
    return pltpu.make_async_remote_copy(
        src_ref=src, dst_ref=dst, send_sem=send, recv_sem=recv, device_id=device, device_id_type=MESH
    )


def lane_swap(v):
    lane = lax.broadcasted_iota(jnp.int32, v.shape, 1)
    return jnp.where(lane % 64 < 32, pltpu.roll(v, 96, 1), pltpu.roll(v, 32, 1))


def head_mean(v, ones_ref, n):
    high = v.astype(BF16)
    low = (v - high.astype(F32)).astype(BF16)
    ones = ones_ref[:n, :n]
    return jnp.dot(high, ones, preferred_element_type=F32) + jnp.dot(low, ones, preferred_element_type=F32)


def mm(a, b):
    return jnp.dot(a, b, preferred_element_type=F32)


def mm_nt(a, b):
    return lax.dot_general(a, b, (((1,), (1,)), ((), ())), preferred_element_type=F32)


def mm_tn(a, b):
    return lax.dot_general(a, b, (((0,), (0,)), ((), ())), preferred_element_type=F32)


BLK = 256


def rows_at(start, size):
    return pl.ds(pl.multiple_of(start, size), size)


def first_kernel(x_ref, ct_ref, wqkv_ref, wo_ref, wg_ref, wu_ref, wd_ref, qcode_ref, kcode_ref, alive_ref, gain1_ref,
                 gain2_ref, gainqk_ref, cos_ref, sin_ref, ones_ref,
                 gg, gu, gd, o_wqkv, o_wo, o_x, o_din, o_normed, o_n2, o_hidden, o_qk, o_q, o_k, o_v, o_att, o_linv,
                 wqkv, wo, xbuf, cbuf, normed, n2, din, hidden, qk, qs, k2, v2, mask, att, linv, give, take,
                 tok_s, tok_r, tok_l, own_l, zs, zr, fs, fr, ms, mr, outs):
    shards = (wqkv_ref, wo_ref, wg_ref, wu_ref, wd_ref)
    full = (wqkv, wo, gg, gu, gd)
    nw = 5
    place = Place()
    z, c, par, near, j = place.z, place.c, place.par, place.near, place.j
    inner = jnp.where(c == 0, z == 2, z == 1)
    outer = jnp.where(c == 0, z == 3, z == 0)
    seg = x_ref.shape[1]
    half = 2 * seg
    seq = 2 * half
    mate = place.column(1 - c, z)
    greet(place)

    def token_copies(a, src, dst, go):
        for b in range(2):
            slot = par if b == 0 else 1 - par
            target = place.column(place.half, 2 * c + slot)
            here = dst.at[rows_at(par * seg, seg)]

            def far_copy():
                cp = remote(src.at[slot], here, tok_s.at[a, b], tok_r.at[a, par], target)
                cp.start() if go else cp.wait_send()

            if b == 0:
                @pl.when(near)
                def _():
                    cp = pltpu.make_async_copy(src.at[slot], here, tok_l.at[a])
                    cp.start() if go else cp.wait()

                pl.when(jnp.logical_not(near))(far_copy)
            else:
                far_copy()

    def token_arrivals(a, src, dst):
        @pl.when(near)
        def _():
            pltpu.make_async_copy(src.at[par], dst.at[rows_at(par * seg, seg)], tok_l.at[a]).wait()

        for h in range(2):
            @pl.when(jnp.logical_not(near & (par == h)))
            def _():
                remote(src.at[0], dst.at[pl.ds(h * seg, seg)], tok_s.at[a, 0], tok_r.at[a, h], place.plane(1)).wait_recv()

    def token_sent(a, src, dst):
        for b in range(2):
            slot = par if b == 0 else 1 - par

            def wait():
                remote(src.at[slot], dst.at[pl.ds(0, seg)], tok_s.at[a, b], tok_r.at[a, 0], place.plane(1)).wait_send()

            if b == 0:
                pl.when(jnp.logical_not(near))(wait)
            else:
                wait()

    pieces = []
    for w in range(nw):
        q = shards[w].shape[0] // 4
        if w < 2:
            pieces.append((w, 0, q))
        else:
            cut = (q // 2 + 31) // 32 * 32
            pieces += [(w, 0, cut), (w, cut, q - cut)]
    QKV_, O_, G0, G1, U0, U1, D0, D1 = range(8)

    def part(n, p, k, side=None):
        w, at, size = pieces[n]
        q = shards[w].shape[0] // 4
        start = pl.multiple_of(place.quarter(k) * q + at, 16)
        if side is not None:
            size = size // 2
            start = pl.multiple_of(start + side * size, 16)
        return full[w].at[p, pl.ds(start, size)]

    def z_copies(n, go):
        w, at, size = pieces[n]
        q = shards[w].shape[0] // 4

        @pl.when(near)
        def _():
            rows = pl.ds(pl.multiple_of(j * q + at, 16), size)
            for i, to in enumerate((2 - c, 2 * place.half + 1 - par)):
                cp = remote(shards[w].at[rows], part(n, par, 0), zs.at[n, i], zr.at[n, par], place.column(c, to))
                cp.start() if go else cp.wait_send()

    def z_onward(n, p):
        return remote(part(n, p, 0), part(n, p, 0), zs.at[n, p], zr.at[n, p], place.column(c, 3 - 3 * c))

    def missing(p, body):
        pl.when(jnp.logical_or(jnp.logical_not(near), par != p))(body)

    def step_copy(n, p, i):
        k, side, to = ((0, None, 1), (0, None, 2), (1, 0, 2), (2, 1, 1))[i]
        return remote(part(n, p, k, side), part(n, p, k, side), fs.at[n, p, i], fr.at[n, p, i], place.plane(to))

    def first(n):
        for p in range(2):
            @functools.partial(missing, p)
            def _():
                z_onward(n, p).wait_recv()
                pl.when(inner)(lambda: z_onward(n, p).start())
                step_copy(n, p, 0).start()
                step_copy(n, p, 1).start()

    def second(n):
        for p in range(2):
            @functools.partial(missing, p)
            def _():
                step_copy(n, p, 0).wait_recv()
                step_copy(n, p, 2).start()
                step_copy(n, p, 1).wait_recv()
                step_copy(n, p, 3).start()

    def third(n):
        for p in range(2):
            @functools.partial(missing, p)
            def _():
                step_copy(n, p, 2).wait_recv()
                step_copy(n, p, 3).wait_recv()

    def sent(n):
        z_copies(n, False)
        for p in range(2):
            @functools.partial(missing, p)
            def _():
                pl.when(inner)(lambda: z_onward(n, p).wait_send())
                for i in range(4):
                    step_copy(n, p, i).wait_send()

    def own_load(w):
        return pltpu.make_async_copy(shards[w], full[w].at[par], own_l.at[w])

    def save(n, src, dst):
        cp = pltpu.make_async_copy(src, dst, outs.at[n])
        saves.append(cp)
        cp.start()

    saves = []

    for n in range(len(pieces)):
        z_copies(n, True)
        if n < 2:
            pl.when(near)(lambda: own_load(n).start())
        if n == U0:
            token_copies(0, x_ref, xbuf, True)
    token_copies(1, ct_ref, cbuf, True)

    for i in range(seq // BLK):
        for jb in range(i + 1):
            same = qcode_ref[i * BLK : (i + 1) * BLK, :] == kcode_ref[:, jb * BLK : (jb + 1) * BLK]
            if i == jb:
                ri = lax.broadcasted_iota(jnp.int32, (BLK, BLK), 0)
                ci = lax.broadcasted_iota(jnp.int32, (BLK, BLK), 1)
                same = jnp.logical_or(ri == ci, jnp.logical_and(ci < ri, same))
            mask[i * BLK : (i + 1) * BLK, jb * BLK : (jb + 1) * BLK] = jnp.where(same, 1.0, 0.0).astype(F32)
    v2[:, :, 128:] = jnp.ones((v2.shape[0], v2.shape[1], 128), BF16)

    first(QKV_)
    first(O_)
    second(QKV_)
    first(G0)
    second(O_)
    first(G1)
    second(G0)
    first(U0)
    second(G1)

    token_arrivals(0, x_ref, xbuf)
    step = 128

    @pl.loop(0, half // step)
    def _(r):
        xs = xbuf[rows_at(r * step, step), :].astype(F32)
        sc = lax.rsqrt(jnp.mean(xs * xs, axis=-1, keepdims=True) + EPS)
        normed[rows_at(c * half + r * step, step), :] = (xs * sc * gain1_ref[...]).astype(BF16)

    def swap_rows(buf, n):
        own = rows_at(c * half, half)
        return remote(buf.at[own], buf.at[own], ms.at[n], mr.at[n], mate)

    def swap_wait(buf, n):
        remote(buf.at[rows_at((1 - c) * half, half)], buf.at[rows_at((1 - c) * half, half)], ms.at[n], mr.at[n], mate).wait_recv()

    swap_rows(normed, 0).start()
    second(U0)
    first(U1)
    save(0, xbuf, o_x)
    swap_wait(normed, 0)
    save(1, normed, o_normed)
    pl.when(near)(lambda: own_load(0).wait())
    third(QKV_)

    @pl.loop(0, seq // BLK)
    def _(r):
        rows = rows_at(r * BLK, BLK)
        cos, sin = cos_ref[rows, :], sin_ref[rows, :]
        lane = lax.broadcasted_iota(jnp.int32, (BLK, 128), 1)
        left = lane < 64
        for p in range(2):
            proj = mm(normed[rows, :], wqkv[p])
            pq = proj[:, :384]
            qk[p, rows, :] = pq
            sc = lax.rsqrt(head_mean(pq * pq, ones_ref, 384) + EPS)
            n = pq * sc * gainqk_ref[...]
            for s in range(3):
                v = n[:, s * 128 : (s + 1) * 128]
                rot = v * cos + lane_swap(v) * sin
                if s < 2:
                    qr = rot.astype(BF16).astype(F32) * 0.125
                    qs[2 * p + s, 0, rows, :] = jnp.where(left, qr, 0.0).astype(BF16)
                    qs[2 * p + s, 1, rows, :] = jnp.where(left, 0.0, qr).astype(BF16)
                else:
                    kr = pltpu.roll(rot, 64, 1)
                    k2[2 * p, rows, :] = jnp.where(left, rot, kr).astype(BF16)
                    k2[2 * p + 1, rows, :] = jnp.where(left, kr, rot).astype(BF16)
            v = proj[:, 384:]
            vr = pltpu.roll(v, 64, 1)
            v2[2 * p, rows, :128] = jnp.where(left, v, vr).astype(BF16)
            v2[2 * p + 1, rows, :128] = jnp.where(left, vr, v).astype(BF16)

    save(2, wqkv, o_wqkv)
    save(3, qk, o_qk)
    save(4, qs, o_q)
    save(5, k2, o_k)
    save(6, v2.at[:, :, pl.ds(0, 128)], o_v)
    first(D0)
    second(U1)
    for i in range(seq // BLK):
        n = (i + 1) * BLK
        rows = pl.ds(i * BLK, BLK)

        @pl.loop(0, k2.shape[0])
        def _(g):
            s = mm_nt(qs[g, :, rows, :].reshape(2 * BLK, 128), k2[g, :n, :])
            e = jnp.exp(s).reshape(2, BLK, n) * mask[rows, :n][None]
            acc = mm(e.astype(BF16).reshape(2 * BLK, n), v2[g, :n, :])
            inv = 1.0 / acc[:, 128:]
            o = acc[:, :128] * inv
            left = lax.broadcasted_iota(jnp.int32, (BLK, 128), 1) < 64
            cols = pl.ds(pl.multiple_of(g * 128, 128), 128)
            att[rows, cols] = jnp.where(left, o[:BLK], o[BLK:]).astype(BF16)
            linv[rows, cols] = jnp.where(left, inv[:BLK], inv[BLK:])

        if i == 1:
            first(D1)
            second(D0)
    save(7, att, o_att)
    save(8, linv, o_linv)
    pl.when(near)(lambda: own_load(1).wait())
    third(O_)
    save(9, wo, o_wo)

    def out_rows(start):
        return mm(att[rows_at(start, BLK), :], wo[...].reshape(2 * wo.shape[1], wo.shape[2]))

    @pl.loop(0, half // BLK)
    def _(r):
        give[rows_at(r * BLK, BLK), :] = out_rows((1 - c) * half + r * BLK).astype(BF16)

    swap_give = remote(give, take, ms.at[1], mr.at[1], mate)
    swap_give.start()

    @pl.loop(0, half // BLK)
    def _(r):
        hidden[rows_at(r * BLK, BLK), :] = out_rows(c * half + r * BLK) + xbuf[rows_at(r * BLK, BLK), :].astype(F32)

    second(D1)
    swap_give.wait_recv()

    @pl.loop(0, half // step)
    def _(r):
        h = hidden[rows_at(r * step, step), :] + take[rows_at(r * step, step), :].astype(F32)
        hidden[rows_at(r * step, step), :] = h
        sc = lax.rsqrt(jnp.mean(h * h, axis=-1, keepdims=True) + EPS)
        n2[rows_at(c * half + r * step, step), :] = (h * sc * gain2_ref[...]).astype(BF16)

    swap_rows(n2, 2).start()
    save(10, hidden, o_hidden)
    token_arrivals(1, ct_ref, cbuf)

    @pl.loop(0, half // step)
    def _(r):
        v = cbuf[rows_at(r * step, step), :].astype(F32) * alive_ref[rows_at(r * step, step), :]
        din[rows_at(c * half + r * step, step), :] = v.astype(BF16)

    swap_rows(din, 3).start()
    swap_wait(n2, 2)
    save(11, n2, o_n2)
    swap_wait(din, 3)
    save(12, din, o_din)
    for n in range(2, len(pieces)):
        third(n)
    for n in range(len(pieces)):
        sent(n)
    token_sent(0, x_ref, xbuf)
    token_sent(1, ct_ref, cbuf)
    swap_rows(normed, 0).wait_send()
    swap_give.wait_send()
    swap_rows(n2, 2).wait_send()
    swap_rows(din, 3).wait_send()
    for cp in saves:
        cp.wait()


def first_part(x, ct, shards, qcode, kcode, alive, gain1, gain2, gainqk, cos, sin, ones):
    anywhere = pl.BlockSpec(memory_space=pl.ANY)
    vmem = pl.BlockSpec(memory_space=pltpu.VMEM)
    dma = pltpu.SemaphoreType.DMA
    seg, width = x.shape[1], x.shape[2]
    half, seq = 2 * seg, 4 * seg
    wqkv, wo, wg, wu, wd = shards
    groups = 4
    SDS = jax.ShapeDtypeStruct
    kept = dict(
        wqkv=((2,) + wqkv.shape, BF16), wo=((2,) + wo.shape, BF16), x=((half, width), BF16), din=((seq, width), BF16),
        normed=((seq, width), BF16), n2=((seq, width), BF16), hidden=((half, width), F32), qk=((2, seq, 384), F32),
        q=((groups, 2, seq, 128), BF16), k=((groups, seq, 128), BF16), v=((groups, seq, 128), BF16), att=((seq, 512), BF16),
        linv=((seq, 512), F32),
    )
    order = ("wqkv", "wo", "x", "din", "normed", "n2", "hidden", "qk", "q", "k", "v", "att", "linv")
    out_shape = [SDS((2,) + w.shape, BF16) for w in (wg, wu, wd)] + [SDS(*kept[k]) for k in order]

    def vm(k):
        return pltpu.VMEM(*kept[k])

    nw = 5
    out = pl.pallas_call(
        first_kernel,
        out_shape=out_shape,
        in_specs=[anywhere] * 7 + [vmem] * 9,
        out_specs=[anywhere] * len(out_shape),
        scratch_shapes=[
            vm("wqkv"), vm("wo"), vm("x"), pltpu.VMEM((half, width), BF16), vm("normed"), vm("n2"), vm("din"), vm("hidden"), vm("qk"),
            vm("q"), vm("k"), pltpu.VMEM((groups, seq, 256), BF16), pltpu.VMEM((seq, seq), F32), vm("att"), vm("linv"), pltpu.VMEM((half, width), BF16),
            pltpu.VMEM((half, width), BF16),
            dma((2, 2)), dma((2, 2)), dma((2,)), dma((2,)), dma((8, 2)), dma((8, 2)), dma((8, 2, 4)), dma((8, 2, 4)),
            dma((4,)), dma((4,)), dma((13,)),
        ],
        compiler_params=pltpu.CompilerParams(collective_id=0, has_side_effects=True, vmem_limit_bytes=60 * 1024 * 1024),
        name="gather_attention",
    )(x, ct, *shards, qcode, kcode, alive, gain1, gain2, gainqk, cos, sin, ones)
    gathered, rest = out[:3], dict(zip(order, out[3:]))
    return gathered, rest


TILE = 384
PIECES = 3


def second_kernel(gg, gu, gd, wg_ref, wu_ref, wd_ref, wqkv_ref, wo_ref, x_ref, din_ref, normed_ref, n2_ref, hidden_ref, qk_ref,
                  q_ref, k_ref, v_ref, att_ref, linv_ref, qrow_ref, kcol_ref, gain1_ref, gain2_ref, gainqk_ref, cos_ref, sin_ref,
                  ones_ref,
                  oo, io, gain_out, s_gu0, s_gu1, s_gu2, s_d, s_o, s_qkv,
                  p_gu0, p_gu1, p_gu2, p_d, p_o, p_qkv, c_gu0, c_gu1, c_gu2, c_d, c_o, c_qkv,
                  g_a, g_b, g_c, g_d, g_o, g_qkv, d_gu0, d_gu1, d_gu2, d_d, d_o, d_qkv, stage, last, give, take, obuf, hgrad,
                  gain_in, attn_in,
                  tok_s, tok_r, tok_l, ps, pr, cs, cr, ls, lr, ll, gs, gr, ms, mr, ld, wl, st_sem):
    grads = (g_a, g_b, g_c, g_d, g_o, g_qkv)
    diag = (d_gu0, d_gu1, d_gu2, d_d, d_o, d_qkv)
    plane_in = (p_gu0, p_gu1, p_gu2, p_d, p_o, p_qkv)
    col_in = (c_gu0, c_gu1, c_gu2, c_d, c_o, c_qkv)
    sums = (s_gu0, s_gu1, s_gu2, s_d, s_o, s_qkv)
    nw = 6
    D_, O_, QKV_ = 3, 4, 5
    place = Place()
    z, c, par, near, j = place.z, place.c, place.par, place.near, place.j
    inner = jnp.where(c == 0, z == 2, z == 1)
    outer = jnp.where(c == 0, z == 3, z == 0)
    half = obuf.shape[0]
    seq = 2 * half
    seg = half // 2
    width = obuf.shape[1]
    mate = place.column(1 - c, z)
    own_at = c * half
    other_at = (1 - c) * half
    step = 128
    greet(place)

    def token_copies(a, src, dst, go):
        for b in range(2):
            h = par if b == 0 else 1 - par
            piece = src.at[rows_at(h * seg, seg)]
            target = place.column(place.half, 2 * c + h)
            there = dst.at[par]

            def far_copy():
                cp = remote(piece, there, tok_s.at[a, b], tok_r.at[a, par], target)
                cp.start() if go else cp.wait_send()

            if b == 0:
                @pl.when(near)
                def _():
                    cp = pltpu.make_async_copy(piece, there, tok_l.at[a])
                    cp.start() if go else cp.wait()

                pl.when(jnp.logical_not(near))(far_copy)
            else:
                far_copy()

    def token_arrivals(a, src, dst):
        for s in range(2):
            @pl.when(jnp.logical_not(near & (par == s)))
            def _():
                remote(src.at[pl.ds(0, seg)], dst.at[s], tok_s.at[a, 0], tok_r.at[a, s], place.plane(1)).wait_recv()

    def rows_of(w, k, side=None):
        q = grads[w].shape[1] // 4
        start, size = pl.multiple_of(place.quarter(k) * q, q), q
        if side is not None:
            size = q // 2
            start = pl.multiple_of(start + side * size, size)
        return pl.ds(start, size)

    def diag_copy(w, side):
        return remote(grads[w].at[:, rows_of(w, 3, side)], diag[w].at[side], ps.at[w, side], pr.at[w, side], place.plane(1 + side))

    def plane_copy(w, i, side):
        src = grads[w].at[:, rows_of(w, 1 + i, side)] if side == i else diag[w].at[side]
        n = 2 + 2 * i + side
        return remote(src, plane_in[w].at[i, side], ps.at[w, n], pr.at[w, n], place.plane(1 + i))

    def begin(w):
        diag_copy(w, 0).start()
        diag_copy(w, 1).start()
        plane_copy(w, 0, 0).start()
        plane_copy(w, 1, 1).start()

    def add_diag(w):
        for side in (0, 1):
            diag_copy(w, side).wait()
            rows = rows_of(w, 2 - side, side)
            for p in range(2):
                diag[w][side, p] = (grads[w][p, rows, :].astype(F32) + diag[w][side, p].astype(F32)).astype(BF16)
            plane_copy(w, 1 - side, side).start()

    def outer_copy(w):
        return remote(diag[w], col_in[w], cs.at[w, 0], cr.at[w, 0], place.column(c, z - 1 + 2 * c))

    def inner_copy(w, p):
        return remote(diag[w].at[:, p], col_in[w].at[:, 1], cs.at[w, p], cr.at[w, 1], place.column(c, 2 * c + p))

    def near_copy(w):
        to = place.column(c, 2 * place.half + 1 - par)
        return remote(diag[w].at[:, 1 - par], col_in[w].at[:, 0], cs.at[w, 0], cr.at[w, 0], to)

    def staged(w):
        e = grads[w].shape[1] // 8
        return stage.at[:, :, pl.ds(0, e), pl.ds(0, grads[w].shape[2])]

    def add_plane(w):
        for i in range(2):
            for side in range(2):
                plane_copy(w, i, side).wait()
        e, n = grads[w].shape[1] // 8, grads[w].shape[2]
        cps = [pltpu.make_async_copy(plane_in[w].at[:, side], staged(w), st_sem.at[side]) for side in range(2)]
        for side in range(2):
            cps[side].start()
            cps[side].wait()
            rows = rows_of(w, 0, side)
            for p in range(2):
                total = (
                    grads[w][p, rows, :].astype(F32)
                    + stage[0, p, :e, :n].astype(F32)
                    + stage[1, p, :e, :n].astype(F32)
                )
                diag[w][side, p] = total.astype(BF16)
        pl.when(outer)(lambda: outer_copy(w).start())
        pl.when(near)(lambda: near_copy(w).start())

    def load_column(w):
        cp = pltpu.make_async_copy(col_in[w], staged(w), st_sem.at[0])
        cp.start()
        cp.wait()

    def add_outer(w):
        @pl.when(inner)
        def _():
            outer_copy(w).wait_recv()
            load_column(w)
            e, n = grads[w].shape[1] // 8, grads[w].shape[2]
            for p in range(2):
                for side in range(2):
                    diag[w][side, p] = (diag[w][side, p].astype(F32) + stage[side, p, :e, :n].astype(F32)).astype(BF16)
                inner_copy(w, p).start()

    def last_view(w, k):
        return last.at[k, pl.ds(0, grads[w].shape[1] // 8), pl.ds(0, grads[w].shape[2])]

    def last_remote(w):
        return remote(last_view(w, 1), sums[w], ls.at[w], lr.at[w], mate)

    def last_local(w):
        return pltpu.make_async_copy(last_view(w, 0), sums[w], ll.at[w])

    def release_last(w):
        @pl.when(near)
        def _():
            last_remote(w).wait_send()
            last_local(w).wait()

    def add_column(w):
        if w >= 1:
            release_last(w - 1)

        @pl.when(near)
        def _():
            e, n = grads[w].shape[1] // 8, grads[w].shape[2]
            near_copy(w).wait_recv()
            inner_copy(w, 0).wait_recv()
            load_column(w)
            for hc in range(2):
                total = (
                    diag[w][hc, par].astype(F32) + stage[hc, 0, :e, :n].astype(F32) + stage[hc, 1, :e, :n].astype(F32)
                )

                @pl.when(c == hc)
                def _():
                    last[0, :e, :n] = total

                @pl.when(c != hc)
                def _():
                    last[1, :e, :n] = total

            last_remote(w).start()
            last_local(w).start()

    def finish(w):
        pl.when(near)(lambda: near_copy(w).wait_send())
        pl.when(jnp.logical_not(near))(lambda: last_remote(w).wait_recv())
        pl.when(outer)(lambda: outer_copy(w).wait_send())

        @pl.when(inner)
        def _():
            inner_copy(w, 0).wait_send()
            inner_copy(w, 1).wait_send()

    def trade(n):
        return remote(give.at[n % 2], take.at[n % 2], ms.at[n], mr.at[n], mate)

    def load(n, src, dst):
        return pltpu.make_async_copy(src, dst, ld.at[n])

    n2 = attn_in

    def ffn(din, wg, wu, wd, acc_o, acc_n, act, gu_rows):
        loads = [load(0, n2_ref, n2), load(1, din_ref, din)]
        for cp in loads:
            cp.start()

        def tile_loads(t, go):
            cols = pl.ds(t * TILE, TILE)
            for p in range(2):
                here = pl.ds(p * TILE, TILE)

                def run(g, u, d):
                    pairs = ((g.at[:, cols], wg.at[:, here]), (u.at[:, cols], wu.at[:, here]), (d.at[cols], wd.at[here]))
                    for k, (src, dst) in enumerate(pairs):
                        cp = pltpu.make_async_copy(src, dst, wl.at[p, k])
                        cp.start() if go else cp.wait()

                if go:
                    mine = near & (par == p)
                    pl.when(mine)(lambda: run(wg_ref, wu_ref, wd_ref))
                    pl.when(jnp.logical_not(mine))(lambda: run(gg.at[p], gu.at[p], gd.at[p]))
                else:
                    run(gg.at[p], gu.at[p], gd.at[p])

        tile_loads(0, True)
        for cp in loads:
            cp.wait()
        for t in range(PIECES):
            tile_loads(t, False)

            @pl.loop(0, seq // BLK)
            def _(r):
                rows = rows_at(r * BLK, BLK)
                a = n2[rows, :]
                g = mm(a, wg[...])
                u = mm(a, wu[...])
                ag = mm_nt(din[rows, :], wd[...])
                sig = jax.nn.sigmoid(g)
                gs_ = g * sig
                av = (gs_ * u).astype(BF16)
                act[t, rows, :] = av
                gv = (ag * u * (sig + gs_ * (1.0 - sig))).astype(BF16)
                uv = (ag * gs_).astype(BF16)
                for p in range(2):
                    gu_rows[rows, 2 * p * TILE : (2 * p + 1) * TILE] = gv[:, p * TILE : (p + 1) * TILE]
                    gu_rows[rows, (2 * p + 1) * TILE : (2 * p + 2) * TILE] = uv[:, p * TILE : (p + 1) * TILE]
                dn = mm_nt(gv, wg[...]) + mm_nt(uv, wu[...])
                do = mm(av, wd[...])
                if t == 0:
                    acc_n[rows, :] = dn
                    acc_o[rows, :] = do
                else:
                    acc_n[rows, :] += dn
                    acc_o[rows, :] += do

            if t + 1 < PIECES:
                tile_loads(t + 1, True)

            @pl.loop(0, width // BLK)
            def _(r):
                cols = pl.ds(pl.multiple_of(r * BLK, BLK), BLK)
                o = mm_tn(n2[:, cols], gu_rows[...]).astype(BF16)
                for p in range(2):
                    grads[t][p, cols, :] = o[:, 2 * p * TILE : 2 * (p + 1) * TILE]

            begin(t)

        @pl.loop(0, half // BLK)
        def _(r):
            rows = rows_at(r * BLK, BLK)
            give[0, rows, :] = acc_n[rows_at(other_at + r * BLK, BLK), :].astype(BF16)
            give[1, rows, :] = acc_o[rows_at(other_at + r * BLK, BLK), :].astype(BF16)

        trade(0).start()
        trade(1).start()
        hid_load = load(2, hidden_ref, hgrad)
        hid_load.start()
        add_diag(0)
        for p in range(2):
            @pl.loop(0, width // BLK)
            def _(r):
                cols = pl.ds(pl.multiple_of(r * BLK, BLK), BLK)
                for k in range(PIECES):
                    rows = pl.ds(k * TILE, TILE)
                    grads[D_][p, rows, cols] = mm_tn(act[k, :, p * TILE : (p + 1) * TILE], din[:, cols]).astype(BF16)

        begin(D_)
        hid_load.wait()
        trade(0).wait_recv()
        trade(1).wait_recv()
        gain_out[8:16, :] = jnp.zeros((8, 128), F32)

        @pl.loop(0, half // step)
        def _(r):
            rows = rows_at(r * step, step)
            own = rows_at(own_at + r * step, step)
            h = hgrad[rows, :]
            obuf[rows, :] = (h + acc_o[own, :] + take[1, rows, :].astype(F32)).astype(BF16)
            ng = acc_n[own, :] + take[0, rows, :].astype(F32)
            sc = lax.rsqrt(jnp.mean(h * h, axis=-1, keepdims=True) + EPS)
            unit = h * sc
            acc_gain(8, ng * unit)
            e = ng * gain2_ref[...]
            hg = din[own, :].astype(F32) + sc * (e - unit * jnp.mean(e * unit, axis=-1, keepdims=True))
            hgrad[rows, :] = hg
            attn_in[own, :] = hg.astype(BF16)

        token_copies(0, obuf, oo, True)

    def acc_gain(at, v):
        s = jnp.sum(v, axis=0, keepdims=True)
        for k in range(width // 128):
            gain_out[at + k : at + k + 1, :] += s[:, k * 128 : (k + 1) * 128]

    gain_out[...] = jnp.zeros(gain_out.shape, F32)
    pl.run_scoped(
        ffn,
        pltpu.VMEM((seq, width), BF16),
        pltpu.VMEM((width, 2 * TILE), BF16), pltpu.VMEM((width, 2 * TILE), BF16), pltpu.VMEM((2 * TILE, width), BF16),
        pltpu.VMEM((seq, width), F32), pltpu.VMEM((seq, width), F32), pltpu.VMEM((PIECES, seq, 2 * TILE), BF16),
        pltpu.VMEM((seq, 4 * TILE), BF16),
    )

    def attn_swap():
        own = rows_at(own_at, half)
        return remote(attn_in.at[own], attn_in.at[own], ms.at[3], mr.at[3], mate)

    attn_swap().start()

    def attention(dos, dq, dk, dv, drow):
        def front(wo, att, linv):
            loads = [load(3, wo_ref, wo), load(4, att_ref, att), load(5, linv_ref, linv)]
            for cp in loads:
                cp.start()
            add_diag(1)
            for cp in loads:
                cp.wait()
            other = rows_at(other_at, half)
            remote(attn_in.at[other], attn_in.at[other], ms.at[3], mr.at[3], mate).wait_recv()

            @pl.loop(0, seq // BLK)
            def _(r):
                rows = rows_at(r * BLK, BLK)
                left = lax.broadcasted_iota(jnp.int32, (BLK, 128), 1) < 64
                for p in range(2):
                    ag = mm_nt(attn_in[rows, :], wo[p]).astype(BF16).astype(F32)
                    for s in range(2):
                        g = 2 * p + s
                        cols = slice(g * 128, (g + 1) * 128)
                        d = ag[:, s * 128 : (s + 1) * 128] * linv[rows, cols]
                        d0, d1 = jnp.where(left, d, 0.0).astype(BF16), jnp.where(left, 0.0, d).astype(BF16)
                        dos[g, 0, rows, :] = d0
                        dos[g, 1, rows, :] = d1
                        o = att[rows, cols].astype(F32)
                        one = jnp.ones((8, 128), BF16)
                        for k, dd in enumerate((d0, d1)):
                            prod = dd.astype(F32) * o
                            high = prod.astype(BF16)
                            low = (prod - high.astype(F32)).astype(BF16)
                            drow[g, k, :, rows] = mm_nt(one, high) + mm_nt(one, low)

            @pl.loop(0, width // BLK)
            def _(r):
                cols = pl.ds(pl.multiple_of(r * BLK, BLK), BLK)
                for p in range(2):
                    grads[O_][p, :, cols] = mm_tn(att[:, p * 256 : (p + 1) * 256], attn_in[:, cols]).astype(BF16)

            begin(O_)
            add_plane(0)
            add_diag(2)

        pl.run_scoped(
            front, pltpu.VMEM(wo_ref.shape, BF16), pltpu.VMEM(att_ref.shape, BF16), pltpu.VMEM(linv_ref.shape, F32),
        )
        def rest(q, k, v, mt, qk, rows_, wqkv, normed):
            trade(1).wait_send()
            x = give.at[1]
            loads = [load(6, q_ref, q), load(7, k_ref, k), load(8, v_ref, v)]
            later = [load(9, qk_ref, qk), load(10, wqkv_ref, wqkv), load(11, normed_ref, normed), load(12, x_ref, x)]
            for cp in loads + later:
                cp.start()
            for cp in loads:
                cp.wait()
            dq[...] = jnp.zeros(dq.shape, F32)
            todo = {0: [], 1: [], 2: [lambda: add_diag(O_)], 3: [lambda: add_outer(0), lambda: add_plane(1), lambda: add_diag(D_)]}
            for jb in range(seq // BLK):
                at = jb * BLK
                ni = seq - at
                keys = pl.ds(at, BLK)
                cols = pl.ds(at, ni)
                ki = lax.broadcasted_iota(jnp.int32, (BLK, ni), 0)
                qi = lax.broadcasted_iota(jnp.int32, (BLK, ni), 1)
                same = jnp.logical_and(ki < qi, kcol_ref[keys, :] == qrow_ref[:, cols])
                mt[:, :ni] = jnp.where(jnp.logical_or(ki == qi, same), 1.0, 0.0).astype(F32)

                @pl.loop(0, 4)
                def _(g):
                    kb = k[g, keys, :]
                    qb = q[g, :, cols, :].reshape(2 * ni, 128)
                    db = dos[g, :, cols, :].reshape(2 * ni, 128)
                    m = mt[:, :ni]
                    e = jnp.exp(mm_nt(kb, qb)) * jnp.concatenate([m, m], axis=1)
                    dv[g, keys, :] = mm(e.astype(BF16), db)
                    dp = mm_nt(v[g, keys, :], db)
                    dr = jnp.concatenate([drow[g, 0, :1, cols], drow[g, 1, :1, cols]], axis=1)
                    ds = (e * (dp - dr)).astype(BF16)
                    dk[g, keys, :] = mm(ds, qb)
                    dqs = mm_tn(ds, kb)
                    left = lax.broadcasted_iota(jnp.int32, (ni, 128), 1) < 64
                    lanes = pl.ds(pl.multiple_of(g * 128, 128), 128)
                    dq[cols, lanes] += jnp.where(left, dqs[:ni], dqs[ni:])

                for f in todo[jb]:
                    f()
            for cp in later:
                cp.wait()

            @pl.loop(0, seq // BLK)
            def _(r):
                rows = rows_at(r * BLK, BLK)
                cos, sin = cos_ref[rows, :], sin_ref[rows, :]
                left = lax.broadcasted_iota(jnp.int32, (BLK, 128), 1) < 64

                def fold(ref, p):
                    a, b = ref[2 * p, rows, :], ref[2 * p + 1, rows, :]
                    return jnp.where(left, a + pltpu.roll(a, 64, 1), b + pltpu.roll(b, 64, 1))

                for p in range(2):
                    raw = qk[p, rows, :]
                    sc = lax.rsqrt(head_mean(raw * raw, ones_ref, 384) + EPS)
                    unit = raw * sc
                    parts = []
                    for s in range(3):
                        if s < 2:
                            v_ = dq[rows, (2 * p + s) * 128 : (2 * p + s + 1) * 128] * 0.125
                        else:
                            v_ = fold(dk, p)
                        v_ = v_.astype(BF16).astype(F32)
                        parts.append(v_ * cos - lane_swap(v_) * sin)
                    ng = jnp.concatenate(parts, axis=1)
                    gsum = jnp.sum(ng * unit, axis=0, keepdims=True)
                    qsum = gsum[:, :128] + gsum[:, 128:256]
                    ksum = gsum[:, 256:]
                    gain_out[16:17, :] += qsum
                    gain_out[17:18, :] += ksum
                    e = ng * gainqk_ref[...]
                    back = sc * (e - unit * head_mean(e * unit, ones_ref, 384))
                    rows_[p, rows, :384] = back.astype(BF16)
                    rows_[p, rows, 384:] = fold(dv, p).astype(BF16)

            def back_rows(start):
                at = rows_at(start, BLK)
                return mm_nt(rows_[0, at, :], wqkv[0]) + mm_nt(rows_[1, at, :], wqkv[1])

            trade(0).wait_send()

            @pl.loop(0, half // BLK)
            def _(r):
                give[0, rows_at(r * BLK, BLK), :] = back_rows(other_at + r * BLK).astype(BF16)

            trade(2).start()
            for p in range(2):
                @pl.loop(0, width // BLK)
                def _(r):
                    cols = pl.ds(pl.multiple_of(r * BLK, BLK), BLK)
                    grads[QKV_][p, cols, :] = mm_tn(normed[:, cols], rows_[p]).astype(BF16)

            begin(QKV_)
            trade(2).wait_recv()
            token_copies(0, obuf, oo, False)

            @pl.loop(0, half // BLK)
            def _(r):
                rows = rows_at(r * BLK, BLK)
                ng = back_rows(own_at + r * BLK) + take[0, rows, :].astype(F32)
                xs = x[rows, :].astype(F32)
                sc = lax.rsqrt(jnp.mean(xs * xs, axis=-1, keepdims=True) + EPS)
                unit = xs * sc
                acc_gain(0, ng * unit)
                e = ng * gain1_ref[...]
                ig = hgrad[rows, :] + sc * (e - unit * jnp.mean(e * unit, axis=-1, keepdims=True))
                obuf[rows, :] = ig.astype(BF16)

        V = pltpu.VMEM
        pl.run_scoped(
            rest, V(q_ref.shape, BF16), V(k_ref.shape, BF16), V(v_ref.shape, BF16), V((BLK, seq), F32), V(qk_ref.shape, F32),
            V((2, seq, 512), BF16), V(wqkv_ref.shape, BF16), V(normed_ref.shape, BF16),
        )

    pl.run_scoped(
        attention, pltpu.VMEM(q_ref.shape, BF16), pltpu.VMEM((seq, 512), F32), pltpu.VMEM((4, seq, 128), F32),
        pltpu.VMEM((4, seq, 128), F32), pltpu.VMEM((4, 2, 8, seq), F32),
    )
    def gain_copy(i):
        to = (place.column(c, 2 * place.half + 1 - par), place.column(c, 2 - 2 * place.half + par), place.plane(1), place.plane(2),
              mate)[i]
        return remote(gain_out, gain_in.at[i], gs.at[i], gr.at[i], to)

    def gain_step(i):
        gain_copy(i).wait()
        gain_out[...] += gain_in[i]
        if i < 4:
            gain_copy(i + 1).start()

    gain_copy(0).start()
    token_copies(1, obuf, io, True)
    add_plane(2)
    add_column(0)
    gain_step(0)
    add_outer(1)
    gain_step(1)
    add_column(1)
    add_plane(D_)
    gain_step(2)
    add_outer(2)
    add_diag(QKV_)
    gain_step(3)
    add_column(2)
    add_plane(O_)
    gain_step(4)
    add_outer(D_)
    add_outer(O_)
    add_plane(QKV_)
    add_column(D_)
    add_column(O_)
    add_outer(QKV_)
    add_column(QKV_)
    release_last(nw - 1)
    for w in range(nw):
        finish(w)
    trade(2).wait_send()
    attn_swap().wait_send()
    token_copies(1, obuf, io, False)
    token_arrivals(0, obuf, oo)
    token_arrivals(1, obuf, io)


def second_part(gathered, shards, kept, qrow, kcol, gain1, gain2, gainqk, cos, sin, ones):
    anywhere = pl.BlockSpec(memory_space=pl.ANY)
    vmem = pl.BlockSpec(memory_space=pltpu.VMEM)
    dma = pltpu.SemaphoreType.DMA
    half, width = kept["x"].shape
    SDS = jax.ShapeDtypeStruct
    wg, wu, wd = shards
    r_d = wd.shape[0]
    sizes = [(width, 2 * TILE)] * 3 + [(r_d, width), (kept["wo"].shape[1], width), (width, kept["wqkv"].shape[2])]
    held = sizes
    nw = 6
    order = ("wqkv", "wo", "x", "din", "normed", "n2", "hidden", "qk", "q", "k", "v", "att", "linv")
    gains = (24, 128)
    out_shape = (
        [SDS((2, half // 2, width), BF16)] * 2
        + [SDS(gains, F32)]
        + [SDS((r // 8, n), F32) for r, n in sizes]
        + [SDS((2, 2, 2, r // 8, n), BF16) for r, n in sizes]
        + [SDS((2, 2, r // 8, n), BF16) for r, n in sizes]
    )
    V = pltpu.VMEM
    e_max, n_max = max(r // 8 for r, _ in sizes), max(n for _, n in sizes)
    out = pl.pallas_call(
        second_kernel,
        out_shape=out_shape,
        in_specs=[anywhere] * (6 + len(order)) + [vmem] * 8,
        out_specs=[anywhere] * 2 + [vmem] + [anywhere] * 18,
        scratch_shapes=[V((2, r, n), BF16) for r, n in held]
        + [V((2, 2, r // 8, n), BF16) for r, n in sizes]
        + [
            V((2, 2, e_max, n_max), BF16), V((2, e_max, n_max), F32), V((2, half, width), BF16), V((2, half, width), BF16),
            V((half, width), BF16), V((half, width), F32), V((5,) + gains, F32), V((2 * half, width), BF16),
        ]
        + [
            dma((2, 2)), dma((2, 2)), dma((2,)), dma((nw, 6)), dma((nw, 6)), dma((nw, 2)), dma((nw, 2)), dma((nw,)), dma((nw,)),
            dma((nw,)), dma((5,)), dma((5,)), dma((4,)), dma((4,)), dma((13,)), dma((2, 3)), dma((2,)),
        ],
        compiler_params=pltpu.CompilerParams(collective_id=1, has_side_effects=True, vmem_limit_bytes=60 * 1024 * 1024),
        name="backward_scatter",
    )(*gathered, *shards, *[kept[k] for k in order], qrow, kcol, gain1, gain2, gainqk, cos, sin, ones)
    return out[0], out[1], out[2], out[3:9]


def rope_tables(length, width):
    k = np.arange(width // 2)
    angles = np.arange(length)[:, None] * (THETA ** (-2.0 * k / width))[None]
    cos, sin = np.cos(angles), np.sin(angles)
    return (
        jnp.asarray(np.concatenate([cos] * 4, axis=1), F32),
        jnp.asarray(np.concatenate([-sin, sin] * 2, axis=1), F32),
    )


def per_device(n_dp, inputs, query_weight, key_weight, value_weight, out_weight, gate_weight, up_weight, down_weight,
               attn_gain, ffn_gain, query_gain, key_gain, cotangent, segment_ids, padding, row_count):
    slots, _, width = inputs.shape
    seq_len = segment_ids.shape[1]
    head_dim = query_gain.shape[0]
    nq, nk = query_weight.shape[1], key_weight.shape[1]
    z = lax.axis_index("tensor")
    c = lax.axis_index("dp") % 2
    groups = n_dp // 8
    half = seq_len // 2

    alive_all = padding * (jnp.arange(slots)[:, None] < row_count[0]).astype(jnp.int32)
    code = (segment_ids + ALIVE * alive_all)[z % 2]
    code = jnp.where(c == z // 2, code, lax.ppermute(code, "dp", [(i, i ^ 1) for i in range(n_dp)]))
    segment, alive_row = code % ALIVE, code // ALIVE
    key_code = jnp.where(alive_row > 0, segment, -1)
    alive_own = lax.dynamic_slice_in_dim(alive_row, c * half, half).astype(F32)

    qkv_shard = jnp.concatenate([query_weight, key_weight, value_weight], axis=1)
    cos, sin = rope_tables(seq_len, head_dim)
    gain_qk = jnp.concatenate([query_gain] * (nq // head_dim) + [key_gain] * (nk // head_dim))[None]
    lanes = np.arange(nq + nk) // head_dim
    ones = jnp.asarray(np.where(lanes[:, None] == lanes[None], 1.0 / head_dim, 0.0), BF16)
    gain1, gain2 = attn_gain[None], ffn_gain[None]
    ffn_shards = (gate_weight, up_weight, down_weight)
    gathered, kept = first_part(
        inputs, cotangent, (qkv_shard, out_weight) + ffn_shards, segment[:, None], key_code[None], alive_own[:, None],
        gain1, gain2, gain_qk, cos, sin, ones,
    )
    outs, in_grad, gains, sums = second_part(
        gathered, ffn_shards, kept, segment[None], key_code[:, None], gain1, gain2, gain_qk, cos, sin, ones
    )
    if groups > 1:
        same = [[g * 8 + k for g in range(groups)] for k in range(8)]
        sums = [lax.psum_scatter(s, "dp", scatter_dimension=0, axis_index_groups=same, tiled=True) for s in sums]
        gains = lax.psum(gains, "dp", axis_index_groups=same)
    down_sum, out_sum, qkv_sum = sums[3:]
    pair = gains[16:18, :head_dim] + gains[16:18, head_dim:]
    return (
        outs,
        in_grad.astype(F32),
        qkv_sum[:, :nq],
        qkv_sum[:, nq : nq + nk],
        qkv_sum[:, nq + nk :],
        out_sum,
        jnp.concatenate([s[:, :TILE] for s in sums[:3]], axis=1),
        jnp.concatenate([s[:, TILE:] for s in sums[:3]], axis=1),
        down_sum,
        gains[:8].reshape(-1),
        gains[8:16].reshape(-1),
        pair[0],
        pair[1],
    )


def solution(mesh):
    return jax.shard_map(
        functools.partial(per_device, mesh.shape["dp"]),
        mesh=mesh,
        in_specs=(
            P("dp", "tensor", None),
            P(None, "tensor"),
            P(None, "tensor"),
            P(None, "tensor"),
            P("tensor", None),
            P(None, "tensor"),
            P(None, "tensor"),
            P("tensor", None),
            P(),
            P(),
            P(),
            P(),
            P("dp", "tensor", None),
            P("dp", None),
            P("dp", None),
            P("dp"),
        ),
        out_specs=(
            P("dp", "tensor", None),
            P("dp", "tensor", None),
            P("dp", "tensor"),
            P("dp", "tensor"),
            P("dp", "tensor"),
            P(("tensor", "dp"), None),
            P("dp", "tensor"),
            P("dp", "tensor"),
            P(("tensor", "dp"), None),
            P(),
            P(),
            P(),
            P(),
        ),
        check_vma=False,
    )
```

```python
import functools

import jax
import jax.numpy as jnp
import numpy as np
from jax import lax
from jax.experimental import pallas as pl
from jax.experimental.pallas import tpu as pltpu
from jax.sharding import PartitionSpec as P

EPS = 1e-05
THETA = 1000000.0
ALIVE = 4096
MESH = pl.DeviceIdType.MESH
BF16 = jnp.bfloat16
F32 = jnp.float32


class Place:
    def __init__(self):
        self.dp = lax.axis_index("dp")
        self.z = lax.axis_index("tensor")
        self.c = lax.rem(self.dp, 2)
        self.j = lax.rem(self.dp // 2, 4)
        self.half = self.z // 2
        self.par = lax.rem(self.z, 2)
        self.near = self.half == self.c

    def plane(self, k):
        j = self.j
        bit = lax.rem(j // k, 2)
        return (self.dp + (1 - 2 * bit) * 2 * k, self.z)

    def column(self, c, z):
        return (self.dp - self.c + c, z)

    def quarter(self, k):
        j = self.j
        low, high = lax.rem(j, 2), j // 2
        if k & 1:
            low = 1 - low
        if k & 2:
            high = 1 - high
        return 2 * high + low


def greet(place):
    barrier = pltpu.get_barrier_semaphore()
    for k in (1, 2):
        pl.semaphore_signal(barrier, inc=1, device_id=place.plane(k), device_id_type=MESH)
    for dc in range(2):
        for dz in range(4):
            if dc or dz:
                c = lax.rem(place.c + dc, 2)
                z = lax.rem(place.z + dz, 4)
                pl.semaphore_signal(barrier, inc=1, device_id=place.column(c, z), device_id_type=MESH)
    pl.semaphore_wait(barrier, 9)


def remote(src, dst, send, recv, device):
    return pltpu.make_async_remote_copy(
        src_ref=src, dst_ref=dst, send_sem=send, recv_sem=recv, device_id=device, device_id_type=MESH
    )


def lane_swap(v):
    lane = lax.broadcasted_iota(jnp.int32, v.shape, 1)
    return jnp.where(lane % 64 < 32, pltpu.roll(v, 96, 1), pltpu.roll(v, 32, 1))


def head_mean(v, ones_ref, n):
    high = v.astype(BF16)
    low = (v - high.astype(F32)).astype(BF16)
    ones = ones_ref[:n, :n]
    return jnp.dot(high, ones, preferred_element_type=F32) + jnp.dot(low, ones, preferred_element_type=F32)


def mm(a, b):
    return jnp.dot(a, b, preferred_element_type=F32)


def mm_nt(a, b):
    return lax.dot_general(a, b, (((1,), (1,)), ((), ())), preferred_element_type=F32)


def mm_tn(a, b):
    return lax.dot_general(a, b, (((0,), (0,)), ((), ())), preferred_element_type=F32)


BLK = 256


def rows_at(start, size):
    return pl.ds(pl.multiple_of(start, size), size)


TILE = 384
PIECES = 3


def layer_kernel(x_ref, ct_ref, wqkv_ref, wo_ref, wg_ref, wu_ref, wd_ref, cols_ref, rows_ref,
                 gain1_ref, gain2_ref, gainqk_ref, cos_ref, sin_ref, ones_ref,
                 oo, io, gain_out, s_q, s_k, s_v, s_o, s_gate, s_up, s_down,
                 gqkv, go, gg, gu, gd, hx, hc, h_normed, h_qk, h_q, h_k, h_v, h_att, h_linv,
                 p_gu0, p_gu1, p_gu2, p_d0, p_d1, p_o, p_qkv, c_gu0, c_gu1, c_gu2, c_d0, c_d1, c_o, c_qkv,
                 g_a, g_b, g_c, g_d0, g_d1, g_o, g_qkv, d_gu0, d_gu1, d_gu2, d_d0, d_d1, d_o, d_qkv, last, give, take, obuf, hgrad,
                 gain_in, attn_in, din,
                 in_s, in_r, tok_s, tok_r, tok_l, zs, zr, fs, fr, ps, pr, cs, cr, ls, lr, ll, gs, gr, ms, mr, ld, wl, pls, cls,
                 outs):
    shards = (wqkv_ref, wo_ref, wg_ref, wu_ref, wd_ref)
    full = (gqkv, go, gg, gu, gd)
    grads = (g_a, g_b, g_c, g_d0, g_d1, g_o, g_qkv)
    diag = (d_gu0, d_gu1, d_gu2, d_d0, d_d1, d_o, d_qkv)
    plane_in = (p_gu0, p_gu1, p_gu2, p_d0, p_d1, p_o, p_qkv)
    col_in = (c_gu0, c_gu1, c_gu2, c_d0, c_d1, c_o, c_qkv)
    nw = 7
    DA_, DB_, O_, QKV_ = 3, 4, 5, 6
    turn = (0, 1, 2, 3, 4, 5, 6)
    place = Place()
    z, c, par, near, j = place.z, place.c, place.par, place.near, place.j
    inner = jnp.where(c == 0, z == 2, z == 1)
    outer = jnp.where(c == 0, z == 3, z == 0)
    half = obuf.shape[0]
    seq = 2 * half
    seg = half // 2
    width = obuf.shape[1]
    mate = place.column(1 - c, z)
    own_at = c * half
    other_at = (1 - c) * half
    step = 128
    n2 = attn_in
    normed_buf = din
    greet(place)

    def fetch_copies(a, src, dst, go):
        for b in range(2):
            slot = par if b == 0 else 1 - par
            target = place.column(place.half, 2 * c + slot)

            def far_copy():
                cp = remote(src.at[slot], dst.at[rows_at(par * seg, seg)], in_s.at[a, b], in_r.at[a, par], target)
                cp.start() if go else cp.wait_send()

            if b == 0:
                pl.when(jnp.logical_not(near))(far_copy)
            else:
                far_copy()

    def fetch_arrivals(a, src, dst):
        for h in range(2):
            @pl.when(jnp.logical_not(near & (par == h)))
            def _():
                remote(src.at[0], dst.at[pl.ds(h * seg, seg)], in_s.at[a, 0], in_r.at[a, h], place.plane(1)).wait_recv()

    def fetch_load(a, src, landed, dst, go):
        for h in range(2):
            here = dst.at[pl.ds(h * seg, seg)]
            came = pltpu.make_async_copy(landed.at[pl.ds(h * seg, seg)], here, tok_l.at[a, h])
            if go:
                mine = near & (par == h)
                pl.when(mine)(lambda: pltpu.make_async_copy(src.at[h], here, tok_l.at[a, h]).start())
                pl.when(jnp.logical_not(mine))(came.start)
            else:
                came.wait()

    pieces = [(0, 256, 0, None), (1, 64, 0, None)]
    for t in range(PIECES):
        pieces += [(2, 256, 0, t), (3, 256, 0, t), (4, TILE // 4, t * TILE, None)]
    WQKV, WO = 0, 1

    def tile_pieces(t):
        return (2 + 3 * t, 3 + 3 * t, 4 + 3 * t)

    def piece_at(ref, n, k, side=None, p=None):
        w, q, at, t = pieces[n]
        start, size = pl.multiple_of(at + place.quarter(k) * q, 16), q
        if side is not None:
            size = q // 2
            start = pl.multiple_of(start + side * size, 16)
        index = (pl.ds(start, size),) + (() if t is None else (pl.ds(t * TILE, TILE),))
        return ref.at[index if p is None else (p,) + index]

    def part(n, p, k, side=None):
        return piece_at(full[pieces[n][0]], n, k, side, p)

    def z_copies(n, go):
        @pl.when(near)
        def _():
            for i, to in enumerate((2 - c, 2 * place.half + 1 - par)):
                cp = remote(piece_at(shards[pieces[n][0]], n, 0), part(n, par, 0), zs.at[n, i], zr.at[n, par], place.column(c, to))
                cp.start() if go else cp.wait_send()

    def z_onward(n, p):
        return remote(part(n, p, 0), part(n, p, 0), zs.at[n, p], zr.at[n, p], place.column(c, 3 - 3 * c))

    def missing(p, body):
        pl.when(jnp.logical_or(jnp.logical_not(near), par != p))(body)

    def step_copy(n, p, i):
        k, side, to = ((0, None, 1), (0, None, 2), (1, 0, 2), (2, 1, 1))[i]
        return remote(part(n, p, k, side), part(n, p, k, side), fs.at[n, p, i], fr.at[n, p, i], place.plane(to))

    def first(n):
        for p in range(2):
            @functools.partial(missing, p)
            def _():
                z_onward(n, p).wait_recv()
                pl.when(inner)(lambda: z_onward(n, p).start())
                step_copy(n, p, 0).start()
                step_copy(n, p, 1).start()

    def second(n):
        for p in range(2):
            @functools.partial(missing, p)
            def _():
                step_copy(n, p, 0).wait_recv()
                step_copy(n, p, 2).start()
                step_copy(n, p, 1).wait_recv()
                step_copy(n, p, 3).start()

    def third(n):
        for p in range(2):
            @functools.partial(missing, p)
            def _():
                step_copy(n, p, 2).wait_recv()
                step_copy(n, p, 3).wait_recv()

    def sent(n):
        z_copies(n, False)
        for p in range(2):
            @functools.partial(missing, p)
            def _():
                pl.when(inner)(lambda: z_onward(n, p).wait_send())
                for i in range(4):
                    step_copy(n, p, i).wait_send()

    def weight_load(w, dst, go):
        for p in range(2):
            came = pltpu.make_async_copy(full[w].at[p], dst.at[p], wl.at[w, p])
            if go:
                mine = near & (par == p)
                pl.when(mine)(lambda: pltpu.make_async_copy(shards[w], dst.at[p], wl.at[w, p]).start())
                pl.when(jnp.logical_not(mine))(came.start)
            else:
                came.wait()

    def token_copies(a, src, dst, go):
        for b in range(2):
            h = par if b == 0 else 1 - par
            piece = src.at[rows_at(h * seg, seg)]
            target = place.column(place.half, 2 * c + h)
            there = dst.at[par]

            def far_copy():
                cp = remote(piece, there, tok_s.at[a, b], tok_r.at[a, par], target)
                cp.start() if go else cp.wait_send()

            if b == 0:
                @pl.when(near)
                def _():
                    cp = pltpu.make_async_copy(piece, there, tok_l.at[a, 0])
                    cp.start() if go else cp.wait()

                pl.when(jnp.logical_not(near))(far_copy)
            else:
                far_copy()

    def token_arrivals(a, src, dst):
        for s in range(2):
            @pl.when(jnp.logical_not(near & (par == s)))
            def _():
                remote(src.at[pl.ds(0, seg)], dst.at[s], tok_s.at[a, 0], tok_r.at[a, s], place.plane(1)).wait_recv()

    def rows_of(w, k, side=None):
        q = grads[w].shape[1] // 4
        start, size = pl.multiple_of(place.quarter(k) * q, q), q
        if side is not None:
            size = q // 2
            start = pl.multiple_of(start + side * size, size)
        return pl.ds(start, size)

    def diag_copy(w, side):
        return remote(grads[w].at[:, rows_of(w, 3, side)], diag[w].at[side], ps.at[w, side], pr.at[w, side], place.plane(1 + side))

    def plane_copy(w, i, side):
        src = grads[w].at[:, rows_of(w, 1 + i, side)] if side == i else diag[w].at[side]
        n = 2 + 2 * i + side
        return remote(src, plane_in[w].at[i, side], ps.at[w, n], pr.at[w, n], place.plane(1 + i))

    def begin(w):
        diag_copy(w, 0).start()
        diag_copy(w, 1).start()
        plane_copy(w, 0, 0).start()
        plane_copy(w, 1, 1).start()

    def add_diag(w):
        for side in (0, 1):
            diag_copy(w, side).wait()
            rows = rows_of(w, 2 - side, side)
            for p in range(2):
                diag[w][side, p] = (grads[w][p, rows, :].astype(F32) + diag[w][side, p].astype(F32)).astype(BF16)
            plane_copy(w, 1 - side, side).start()

    def outer_copy(w):
        return remote(diag[w], col_in[w], cs.at[w, 0], cr.at[w, 0], place.column(c, z - 1 + 2 * c))

    def inner_copy(w, p):
        return remote(diag[w].at[:, p], col_in[w].at[:, 1], cs.at[w, p], cr.at[w, 1], place.column(c, 2 * c + p))

    def near_copy(w):
        to = place.column(c, 2 * place.half + 1 - par)
        return remote(diag[w].at[:, 1 - par], col_in[w].at[:, 0], cs.at[w, 0], cr.at[w, 0], to)

    def plane_local(w, i, side):
        return pltpu.make_async_copy(plane_in[w].at[i, side], grads[w].at[:, rows_of(w, 1 + i, side)], pls.at[w, i, side])

    def col_local(w, side):
        return pltpu.make_async_copy(col_in[w].at[side], grads[w].at[:, rows_of(w, 3, side)], cls.at[w, side])

    def load_plane(w):
        for i in range(2):
            for side in range(2):
                plane_copy(w, i, side).wait()
        for i in range(2):
            for side in range(2):
                plane_local(w, i, side).start()

    def add_plane(w):
        for side in range(2):
            for i in range(2):
                plane_local(w, i, side).wait()
            mine, one, two = rows_of(w, 0, side), rows_of(w, 1, side), rows_of(w, 2, side)
            for p in range(2):
                total = grads[w][p, mine, :].astype(F32) + grads[w][p, one, :].astype(F32) + grads[w][p, two, :].astype(F32)
                diag[w][side, p] = total.astype(BF16)
        pl.when(outer)(lambda: outer_copy(w).start())
        pl.when(near)(lambda: near_copy(w).start())

    def load_outer(w):
        @pl.when(inner)
        def _():
            outer_copy(w).wait_recv()
            for side in range(2):
                col_local(w, side).start()

    def add_outer(w):
        @pl.when(inner)
        def _():
            for side in range(2):
                col_local(w, side).wait()
            for p in range(2):
                for side in range(2):
                    came = grads[w][p, rows_of(w, 3, side), :].astype(F32)
                    diag[w][side, p] = (diag[w][side, p].astype(F32) + came).astype(BF16)
                inner_copy(w, p).start()

    def last_copies(w, k):
        e = grads[w].shape[1] // 8
        if w < PIECES:
            cut = ((0, TILE, s_gate, w * TILE), (TILE, TILE, s_up, w * TILE))
        elif w == QKV_:
            cut = ((0, 256, s_q, 0), (256, 128, s_k, 0), (384, 128, s_v, 0))
        else:
            n = grads[w].shape[2]
            cut = ((0, n, s_o, 0),) if w == O_ else ((0, n, s_down, (w - DA_) * n),)
        return [(last.at[turn[w] % 2, k, pl.ds(0, e), pl.ds(at, n)], ref.at[:, pl.ds(to, n)]) for at, n, ref, to in cut]

    def last_remote(w):
        return [remote(src, dst, ls.at[w, i], lr.at[w, i], mate) for i, (src, dst) in enumerate(last_copies(w, 1))]

    def last_local(w):
        return [pltpu.make_async_copy(src, dst, ll.at[w, i]) for i, (src, dst) in enumerate(last_copies(w, 0))]

    def release_last(w):
        @pl.when(near)
        def _():
            for cp in last_remote(w):
                cp.wait_send()
            for cp in last_local(w):
                cp.wait()

    def load_column(w):
        @pl.when(near)
        def _():
            near_copy(w).wait_recv()
            inner_copy(w, 0).wait_recv()
            for side in range(2):
                col_local(w, side).start()

    def add_column(w):
        if turn[w] >= 2:
            release_last(turn.index(turn[w] - 2))

        @pl.when(near)
        def _():
            e, n = grads[w].shape[1] // 8, grads[w].shape[2]
            for hc in range(2):
                col_local(w, hc).wait()
                came = rows_of(w, 3, hc)
                total = diag[w][hc, par].astype(F32) + grads[w][0, came, :].astype(F32) + grads[w][1, came, :].astype(F32)

                @pl.when(c == hc)
                def _():
                    last[turn[w] % 2, 0, :e, :n] = total

                @pl.when(c != hc)
                def _():
                    last[turn[w] % 2, 1, :e, :n] = total

            for cp in last_remote(w) + last_local(w):
                cp.start()

    def finish(w):
        pl.when(near)(lambda: near_copy(w).wait_send())

        @pl.when(jnp.logical_not(near))
        def _():
            for cp in last_remote(w):
                cp.wait_recv()

        pl.when(outer)(lambda: outer_copy(w).wait_send())

        @pl.when(inner)
        def _():
            inner_copy(w, 0).wait_send()
            inner_copy(w, 1).wait_send()

    def trade(n):
        return remote(give.at[n % 2], take.at[n % 2], ms.at[n], mr.at[n], mate)

    def load(n, src, dst):
        return pltpu.make_async_copy(src, dst, ld.at[n])

    for n in range(len(pieces)):
        z_copies(n, True)
        if n == 4:
            fetch_copies(0, x_ref, hx, True)
        if n == 7:
            fetch_copies(1, ct_ref, hc, True)

    def swap_rows(buf, n):
        own = rows_at(own_at, half)
        return remote(buf.at[own], buf.at[own], ms.at[n], mr.at[n], mate)

    def swap_wait(buf, n):
        other = rows_at(other_at, half)
        remote(buf.at[other], buf.at[other], ms.at[n], mr.at[n], mate).wait_recv()

    def phase_one(wqkv, wo, xbuf, cbuf, qk, qs, k2, v2, mask, att, linv):
        saves = []

        def save(n, src, dst):
            cp = pltpu.make_async_copy(src, dst, outs.at[n])
            saves.append(cp)
            cp.start()

        for i in range(seq // BLK):
            for jb in range(i + 1):
                same = cols_ref[i * BLK : (i + 1) * BLK, :1] == rows_ref[1:, jb * BLK : (jb + 1) * BLK]
                if i == jb:
                    ri = lax.broadcasted_iota(jnp.int32, (BLK, BLK), 0)
                    ci = lax.broadcasted_iota(jnp.int32, (BLK, BLK), 1)
                    same = jnp.logical_or(ri == ci, jnp.logical_and(ci < ri, same))
                mask[i * BLK : (i + 1) * BLK, jb * BLK : (jb + 1) * BLK] = jnp.where(same, 1.0, 0.0).astype(F32)
        v2[:, :, 128:] = jnp.ones((v2.shape[0], v2.shape[1], 128), BF16)
        first(WQKV)
        first(WO)
        second(WQKV)
        second(WO)
        for n in tile_pieces(0):
            first(n)
        third(WQKV)
        weight_load(0, wqkv, True)
        for n in tile_pieces(0):
            second(n)
        third(WO)
        weight_load(1, wo, True)

        fetch_arrivals(0, x_ref, hx)
        fetch_load(0, x_ref, hx, xbuf, True)
        fetch_load(0, x_ref, hx, xbuf, False)

        @pl.loop(0, half // step)
        def _(r):
            xs = xbuf[rows_at(r * step, step), :].astype(F32)
            sc = lax.rsqrt(jnp.mean(xs * xs, axis=-1, keepdims=True) + EPS)
            normed_buf[rows_at(own_at + r * step, step), :] = (xs * sc * gain1_ref[...]).astype(BF16)

        swap_rows(normed_buf, 4).start()
        first(tile_pieces(1)[0])
        weight_load(0, wqkv, False)
        swap_wait(normed_buf, 4)
        normed = normed_buf
        save(1, normed, h_normed)

        @pl.loop(0, seq // BLK)
        def _(r):
            rows = rows_at(r * BLK, BLK)
            cos, sin = cos_ref[rows, :], sin_ref[rows, :]
            lane = lax.broadcasted_iota(jnp.int32, (BLK, 128), 1)
            left = lane < 64
            for p in range(2):
                proj = mm(normed[rows, :], wqkv[p])
                pq = proj[:, :384]
                qk[p, rows, :] = pq
                sc = lax.rsqrt(head_mean(pq * pq, ones_ref, 384) + EPS)
                n = pq * sc * gainqk_ref[...]
                for s in range(3):
                    v = n[:, s * 128 : (s + 1) * 128]
                    rot = v * cos + lane_swap(v) * sin
                    if s < 2:
                        qr = rot.astype(BF16).astype(F32) * 0.125
                        qs[2 * p + s, 0, rows, :] = jnp.where(left, qr, 0.0).astype(BF16)
                        qs[2 * p + s, 1, rows, :] = jnp.where(left, 0.0, qr).astype(BF16)
                    else:
                        kr = pltpu.roll(rot, 64, 1)
                        k2[2 * p, rows, :] = jnp.where(left, rot, kr).astype(BF16)
                        k2[2 * p + 1, rows, :] = jnp.where(left, kr, rot).astype(BF16)
                v = proj[:, 384:]
                vr = pltpu.roll(v, 64, 1)
                v2[2 * p, rows, :128] = jnp.where(left, v, vr).astype(BF16)
                v2[2 * p + 1, rows, :128] = jnp.where(left, vr, v).astype(BF16)

        save(3, qk, h_qk)
        save(4, qs, h_q)
        save(5, k2, h_k)
        save(6, v2.at[:, :, pl.ds(0, 128)], h_v)
        first(tile_pieces(1)[1])
        first(tile_pieces(1)[2])
        second(tile_pieces(1)[0])
        for i in range(seq // BLK):
            n = (i + 1) * BLK
            rows = pl.ds(i * BLK, BLK)

            @pl.loop(0, k2.shape[0])
            def _(g):
                s = mm_nt(qs[g, :, rows, :].reshape(2 * BLK, 128), k2[g, :n, :])
                e = jnp.exp(s).reshape(2, BLK, n) * mask[rows, :n][None]
                acc = mm(e.astype(BF16).reshape(2 * BLK, n), v2[g, :n, :])
                inv = 1.0 / acc[:, 128:]
                o = acc[:, :128] * inv
                left = lax.broadcasted_iota(jnp.int32, (BLK, 128), 1) < 64
                cols = pl.ds(pl.multiple_of(g * 128, 128), 128)
                att[rows, cols] = jnp.where(left, o[:BLK], o[BLK:]).astype(BF16)
                linv[rows, cols] = jnp.where(left, inv[:BLK], inv[BLK:])

        save(7, att, h_att)
        save(8, linv, h_linv)
        second(tile_pieces(1)[1])
        second(tile_pieces(1)[2])
        weight_load(1, wo, False)

        def out_rows(start):
            return mm(att[rows_at(start, BLK), :], wo[...].reshape(2 * wo.shape[1], wo.shape[2]))

        @pl.loop(0, half // BLK)
        def _(r):
            give[0, rows_at(r * BLK, BLK), :] = out_rows(other_at + r * BLK).astype(BF16)

        saves[0].wait()
        swap_rows(normed_buf, 4).wait_send()
        swap_give = remote(give.at[0], take.at[0], ms.at[5], mr.at[5], mate)
        swap_give.start()

        @pl.loop(0, half // BLK)
        def _(r):
            hgrad[rows_at(r * BLK, BLK), :] = out_rows(own_at + r * BLK) + xbuf[rows_at(r * BLK, BLK), :].astype(F32)

        fetch_arrivals(1, ct_ref, hc)
        fetch_load(1, ct_ref, hc, cbuf, True)
        swap_give.wait_recv()

        @pl.loop(0, half // step)
        def _(r):
            h = hgrad[rows_at(r * step, step), :] + take[0, rows_at(r * step, step), :].astype(F32)
            hgrad[rows_at(r * step, step), :] = h
            sc = lax.rsqrt(jnp.mean(h * h, axis=-1, keepdims=True) + EPS)
            n2[rows_at(own_at + r * step, step), :] = (h * sc * gain2_ref[...]).astype(BF16)

        swap_rows(n2, 6).start()
        fetch_load(1, ct_ref, hc, cbuf, False)

        @pl.loop(0, half // step)
        def _(r):
            own = rows_at(own_at + r * step, step)
            v = cbuf[rows_at(r * step, step), :].astype(F32) * jnp.where(cols_ref[own, 1:] >= 0, 1.0, 0.0)
            din[own, :] = v.astype(BF16)

        swap_rows(din, 7).start()
        for n in tile_pieces(0):
            third(n)
        swap_wait(n2, 6)
        swap_wait(din, 7)
        swap_rows(n2, 6).wait_send()
        swap_rows(din, 7).wait_send()
        swap_give.wait_send()
        for cp in saves[1:]:
            cp.wait()

    V = pltpu.VMEM
    gain_out[...] = jnp.zeros(gain_out.shape, F32)
    pl.run_scoped(
        phase_one, V(gqkv.shape, BF16), V(go.shape, BF16), V((half, width), BF16), V((half, width), BF16), V(h_qk.shape, F32),
        V(h_q.shape, BF16), V(h_k.shape, BF16), V((4, seq, 256), BF16), V((seq, seq), F32), V(h_att.shape, BF16),
        V(h_linv.shape, F32),
    )

    def ffn(wg, wu, wd, acc_o, acc_n, act, gu_rows):
        def tile_loads(t, go):
            cols = pl.ds(t * TILE, TILE)
            for p in range(2):
                here = pl.ds(p * TILE, TILE)

                def run(g, u, d):
                    pairs = ((g.at[:, cols], wg.at[:, here]), (u.at[:, cols], wu.at[:, here]), (d.at[cols], wd.at[here]))
                    for k, (src, dst) in enumerate(pairs):
                        cp = pltpu.make_async_copy(src, dst, wl.at[2 + k, p])
                        cp.start() if go else cp.wait()

                if go:
                    mine = near & (par == p)
                    pl.when(mine)(lambda: run(wg_ref, wu_ref, wd_ref))
                    pl.when(jnp.logical_not(mine))(lambda: run(gg.at[p], gu.at[p], gd.at[p]))
                else:
                    run(gg.at[p], gu.at[p], gd.at[p])

        ones_, twos = tile_pieces(1), tile_pieces(2)
        tile_loads(0, True)
        for t in range(PIECES):
            tile_loads(t, False)

            @pl.loop(0, seq // BLK)
            def _(r):
                rows = rows_at(r * BLK, BLK)
                a = n2[rows, :]
                g = mm(a, wg[...])
                u = mm(a, wu[...])
                ag = mm_nt(din[rows, :], wd[...])
                sig = jax.nn.sigmoid(g)
                gs_ = g * sig
                av = (gs_ * u).astype(BF16)
                act[t, rows, :] = av
                gv = (ag * u * (sig + gs_ * (1.0 - sig))).astype(BF16)
                uv = (ag * gs_).astype(BF16)
                for p in range(2):
                    gu_rows[rows, 2 * p * TILE : (2 * p + 1) * TILE] = gv[:, p * TILE : (p + 1) * TILE]
                    gu_rows[rows, (2 * p + 1) * TILE : (2 * p + 2) * TILE] = uv[:, p * TILE : (p + 1) * TILE]
                dn = mm_nt(gv, wg[...]) + mm_nt(uv, wu[...])
                do = mm(av, wd[...])
                if t == 0:
                    acc_n[rows, :] = dn
                    acc_o[rows, :] = do
                else:
                    acc_n[rows, :] += dn
                    acc_o[rows, :] += do

            if t == 0:
                for n in twos:
                    first(n)
                second(twos[0])
            if t == 1:
                for n in twos:
                    third(n)
                tile_loads(2, True)

            @pl.loop(0, width // BLK)
            def _(r):
                cols = pl.ds(pl.multiple_of(r * BLK, BLK), BLK)
                o = mm_tn(n2[:, cols], gu_rows[...]).astype(BF16)
                for p in range(2):
                    grads[t][p, cols, :] = o[:, 2 * p * TILE : 2 * (p + 1) * TILE]

            if t == 1:
                add_diag(0)
            begin(t)
            if t == 0:
                second(twos[1])
                second(twos[2])
                for n in ones_:
                    third(n)
                tile_loads(1, True)

        @pl.loop(0, half // BLK)
        def _(r):
            rows = rows_at(r * BLK, BLK)
            give[0, rows, :] = acc_n[rows_at(other_at + r * BLK, BLK), :].astype(BF16)
            give[1, rows, :] = acc_o[rows_at(other_at + r * BLK, BLK), :].astype(BF16)

        trade(0).start()
        trade(1).start()
        load_plane(0)
        for w in (DA_, DB_):
            n = width // 2
            for p in range(2):
                @pl.loop(0, n // BLK)
                def _(r):
                    cols = pl.ds(pl.multiple_of(r * BLK, BLK), BLK)
                    come = pl.ds(pl.multiple_of((w - DA_) * n + r * BLK, BLK), BLK)
                    for k in range(PIECES):
                        rows = pl.ds(k * TILE, TILE)
                        grads[w][p, rows, cols] = mm_tn(act[k, :, p * TILE : (p + 1) * TILE], din[:, come]).astype(BF16)

            if w == DA_:
                add_diag(1)
            begin(w)
            if w == DA_:
                add_plane(0)

        trade(0).wait_recv()
        trade(1).wait_recv()

        @pl.loop(0, half // step)
        def _(r):
            rows = rows_at(r * step, step)
            own = rows_at(own_at + r * step, step)
            h = hgrad[rows, :]
            obuf[rows, :] = (h + acc_o[own, :] + take[1, rows, :].astype(F32)).astype(BF16)
            ng = acc_n[own, :] + take[0, rows, :].astype(F32)
            sc = lax.rsqrt(jnp.mean(h * h, axis=-1, keepdims=True) + EPS)
            unit = h * sc
            acc_gain(8, ng * unit)
            e = ng * gain2_ref[...]
            hg = din[own, :].astype(F32) + sc * (e - unit * jnp.mean(e * unit, axis=-1, keepdims=True))
            hgrad[rows, :] = hg
            attn_in[own, :] = hg.astype(BF16)

        token_copies(0, obuf, oo, True)

    def acc_gain(at, v):
        s = jnp.sum(v, axis=0, keepdims=True)
        for k in range(width // 128):
            gain_out[at + k : at + k + 1, :] += s[:, k * 128 : (k + 1) * 128]

    pl.run_scoped(
        ffn,
        pltpu.VMEM((width, 2 * TILE), BF16), pltpu.VMEM((width, 2 * TILE), BF16), pltpu.VMEM((2 * TILE, width), BF16),
        pltpu.VMEM((seq, width), F32), pltpu.VMEM((seq, width), F32), pltpu.VMEM((PIECES, seq, 2 * TILE), BF16),
        pltpu.VMEM((seq, 4 * TILE), BF16),
    )

    def attn_swap():
        own = rows_at(own_at, half)
        return remote(attn_in.at[own], attn_in.at[own], ms.at[3], mr.at[3], mate)

    attn_swap().start()

    def attention(dos, dq, dk, dv, drow):
        def front(wo, att, linv):
            loads = [load(4, h_att, att), load(5, h_linv, linv)]
            for cp in loads:
                cp.start()
            weight_load(1, wo, True)
            for cp in loads:
                cp.wait()
            weight_load(1, wo, False)
            other = rows_at(other_at, half)
            remote(attn_in.at[other], attn_in.at[other], ms.at[3], mr.at[3], mate).wait_recv()

            @pl.loop(0, seq // BLK)
            def _(r):
                rows = rows_at(r * BLK, BLK)
                left = lax.broadcasted_iota(jnp.int32, (BLK, 128), 1) < 64
                for p in range(2):
                    ag = mm_nt(attn_in[rows, :], wo[p]).astype(BF16).astype(F32)
                    for s in range(2):
                        g = 2 * p + s
                        cols = slice(g * 128, (g + 1) * 128)
                        d = ag[:, s * 128 : (s + 1) * 128] * linv[rows, cols]
                        d0, d1 = jnp.where(left, d, 0.0).astype(BF16), jnp.where(left, 0.0, d).astype(BF16)
                        dos[g, 0, rows, :] = d0
                        dos[g, 1, rows, :] = d1
                        o = att[rows, cols].astype(F32)
                        one = jnp.ones((8, 128), BF16)
                        for k, dd in enumerate((d0, d1)):
                            prod = dd.astype(F32) * o
                            high = prod.astype(BF16)
                            low = (prod - high.astype(F32)).astype(BF16)
                            drow[g, k, :, rows] = mm_nt(one, high) + mm_nt(one, low)

            @pl.loop(0, width // BLK)
            def _(r):
                cols = pl.ds(pl.multiple_of(r * BLK, BLK), BLK)
                for p in range(2):
                    grads[O_][p, :, cols] = mm_tn(att[:, p * 256 : (p + 1) * 256], attn_in[:, cols]).astype(BF16)

            add_diag(2)
            begin(O_)
            load_plane(1)
            load_outer(0)

        pl.run_scoped(
            front, pltpu.VMEM(go.shape, BF16), pltpu.VMEM(h_att.shape, BF16), pltpu.VMEM(h_linv.shape, F32),
        )
        def rest(q, k, v, mt, qk, rows_, wqkv):
            normed = din
            trade(1).wait_send()
            x = give.at[1]
            loads = [load(6, h_q, q), load(7, h_k, k), load(8, h_v, v)]
            later = [load(9, h_qk, qk), load(11, h_normed, normed)]
            for cp in loads + later:
                cp.start()
            weight_load(0, wqkv, True)
            fetch_load(0, x_ref, hx, x, True)
            for cp in loads:
                cp.wait()
            dq[...] = jnp.zeros(dq.shape, F32)
            todo = {
                0: [lambda: add_plane(1), lambda: add_outer(0)],
                1: [lambda: add_diag(DA_)],
                2: [lambda: load_plane(2), lambda: load_column(0), lambda: load_outer(1)],
                3: [lambda: add_plane(2), lambda: add_column(0), lambda: add_outer(1), lambda: add_diag(DB_)],
            }
            for jb in range(seq // BLK):
                at = jb * BLK
                ni = seq - at
                keys = pl.ds(at, BLK)
                cols = pl.ds(at, ni)
                ki = lax.broadcasted_iota(jnp.int32, (BLK, ni), 0)
                qi = lax.broadcasted_iota(jnp.int32, (BLK, ni), 1)
                same = jnp.logical_and(ki < qi, cols_ref[keys, 1:] == rows_ref[:1, cols])
                mt[:, :ni] = jnp.where(jnp.logical_or(ki == qi, same), 1.0, 0.0).astype(F32)

                @pl.loop(0, 4)
                def _(g):
                    kb = k[g, keys, :]
                    qb = q[g, :, cols, :].reshape(2 * ni, 128)
                    db = dos[g, :, cols, :].reshape(2 * ni, 128)
                    m = mt[:, :ni]
                    e = jnp.exp(mm_nt(kb, qb)) * jnp.concatenate([m, m], axis=1)
                    dv[g, keys, :] = mm(e.astype(BF16), db)
                    dp = mm_nt(v[g, keys, :], db)
                    dr = jnp.concatenate([drow[g, 0, :1, cols], drow[g, 1, :1, cols]], axis=1)
                    ds = (e * (dp - dr)).astype(BF16)
                    dk[g, keys, :] = mm(ds, qb)
                    dqs = mm_tn(ds, kb)
                    left = lax.broadcasted_iota(jnp.int32, (ni, 128), 1) < 64
                    lanes = pl.ds(pl.multiple_of(g * 128, 128), 128)
                    dq[cols, lanes] += jnp.where(left, dqs[:ni], dqs[ni:])

                for f in todo[jb]:
                    f()
            for cp in later:
                cp.wait()
            weight_load(0, wqkv, False)
            fetch_load(0, x_ref, hx, x, False)

            @pl.loop(0, seq // BLK)
            def _(r):
                rows = rows_at(r * BLK, BLK)
                cos, sin = cos_ref[rows, :], sin_ref[rows, :]
                left = lax.broadcasted_iota(jnp.int32, (BLK, 128), 1) < 64

                def fold(ref, p):
                    a, b = ref[2 * p, rows, :], ref[2 * p + 1, rows, :]
                    return jnp.where(left, a + pltpu.roll(a, 64, 1), b + pltpu.roll(b, 64, 1))

                for p in range(2):
                    raw = qk[p, rows, :]
                    sc = lax.rsqrt(head_mean(raw * raw, ones_ref, 384) + EPS)
                    unit = raw * sc
                    parts = []
                    for s in range(3):
                        if s < 2:
                            v_ = dq[rows, (2 * p + s) * 128 : (2 * p + s + 1) * 128] * 0.125
                        else:
                            v_ = fold(dk, p)
                        v_ = v_.astype(BF16).astype(F32)
                        parts.append(v_ * cos - lane_swap(v_) * sin)
                    ng = jnp.concatenate(parts, axis=1)
                    gsum = jnp.sum(ng * unit, axis=0, keepdims=True)
                    qsum = gsum[:, :128] + gsum[:, 128:256]
                    ksum = gsum[:, 256:]
                    gain_out[16:17, :] += qsum
                    gain_out[17:18, :] += ksum
                    e = ng * gainqk_ref[...]
                    back = sc * (e - unit * head_mean(e * unit, ones_ref, 384))
                    rows_[p, rows, :384] = back.astype(BF16)
                    rows_[p, rows, 384:] = fold(dv, p).astype(BF16)

            def back_rows(start):
                at = rows_at(start, BLK)
                return mm_nt(rows_[0, at, :], wqkv[0]) + mm_nt(rows_[1, at, :], wqkv[1])

            trade(0).wait_send()

            @pl.loop(0, half // BLK)
            def _(r):
                give[0, rows_at(r * BLK, BLK), :] = back_rows(other_at + r * BLK).astype(BF16)

            trade(2).start()
            load_plane(DA_)
            add_diag(O_)
            for p in range(2):
                @pl.loop(0, width // BLK)
                def _(r):
                    cols = pl.ds(pl.multiple_of(r * BLK, BLK), BLK)
                    grads[QKV_][p, cols, :] = mm_tn(normed[:, cols], rows_[p]).astype(BF16)

            begin(QKV_)
            add_plane(DA_)
            load_column(1)
            load_outer(2)
            trade(2).wait_recv()
            token_copies(0, obuf, oo, False)

            @pl.loop(0, half // BLK)
            def _(r):
                rows = rows_at(r * BLK, BLK)
                ng = back_rows(own_at + r * BLK) + take[0, rows, :].astype(F32)
                xs = x[rows, :].astype(F32)
                sc = lax.rsqrt(jnp.mean(xs * xs, axis=-1, keepdims=True) + EPS)
                unit = xs * sc
                acc_gain(0, ng * unit)
                e = ng * gain1_ref[...]
                ig = hgrad[rows, :] + sc * (e - unit * jnp.mean(e * unit, axis=-1, keepdims=True))
                obuf[rows, :] = ig.astype(BF16)

        pl.run_scoped(
            rest, V(h_q.shape, BF16), V(h_k.shape, BF16), V(h_v.shape, BF16), V((BLK, seq), F32), V(h_qk.shape, F32),
            V((2, seq, 512), BF16), V(gqkv.shape, BF16),
        )

    pl.run_scoped(
        attention, pltpu.VMEM(h_q.shape, BF16), pltpu.VMEM((seq, 512), F32), pltpu.VMEM((4, seq, 128), F32),
        pltpu.VMEM((4, seq, 128), F32), pltpu.VMEM((4, 2, 8, seq), F32),
    )
    def gain_copy(i):
        to = (place.column(c, 2 * place.half + 1 - par), place.column(c, 2 - 2 * place.half + par), place.plane(1), place.plane(2),
              mate)[i]
        return remote(gain_out, gain_in.at[i], gs.at[i], gr.at[i], to)

    def gain_step(i):
        gain_copy(i).wait()
        gain_out[...] += gain_in[i]
        if i < 4:
            gain_copy(i + 1).start()

    gain_copy(0).start()
    token_copies(1, obuf, io, True)
    add_column(1)
    add_outer(2)
    load_plane(DB_)
    gain_step(0)
    load_outer(DA_)
    load_column(2)
    add_plane(DB_)
    load_plane(O_)
    gain_step(1)
    add_outer(DA_)
    add_column(2)
    add_diag(QKV_)
    add_plane(O_)
    gain_step(2)
    load_outer(DB_)
    load_column(DA_)
    gain_step(3)
    add_outer(DB_)
    add_column(DA_)
    load_outer(O_)
    load_plane(QKV_)
    gain_step(4)
    add_plane(QKV_)
    add_outer(O_)
    load_column(DB_)
    load_outer(QKV_)
    add_column(DB_)
    load_column(O_)
    add_outer(QKV_)
    add_column(O_)
    load_column(QKV_)
    add_column(QKV_)
    release_last(O_)
    release_last(QKV_)
    for w in range(nw):
        finish(w)
    for n in range(len(pieces)):
        sent(n)
    fetch_copies(0, x_ref, hx, False)
    fetch_copies(1, ct_ref, hc, False)
    trade(2).wait_send()
    attn_swap().wait_send()
    token_copies(1, obuf, io, False)
    token_arrivals(0, obuf, oo)
    token_arrivals(1, obuf, io)


def layer(x, ct, shards, vectors):
    anywhere = pl.BlockSpec(memory_space=pl.ANY)
    vmem = pl.BlockSpec(memory_space=pltpu.VMEM)
    dma = pltpu.SemaphoreType.DMA
    SDS, V = jax.ShapeDtypeStruct, pltpu.VMEM
    seg, width = x.shape[1], x.shape[2]
    half, seq = 2 * seg, 4 * seg
    wqkv, wo, wg, wu, wd = shards
    sizes = [(width, 2 * TILE)] * 3 + [(wd.shape[0], width // 2)] * 2 + [(wo.shape[0], width), (width, wqkv.shape[1])]
    nw, pieces = 7, 2 + 3 * PIECES
    gains = (24, 128)
    results = [(width // 8, 256), (width // 8, 128), (width // 8, 128), (wo.shape[0] // 8, width)]
    results += [(width // 8, wg.shape[1])] * 2 + [(wd.shape[0] // 8, width)]
    held = [((half, width), BF16), ((half, width), BF16), ((seq, width), BF16), ((2, seq, 384), F32), ((4, 2, seq, 128), BF16),
            ((4, seq, 128), BF16), ((4, seq, 128), BF16), ((seq, 512), BF16), ((seq, 512), F32)]
    out_shape = (
        [SDS((2, seg, width), BF16)] * 2
        + [SDS(gains, F32)]
        + [SDS(r, F32) for r in results]
        + [SDS((2,) + s.shape, BF16) for s in shards]
        + [SDS(*h) for h in held]
        + [SDS((2, 2, 2, r // 8, n), BF16) for r, n in sizes]
        + [SDS((2, 2, r // 8, n), BF16) for r, n in sizes]
    )
    e_max, n_max = max(r // 8 for r, _ in sizes), max(n for _, n in sizes)
    out = pl.pallas_call(
        layer_kernel,
        out_shape=out_shape,
        in_specs=[anywhere] * 7 + [vmem] * len(vectors),
        out_specs=[anywhere] * 2 + [vmem] + [anywhere] * (len(out_shape) - 3),
        scratch_shapes=[V((2, r, n), BF16) for r, n in sizes]
        + [V((2, 2, r // 8, n), BF16) for r, n in sizes]
        + [
            V((2, 2, e_max, n_max), F32), V((2, half, width), BF16), V((2, half, width), BF16), V((half, width), BF16),
            V((half, width), F32), V((5,) + gains, F32), V((seq, width), BF16), V((seq, width), BF16),
        ]
        + [
            dma((2, 2)), dma((2, 2)), dma((2, 2)), dma((2, 2)), dma((2, 2)), dma((pieces, 2)), dma((pieces, 2)),
            dma((pieces, 2, 4)), dma((pieces, 2, 4)), dma((nw, 6)), dma((nw, 6)), dma((nw, 2)), dma((nw, 2)), dma((nw, 3)),
            dma((nw, 3)), dma((nw, 3)), dma((5,)), dma((5,)), dma((8,)), dma((8,)), dma((13,)), dma((5, 2)), dma((nw, 2, 2)),
            dma((nw, 2)), dma((9,)),
        ],
        compiler_params=pltpu.CompilerParams(collective_id=0, has_side_effects=True, vmem_limit_bytes=60 * 1024 * 1024),
        name="layer",
    )(x, ct, *shards, *vectors)
    return out[0], out[1], out[2], out[3:10]


def rope_tables(length, width):
    k = np.arange(width // 2)
    angles = np.arange(length)[:, None] * (THETA ** (-2.0 * k / width))[None]
    cos, sin = np.cos(angles), np.sin(angles)
    return (
        jnp.asarray(np.concatenate([cos] * 4, axis=1), F32),
        jnp.asarray(np.concatenate([-sin, sin] * 2, axis=1), F32),
    )


def per_device(n_dp, inputs, query_weight, key_weight, value_weight, out_weight, gate_weight, up_weight, down_weight,
               attn_gain, ffn_gain, query_gain, key_gain, cotangent, segment_ids, padding, row_count):
    slots, _, width = inputs.shape
    seq_len = segment_ids.shape[1]
    head_dim = query_gain.shape[0]
    nq, nk = query_weight.shape[1], key_weight.shape[1]
    z = lax.axis_index("tensor")
    c = lax.axis_index("dp") % 2
    groups = n_dp // 8

    alive_all = padding * (jnp.arange(slots)[:, None] < row_count[0]).astype(jnp.int32)
    code = (segment_ids + ALIVE * alive_all)[z % 2]
    code = jnp.where(c == z // 2, code, lax.ppermute(code, "dp", [(i, i ^ 1) for i in range(n_dp)]))
    segment, alive_row = code % ALIVE, code // ALIVE
    key_code = jnp.where(alive_row > 0, segment, -1)
    codes = jnp.stack([segment, key_code])

    qkv_shard = jnp.concatenate([query_weight, key_weight, value_weight], axis=1)
    cos, sin = rope_tables(seq_len, head_dim)
    gain_qk = jnp.concatenate([query_gain] * (nq // head_dim) + [key_gain] * (nk // head_dim))[None]
    lanes = np.arange(nq + nk) // head_dim
    ones = jnp.asarray(np.where(lanes[:, None] == lanes[None], 1.0 / head_dim, 0.0), BF16)
    gain1, gain2 = attn_gain[None], ffn_gain[None]
    outs, in_grad, gains, sums = layer(
        inputs, cotangent, (qkv_shard, out_weight, gate_weight, up_weight, down_weight),
        (codes.T, codes, gain1, gain2, gain_qk, cos, sin,
         ones),
    )
    if groups > 1:
        same = [[g * 8 + k for g in range(groups)] for k in range(8)]
        sums = [lax.psum_scatter(s, "dp", scatter_dimension=0, axis_index_groups=same, tiled=True) for s in sums]
        gains = lax.psum(gains, "dp", axis_index_groups=same)
    pair = gains[16:18, :head_dim] + gains[16:18, head_dim:]
    return (
        outs,
        in_grad.astype(F32),
        *sums,
        gains[:8].reshape(-1),
        gains[8:16].reshape(-1),
        pair[0],
        pair[1],
    )


def solution(mesh):
    return jax.shard_map(
        functools.partial(per_device, mesh.shape["dp"]),
        mesh=mesh,
        in_specs=(
            P("dp", "tensor", None),
            P(None, "tensor"),
            P(None, "tensor"),
            P(None, "tensor"),
            P("tensor", None),
            P(None, "tensor"),
            P(None, "tensor"),
            P("tensor", None),
            P(),
            P(),
            P(),
            P(),
            P("dp", "tensor", None),
            P("dp", None),
            P("dp", None),
            P("dp"),
        ),
        out_specs=(
            P("dp", "tensor", None),
            P("dp", "tensor", None),
            P("dp", "tensor"),
            P("dp", "tensor"),
            P("dp", "tensor"),
            P(("tensor", "dp"), None),
            P("dp", "tensor"),
            P("dp", "tensor"),
            P(("tensor", "dp"), None),
            P(),
            P(),
            P(),
            P(),
        ),
        check_vma=False,
    )
```

```python
import functools

import jax
import jax.numpy as jnp
import numpy as np
from jax import lax
from jax.experimental import pallas as pl
from jax.experimental.pallas import tpu as pltpu
from jax.sharding import PartitionSpec as P

EPS = 1e-05
THETA = 1000000.0
ALIVE = 4096
MESH = pl.DeviceIdType.MESH
BF16 = jnp.bfloat16
F32 = jnp.float32


class Place:
    def __init__(self):
        self.dp = lax.axis_index("dp")
        self.z = lax.axis_index("tensor")
        self.c = lax.rem(self.dp, 2)
        self.j = lax.rem(self.dp // 2, 4)
        self.half = self.z // 2
        self.par = lax.rem(self.z, 2)
        self.near = self.half == self.c

    def plane(self, k):
        j = self.j
        bit = lax.rem(j // k, 2)
        return (self.dp + (1 - 2 * bit) * 2 * k, self.z)

    def column(self, c, z):
        return (self.dp - self.c + c, z)

    def quarter(self, k):
        j = self.j
        low, high = lax.rem(j, 2), j // 2
        if k & 1:
            low = 1 - low
        if k & 2:
            high = 1 - high
        return 2 * high + low


def greet(place):
    barrier = pltpu.get_barrier_semaphore()
    for k in (1, 2):
        pl.semaphore_signal(barrier, inc=1, device_id=place.plane(k), device_id_type=MESH)
    for dc in range(2):
        for dz in range(4):
            if dc or dz:
                c = lax.rem(place.c + dc, 2)
                z = lax.rem(place.z + dz, 4)
                pl.semaphore_signal(barrier, inc=1, device_id=place.column(c, z), device_id_type=MESH)
    pl.semaphore_wait(barrier, 9)


def remote(src, dst, send, recv, device):
    return pltpu.make_async_remote_copy(
        src_ref=src, dst_ref=dst, send_sem=send, recv_sem=recv, device_id=device, device_id_type=MESH
    )


def lane_swap(v):
    lane = lax.broadcasted_iota(jnp.int32, v.shape, 1)
    return jnp.where(lane % 64 < 32, pltpu.roll(v, 96, 1), pltpu.roll(v, 32, 1))


def head_mean(v, ones_ref, n):
    high = v.astype(BF16)
    low = (v - high.astype(F32)).astype(BF16)
    ones = ones_ref[:n, :n]
    return jnp.dot(high, ones, preferred_element_type=F32) + jnp.dot(low, ones, preferred_element_type=F32)


def mm(a, b):
    return jnp.dot(a, b, preferred_element_type=F32)


def mm_nt(a, b):
    return lax.dot_general(a, b, (((1,), (1,)), ((), ())), preferred_element_type=F32)


def mm_tn(a, b):
    return lax.dot_general(a, b, (((0,), (0,)), ((), ())), preferred_element_type=F32)


BLK = 256


def rows_at(start, size):
    return pl.ds(pl.multiple_of(start, size), size)


TILE = 384
PIECES = 3


def layer_kernel(x_ref, ct_ref, wqkv_ref, wo_ref, wg_ref, wu_ref, wd_ref, cols_ref, rows_ref,
                 gain1_ref, gain2_ref, gainqk_ref, cos_ref, sin_ref, ones_ref,
                 oo, io, gain_out, s_q, s_k, s_v, s_o, s_gate, s_up, s_down,
                 gqkv, go, gg, gu, gd, hx, hc, h_normed, h_qk, h_q, h_k, h_v, h_att, h_linv,
                 p_gu0, p_gu1, p_gu2, p_d0, p_d1, p_o, p_qkv, c_gu0, c_gu1, c_gu2, c_d0, c_d1, c_o, c_qkv,
                 g_a, g_b, g_c, g_d0, g_d1, g_o, g_qkv, d_gu0, d_gu1, d_gu2, d_d0, d_d1, d_o, d_qkv, last, give, take, obuf, hgrad,
                 gain_in, attn_in, din,
                 in_s, in_r, tok_s, tok_r, tok_l, zs, zr, fs, fr, ps, pr, cs, cr, ls, lr, ll, gs, gr, ms, mr, ld, wl, pls, cls,
                 outs):
    shards = (wqkv_ref, wo_ref, wg_ref, wu_ref, wd_ref)
    full = (gqkv, go, gg, gu, gd)
    grads = (g_a, g_b, g_c, g_d0, g_d1, g_o, g_qkv)
    diag = (d_gu0, d_gu1, d_gu2, d_d0, d_d1, d_o, d_qkv)
    plane_in = (p_gu0, p_gu1, p_gu2, p_d0, p_d1, p_o, p_qkv)
    col_in = (c_gu0, c_gu1, c_gu2, c_d0, c_d1, c_o, c_qkv)
    nw = 7
    DA_, DB_, O_, QKV_ = 3, 4, 5, 6
    turn = (0, 1, 2, 3, 4, 5, 6)
    place = Place()
    z, c, par, near, j = place.z, place.c, place.par, place.near, place.j
    inner = jnp.where(c == 0, z == 2, z == 1)
    outer = jnp.where(c == 0, z == 3, z == 0)
    half = obuf.shape[0]
    seq = 2 * half
    seg = half // 2
    width = obuf.shape[1]
    mate = place.column(1 - c, z)
    own_at = c * half
    other_at = (1 - c) * half
    step = 128
    n2 = attn_in
    normed_buf = din
    greet(place)

    def fetch_copies(a, src, dst, go):
        for b in range(2):
            slot = par if b == 0 else 1 - par
            target = place.column(place.half, 2 * c + slot)

            def far_copy():
                cp = remote(src.at[slot], dst.at[rows_at(par * seg, seg)], in_s.at[a, b], in_r.at[a, par], target)
                cp.start() if go else cp.wait_send()

            if b == 0:
                pl.when(jnp.logical_not(near))(far_copy)
            else:
                far_copy()

    def fetch_arrivals(a, src, dst):
        for h in range(2):
            @pl.when(jnp.logical_not(near & (par == h)))
            def _():
                remote(src.at[0], dst.at[pl.ds(h * seg, seg)], in_s.at[a, 0], in_r.at[a, h], place.plane(1)).wait_recv()

    def fetch_load(a, src, landed, dst, go):
        for h in range(2):
            here = dst.at[pl.ds(h * seg, seg)]
            came = pltpu.make_async_copy(landed.at[pl.ds(h * seg, seg)], here, tok_l.at[a, h])
            if go:
                mine = near & (par == h)
                pl.when(mine)(lambda: pltpu.make_async_copy(src.at[h], here, tok_l.at[a, h]).start())
                pl.when(jnp.logical_not(mine))(came.start)
            else:
                came.wait()

    pieces = [(0, 256, 0, None), (1, 64, 0, None)]
    for t in range(PIECES):
        pieces += [(2, 256, 0, t), (3, 256, 0, t), (4, TILE // 4, t * TILE, None)]
    WQKV, WO = 0, 1

    def tile_pieces(t):
        return (2 + 3 * t, 3 + 3 * t, 4 + 3 * t)

    def piece_at(ref, n, k, side=None, p=None):
        w, q, at, t = pieces[n]
        start, size = pl.multiple_of(at + place.quarter(k) * q, 16), q
        if side is not None:
            size = q // 2
            start = pl.multiple_of(start + side * size, 16)
        index = (pl.ds(start, size),) + (() if t is None else (pl.ds(t * TILE, TILE),))
        return ref.at[index if p is None else (p,) + index]

    def part(n, p, k, side=None):
        return piece_at(full[pieces[n][0]], n, k, side, p)

    def z_copies(n, go):
        @pl.when(near)
        def _():
            for i, to in enumerate((2 - c, 2 * place.half + 1 - par)):
                cp = remote(piece_at(shards[pieces[n][0]], n, 0), part(n, par, 0), zs.at[n, i], zr.at[n, par], place.column(c, to))
                cp.start() if go else cp.wait_send()

    def z_onward(n, p):
        return remote(part(n, p, 0), part(n, p, 0), zs.at[n, p], zr.at[n, p], place.column(c, 3 - 3 * c))

    def missing(p, body):
        pl.when(jnp.logical_or(jnp.logical_not(near), par != p))(body)

    def step_copy(n, p, i):
        k, side, to = ((0, None, 1), (0, None, 2), (1, 0, 2), (2, 1, 1))[i]
        return remote(part(n, p, k, side), part(n, p, k, side), fs.at[n, p, i], fr.at[n, p, i], place.plane(to))

    def first(n):
        for p in range(2):
            @functools.partial(missing, p)
            def _():
                z_onward(n, p).wait_recv()
                pl.when(inner)(lambda: z_onward(n, p).start())
                step_copy(n, p, 0).start()
                step_copy(n, p, 1).start()

    def second(n):
        for p in range(2):
            @functools.partial(missing, p)
            def _():
                step_copy(n, p, 0).wait_recv()
                step_copy(n, p, 2).start()
                step_copy(n, p, 1).wait_recv()
                step_copy(n, p, 3).start()

    def third(n):
        for p in range(2):
            @functools.partial(missing, p)
            def _():
                step_copy(n, p, 2).wait_recv()
                step_copy(n, p, 3).wait_recv()

    def sent(n):
        z_copies(n, False)
        for p in range(2):
            @functools.partial(missing, p)
            def _():
                pl.when(inner)(lambda: z_onward(n, p).wait_send())
                for i in range(4):
                    step_copy(n, p, i).wait_send()

    def weight_load(w, dst, go):
        for p in range(2):
            came = pltpu.make_async_copy(full[w].at[p], dst.at[p], wl.at[w, p])
            if go:
                mine = near & (par == p)
                pl.when(mine)(lambda: pltpu.make_async_copy(shards[w], dst.at[p], wl.at[w, p]).start())
                pl.when(jnp.logical_not(mine))(came.start)
            else:
                came.wait()

    def token_copies(a, src, dst, go):
        for b in range(2):
            h = par if b == 0 else 1 - par
            piece = src.at[rows_at(h * seg, seg)]
            target = place.column(place.half, 2 * c + h)
            there = dst.at[par]

            def far_copy():
                cp = remote(piece, there, tok_s.at[a, b], tok_r.at[a, par], target)
                cp.start() if go else cp.wait_send()

            if b == 0:
                @pl.when(near)
                def _():
                    cp = pltpu.make_async_copy(piece, there, tok_l.at[a, 0])
                    cp.start() if go else cp.wait()

                pl.when(jnp.logical_not(near))(far_copy)
            else:
                far_copy()

    def token_arrivals(a, src, dst):
        for s in range(2):
            @pl.when(jnp.logical_not(near & (par == s)))
            def _():
                remote(src.at[pl.ds(0, seg)], dst.at[s], tok_s.at[a, 0], tok_r.at[a, s], place.plane(1)).wait_recv()

    def rows_of(w, k, side=None):
        q = grads[w].shape[1] // 4
        start, size = pl.multiple_of(place.quarter(k) * q, q), q
        if side is not None:
            size = q // 2
            start = pl.multiple_of(start + side * size, size)
        return pl.ds(start, size)

    def diag_copy(w, side):
        return remote(grads[w].at[:, rows_of(w, 3, side)], diag[w].at[side], ps.at[w, side], pr.at[w, side], place.plane(1 + side))

    def plane_copy(w, i, side):
        src = grads[w].at[:, rows_of(w, 1 + i, side)] if side == i else diag[w].at[side]
        n = 2 + 2 * i + side
        return remote(src, plane_in[w].at[i, side], ps.at[w, n], pr.at[w, n], place.plane(1 + i))

    def begin(w):
        diag_copy(w, 0).start()
        diag_copy(w, 1).start()
        plane_copy(w, 0, 0).start()
        plane_copy(w, 1, 1).start()

    def add_diag(w):
        for side in (0, 1):
            diag_copy(w, side).wait()
            rows = rows_of(w, 2 - side, side)
            for p in range(2):
                diag[w][side, p] = (grads[w][p, rows, :].astype(F32) + diag[w][side, p].astype(F32)).astype(BF16)
            plane_copy(w, 1 - side, side).start()

    def outer_copy(w):
        return remote(diag[w], col_in[w], cs.at[w, 0], cr.at[w, 0], place.column(c, z - 1 + 2 * c))

    def inner_copy(w, p):
        return remote(diag[w].at[:, p], col_in[w].at[:, 1], cs.at[w, p], cr.at[w, 1], place.column(c, 2 * c + p))

    def near_copy(w):
        to = place.column(c, 2 * place.half + 1 - par)
        return remote(diag[w].at[:, 1 - par], col_in[w].at[:, 0], cs.at[w, 0], cr.at[w, 0], to)

    def plane_local(w, i, side):
        return pltpu.make_async_copy(plane_in[w].at[i, side], grads[w].at[:, rows_of(w, 1 + i, side)], pls.at[w, i, side])

    def col_local(w, side):
        return pltpu.make_async_copy(col_in[w].at[side], grads[w].at[:, rows_of(w, 3, side)], cls.at[w, side])

    def load_plane(w):
        for i in range(2):
            for side in range(2):
                plane_copy(w, i, side).wait()
        for i in range(2):
            for side in range(2):
                plane_local(w, i, side).start()

    def add_plane(w):
        for side in range(2):
            for i in range(2):
                plane_local(w, i, side).wait()
            mine, one, two = rows_of(w, 0, side), rows_of(w, 1, side), rows_of(w, 2, side)
            for p in range(2):
                total = grads[w][p, mine, :].astype(F32) + grads[w][p, one, :].astype(F32) + grads[w][p, two, :].astype(F32)
                diag[w][side, p] = total.astype(BF16)
        pl.when(outer)(lambda: outer_copy(w).start())
        pl.when(near)(lambda: near_copy(w).start())

    def load_outer(w):
        @pl.when(inner)
        def _():
            outer_copy(w).wait_recv()
            for side in range(2):
                col_local(w, side).start()

    def add_outer(w):
        @pl.when(inner)
        def _():
            for side in range(2):
                col_local(w, side).wait()
            for p in range(2):
                for side in range(2):
                    came = grads[w][p, rows_of(w, 3, side), :].astype(F32)
                    diag[w][side, p] = (diag[w][side, p].astype(F32) + came).astype(BF16)
                inner_copy(w, p).start()

    def last_copies(w, k):
        e = grads[w].shape[1] // 8
        if w < PIECES:
            cut = ((0, TILE, s_gate, w * TILE), (TILE, TILE, s_up, w * TILE))
        elif w == QKV_:
            cut = ((0, 256, s_q, 0), (256, 128, s_k, 0), (384, 128, s_v, 0))
        else:
            n = grads[w].shape[2]
            cut = ((0, n, s_o, 0),) if w == O_ else ((0, n, s_down, (w - DA_) * n),)
        return [(last.at[turn[w] % 2, k, pl.ds(0, e), pl.ds(at, n)], ref.at[:, pl.ds(to, n)]) for at, n, ref, to in cut]

    def last_remote(w):
        return [remote(src, dst, ls.at[w, i], lr.at[w, i], mate) for i, (src, dst) in enumerate(last_copies(w, 1))]

    def last_local(w):
        return [pltpu.make_async_copy(src, dst, ll.at[w, i]) for i, (src, dst) in enumerate(last_copies(w, 0))]

    def release_last(w):
        @pl.when(near)
        def _():
            for cp in last_remote(w):
                cp.wait_send()
            for cp in last_local(w):
                cp.wait()

    def load_column(w):
        @pl.when(near)
        def _():
            near_copy(w).wait_recv()
            inner_copy(w, 0).wait_recv()
            for side in range(2):
                col_local(w, side).start()

    def add_column(w):
        if turn[w] >= 2:
            release_last(turn.index(turn[w] - 2))

        @pl.when(near)
        def _():
            e, n = grads[w].shape[1] // 8, grads[w].shape[2]
            for hc in range(2):
                col_local(w, hc).wait()
                came = rows_of(w, 3, hc)
                total = diag[w][hc, par].astype(F32) + grads[w][0, came, :].astype(F32) + grads[w][1, came, :].astype(F32)

                @pl.when(c == hc)
                def _():
                    last[turn[w] % 2, 0, :e, :n] = total

                @pl.when(c != hc)
                def _():
                    last[turn[w] % 2, 1, :e, :n] = total

            for cp in last_remote(w) + last_local(w):
                cp.start()

    def finish(w):
        pl.when(near)(lambda: near_copy(w).wait_send())

        @pl.when(jnp.logical_not(near))
        def _():
            for cp in last_remote(w):
                cp.wait_recv()

        pl.when(outer)(lambda: outer_copy(w).wait_send())

        @pl.when(inner)
        def _():
            inner_copy(w, 0).wait_send()
            inner_copy(w, 1).wait_send()

    def trade(n):
        return remote(give.at[n % 2], take.at[n % 2], ms.at[n], mr.at[n], mate)

    def load(n, src, dst):
        return pltpu.make_async_copy(src, dst, ld.at[n])

    for n in range(len(pieces)):
        z_copies(n, True)
        if n == 3:
            fetch_copies(0, x_ref, hx, True)
        if n == 7:
            fetch_copies(1, ct_ref, hc, True)

    def swap_rows(buf, n):
        own = rows_at(own_at, half)
        return remote(buf.at[own], buf.at[own], ms.at[n], mr.at[n], mate)

    def swap_wait(buf, n):
        other = rows_at(other_at, half)
        remote(buf.at[other], buf.at[other], ms.at[n], mr.at[n], mate).wait_recv()

    def phase_one(wqkv, wo, xbuf, cbuf, qk, qs, k2, v2, mask, att, linv):
        saves = []

        def save(n, src, dst):
            cp = pltpu.make_async_copy(src, dst, outs.at[n])
            saves.append(cp)
            cp.start()

        for i in range(seq // BLK):
            for jb in range(i + 1):
                same = cols_ref[i * BLK : (i + 1) * BLK, :1] == rows_ref[1:, jb * BLK : (jb + 1) * BLK]
                if i == jb:
                    ri = lax.broadcasted_iota(jnp.int32, (BLK, BLK), 0)
                    ci = lax.broadcasted_iota(jnp.int32, (BLK, BLK), 1)
                    same = jnp.logical_or(ri == ci, jnp.logical_and(ci < ri, same))
                mask[i * BLK : (i + 1) * BLK, jb * BLK : (jb + 1) * BLK] = jnp.where(same, 1.0, 0.0).astype(F32)
        v2[:, :, 128:] = jnp.ones((v2.shape[0], v2.shape[1], 128), BF16)
        first(WQKV)
        first(WO)
        second(WQKV)
        second(WO)
        for n in tile_pieces(0):
            first(n)
        third(WQKV)
        weight_load(0, wqkv, True)
        for n in tile_pieces(0):
            second(n)
        third(WO)
        weight_load(1, wo, True)

        fetch_arrivals(0, x_ref, hx)
        fetch_load(0, x_ref, hx, xbuf, True)
        fetch_load(0, x_ref, hx, xbuf, False)

        @pl.loop(0, half // step)
        def _(r):
            xs = xbuf[rows_at(r * step, step), :].astype(F32)
            sc = lax.rsqrt(jnp.mean(xs * xs, axis=-1, keepdims=True) + EPS)
            normed_buf[rows_at(own_at + r * step, step), :] = (xs * sc * gain1_ref[...]).astype(BF16)

        swap_rows(normed_buf, 4).start()
        first(tile_pieces(1)[0])
        weight_load(0, wqkv, False)
        swap_wait(normed_buf, 4)
        normed = normed_buf
        save(1, normed, h_normed)

        @pl.loop(0, seq // BLK)
        def _(r):
            rows = rows_at(r * BLK, BLK)
            cos, sin = cos_ref[rows, :], sin_ref[rows, :]
            lane = lax.broadcasted_iota(jnp.int32, (BLK, 128), 1)
            left = lane < 64
            for p in range(2):
                proj = mm(normed[rows, :], wqkv[p])
                pq = proj[:, :384]
                qk[p, rows, :] = pq
                sc = lax.rsqrt(head_mean(pq * pq, ones_ref, 384) + EPS)
                n = pq * sc * gainqk_ref[...]
                for s in range(3):
                    v = n[:, s * 128 : (s + 1) * 128]
                    rot = v * cos + lane_swap(v) * sin
                    if s < 2:
                        qr = rot.astype(BF16).astype(F32) * 0.125
                        qs[2 * p + s, 0, rows, :] = jnp.where(left, qr, 0.0).astype(BF16)
                        qs[2 * p + s, 1, rows, :] = jnp.where(left, 0.0, qr).astype(BF16)
                    else:
                        kr = pltpu.roll(rot, 64, 1)
                        k2[2 * p, rows, :] = jnp.where(left, rot, kr).astype(BF16)
                        k2[2 * p + 1, rows, :] = jnp.where(left, kr, rot).astype(BF16)
                v = proj[:, 384:]
                vr = pltpu.roll(v, 64, 1)
                v2[2 * p, rows, :128] = jnp.where(left, v, vr).astype(BF16)
                v2[2 * p + 1, rows, :128] = jnp.where(left, vr, v).astype(BF16)

        save(3, qk, h_qk)
        save(4, qs, h_q)
        save(5, k2, h_k)
        save(6, v2.at[:, :, pl.ds(0, 128)], h_v)
        first(tile_pieces(1)[1])
        first(tile_pieces(1)[2])
        second(tile_pieces(1)[0])
        for i in range(seq // BLK):
            n = (i + 1) * BLK
            rows = pl.ds(i * BLK, BLK)

            @pl.loop(0, k2.shape[0])
            def _(g):
                s = mm_nt(qs[g, :, rows, :].reshape(2 * BLK, 128), k2[g, :n, :])
                e = jnp.exp(s).reshape(2, BLK, n) * mask[rows, :n][None]
                acc = mm(e.astype(BF16).reshape(2 * BLK, n), v2[g, :n, :])
                inv = 1.0 / acc[:, 128:]
                o = acc[:, :128] * inv
                left = lax.broadcasted_iota(jnp.int32, (BLK, 128), 1) < 64
                cols = pl.ds(pl.multiple_of(g * 128, 128), 128)
                att[rows, cols] = jnp.where(left, o[:BLK], o[BLK:]).astype(BF16)
                linv[rows, cols] = jnp.where(left, inv[:BLK], inv[BLK:])

        save(7, att, h_att)
        save(8, linv, h_linv)
        second(tile_pieces(1)[1])
        second(tile_pieces(1)[2])
        weight_load(1, wo, False)

        def out_rows(start):
            return mm(att[rows_at(start, BLK), :], wo[...].reshape(2 * wo.shape[1], wo.shape[2]))

        @pl.loop(0, half // BLK)
        def _(r):
            give[0, rows_at(r * BLK, BLK), :] = out_rows(other_at + r * BLK).astype(BF16)

        saves[0].wait()
        swap_rows(normed_buf, 4).wait_send()
        swap_give = remote(give.at[0], take.at[0], ms.at[5], mr.at[5], mate)
        swap_give.start()

        @pl.loop(0, half // BLK)
        def _(r):
            hgrad[rows_at(r * BLK, BLK), :] = out_rows(own_at + r * BLK) + xbuf[rows_at(r * BLK, BLK), :].astype(F32)

        fetch_arrivals(1, ct_ref, hc)
        fetch_load(1, ct_ref, hc, cbuf, True)
        swap_give.wait_recv()

        @pl.loop(0, half // step)
        def _(r):
            h = hgrad[rows_at(r * step, step), :] + take[0, rows_at(r * step, step), :].astype(F32)
            hgrad[rows_at(r * step, step), :] = h
            sc = lax.rsqrt(jnp.mean(h * h, axis=-1, keepdims=True) + EPS)
            n2[rows_at(own_at + r * step, step), :] = (h * sc * gain2_ref[...]).astype(BF16)

        swap_rows(n2, 6).start()
        fetch_load(1, ct_ref, hc, cbuf, False)

        @pl.loop(0, half // step)
        def _(r):
            own = rows_at(own_at + r * step, step)
            v = cbuf[rows_at(r * step, step), :].astype(F32) * jnp.where(cols_ref[own, 1:] >= 0, 1.0, 0.0)
            din[own, :] = v.astype(BF16)

        swap_rows(din, 7).start()
        for n in tile_pieces(0):
            third(n)
        swap_wait(n2, 6)
        swap_wait(din, 7)
        swap_rows(n2, 6).wait_send()
        swap_rows(din, 7).wait_send()
        swap_give.wait_send()
        for cp in saves[1:]:
            cp.wait()

    V = pltpu.VMEM
    gain_out[...] = jnp.zeros(gain_out.shape, F32)
    pl.run_scoped(
        phase_one, V(gqkv.shape, BF16), V(go.shape, BF16), V((half, width), BF16), V((half, width), BF16), V(h_qk.shape, F32),
        V(h_q.shape, BF16), V(h_k.shape, BF16), V((4, seq, 256), BF16), V((seq, seq), F32), V(h_att.shape, BF16),
        V(h_linv.shape, F32),
    )

    def ffn(wg, wu, wd, acc_o, acc_n, act, gu_rows):
        def tile_loads(t, go):
            cols = pl.ds(t * TILE, TILE)
            for p in range(2):
                here = pl.ds(p * TILE, TILE)

                def run(g, u, d):
                    pairs = ((g.at[:, cols], wg.at[:, here]), (u.at[:, cols], wu.at[:, here]), (d.at[cols], wd.at[here]))
                    for k, (src, dst) in enumerate(pairs):
                        cp = pltpu.make_async_copy(src, dst, wl.at[2 + k, p])
                        cp.start() if go else cp.wait()

                if go:
                    mine = near & (par == p)
                    pl.when(mine)(lambda: run(wg_ref, wu_ref, wd_ref))
                    pl.when(jnp.logical_not(mine))(lambda: run(gg.at[p], gu.at[p], gd.at[p]))
                else:
                    run(gg.at[p], gu.at[p], gd.at[p])

        ones_, twos = tile_pieces(1), tile_pieces(2)
        tile_loads(0, True)
        for t in range(PIECES):
            tile_loads(t, False)

            @pl.loop(0, seq // BLK)
            def _(r):
                rows = rows_at(r * BLK, BLK)
                a = n2[rows, :]
                g = mm(a, wg[...])
                u = mm(a, wu[...])
                ag = mm_nt(din[rows, :], wd[...])
                sig = jax.nn.sigmoid(g)
                gs_ = g * sig
                av = (gs_ * u).astype(BF16)
                act[t, rows, :] = av
                gv = (ag * u * (sig + gs_ * (1.0 - sig))).astype(BF16)
                uv = (ag * gs_).astype(BF16)
                for p in range(2):
                    gu_rows[rows, 2 * p * TILE : (2 * p + 1) * TILE] = gv[:, p * TILE : (p + 1) * TILE]
                    gu_rows[rows, (2 * p + 1) * TILE : (2 * p + 2) * TILE] = uv[:, p * TILE : (p + 1) * TILE]
                dn = mm_nt(gv, wg[...]) + mm_nt(uv, wu[...])
                do = mm(av, wd[...])
                if t == 0:
                    acc_n[rows, :] = dn
                    acc_o[rows, :] = do
                else:
                    acc_n[rows, :] += dn
                    acc_o[rows, :] += do

            if t == 0:
                for n in twos:
                    first(n)
                second(twos[0])
            if t == 2:
                load_plane(0)
            if t == 1:
                for n in twos:
                    third(n)
                tile_loads(2, True)

            @pl.loop(0, width // BLK)
            def _(r):
                cols = pl.ds(pl.multiple_of(r * BLK, BLK), BLK)
                o = mm_tn(n2[:, cols], gu_rows[...]).astype(BF16)
                for p in range(2):
                    grads[t][p, cols, :] = o[:, 2 * p * TILE : 2 * (p + 1) * TILE]

            if t == 1:
                add_diag(0)
            begin(t)
            if t == 2:
                add_plane(0)
            if t == 0:
                second(twos[1])
                second(twos[2])
                for n in ones_:
                    third(n)
                tile_loads(1, True)

        @pl.loop(0, half // BLK)
        def _(r):
            rows = rows_at(r * BLK, BLK)
            give[0, rows, :] = acc_n[rows_at(other_at + r * BLK, BLK), :].astype(BF16)
            give[1, rows, :] = acc_o[rows_at(other_at + r * BLK, BLK), :].astype(BF16)

        trade(0).start()
        trade(1).start()
        for w in (DA_, DB_):
            n = width // 2
            for p in range(2):
                @pl.loop(0, n // BLK)
                def _(r):
                    cols = pl.ds(pl.multiple_of(r * BLK, BLK), BLK)
                    come = pl.ds(pl.multiple_of((w - DA_) * n + r * BLK, BLK), BLK)
                    for k in range(PIECES):
                        rows = pl.ds(k * TILE, TILE)
                        grads[w][p, rows, cols] = mm_tn(act[k, :, p * TILE : (p + 1) * TILE], din[:, come]).astype(BF16)

            if w == DA_:
                add_diag(1)
            begin(w)
            if w == DB_:
                load_plane(1)
                load_outer(0)

        trade(0).wait_recv()
        trade(1).wait_recv()

        @pl.loop(0, half // step)
        def _(r):
            rows = rows_at(r * step, step)
            own = rows_at(own_at + r * step, step)
            h = hgrad[rows, :]
            obuf[rows, :] = (h + acc_o[own, :] + take[1, rows, :].astype(F32)).astype(BF16)
            ng = acc_n[own, :] + take[0, rows, :].astype(F32)
            sc = lax.rsqrt(jnp.mean(h * h, axis=-1, keepdims=True) + EPS)
            unit = h * sc
            acc_gain(8, ng * unit)
            e = ng * gain2_ref[...]
            hg = din[own, :].astype(F32) + sc * (e - unit * jnp.mean(e * unit, axis=-1, keepdims=True))
            hgrad[rows, :] = hg
            attn_in[own, :] = hg.astype(BF16)

        add_plane(1)
        add_outer(0)
        token_copies(0, obuf, oo, True)

    def acc_gain(at, v):
        s = jnp.sum(v, axis=0, keepdims=True)
        for k in range(width // 128):
            gain_out[at + k : at + k + 1, :] += s[:, k * 128 : (k + 1) * 128]

    pl.run_scoped(
        ffn,
        pltpu.VMEM((width, 2 * TILE), BF16), pltpu.VMEM((width, 2 * TILE), BF16), pltpu.VMEM((2 * TILE, width), BF16),
        pltpu.VMEM((seq, width), F32), pltpu.VMEM((seq, width), F32), pltpu.VMEM((PIECES, seq, 2 * TILE), BF16),
        pltpu.VMEM((seq, 4 * TILE), BF16),
    )

    def gain_copy(i):
        to = (mate, place.column(c, 2 * place.half + 1 - par), place.column(c, 2 - 2 * place.half + par), place.plane(1),
              place.plane(2))[i]
        return remote(gain_out, gain_in.at[i], gs.at[i], gr.at[i], to)

    def attn_swap():
        own = rows_at(own_at, half)
        return remote(attn_in.at[own], attn_in.at[own], ms.at[3], mr.at[3], mate)

    attn_swap().start()

    def attention(dos, dq, dk, dv, drow):
        def front(wo, att, linv):
            loads = [load(4, h_att, att), load(5, h_linv, linv)]
            for cp in loads:
                cp.start()
            weight_load(1, wo, True)
            for cp in loads:
                cp.wait()
            weight_load(1, wo, False)
            other = rows_at(other_at, half)
            remote(attn_in.at[other], attn_in.at[other], ms.at[3], mr.at[3], mate).wait_recv()

            @pl.loop(0, seq // BLK)
            def _(r):
                rows = rows_at(r * BLK, BLK)
                left = lax.broadcasted_iota(jnp.int32, (BLK, 128), 1) < 64
                for p in range(2):
                    ag = mm_nt(attn_in[rows, :], wo[p]).astype(BF16).astype(F32)
                    for s in range(2):
                        g = 2 * p + s
                        cols = slice(g * 128, (g + 1) * 128)
                        d = ag[:, s * 128 : (s + 1) * 128] * linv[rows, cols]
                        d0, d1 = jnp.where(left, d, 0.0).astype(BF16), jnp.where(left, 0.0, d).astype(BF16)
                        dos[g, 0, rows, :] = d0
                        dos[g, 1, rows, :] = d1
                        o = att[rows, cols].astype(F32)
                        one = jnp.ones((8, 128), BF16)
                        for k, dd in enumerate((d0, d1)):
                            prod = dd.astype(F32) * o
                            high = prod.astype(BF16)
                            low = (prod - high.astype(F32)).astype(BF16)
                            drow[g, k, :, rows] = mm_nt(one, high) + mm_nt(one, low)

            @pl.loop(0, width // BLK)
            def _(r):
                cols = pl.ds(pl.multiple_of(r * BLK, BLK), BLK)
                for p in range(2):
                    grads[O_][p, :, cols] = mm_tn(att[:, p * 256 : (p + 1) * 256], attn_in[:, cols]).astype(BF16)

            add_diag(2)
            begin(O_)
            load_column(0)
            load_outer(1)

        pl.run_scoped(
            front, pltpu.VMEM(go.shape, BF16), pltpu.VMEM(h_att.shape, BF16), pltpu.VMEM(h_linv.shape, F32),
        )
        def rest(q, k, v, mt, qk, rows_, wqkv):
            normed = din
            trade(1).wait_send()
            x = give.at[1]
            loads = [load(6, h_q, q), load(7, h_k, k), load(8, h_v, v)]
            later = [load(9, h_qk, qk), load(11, h_normed, normed)]
            for cp in loads + later:
                cp.start()
            weight_load(0, wqkv, True)
            fetch_load(0, x_ref, hx, x, True)
            for cp in loads:
                cp.wait()
            dq[...] = jnp.zeros(dq.shape, F32)
            todo = {
                0: [lambda: add_column(0), lambda: add_outer(1)],
                1: [lambda: add_diag(DA_)],
                2: [lambda: load_plane(2)],
                3: [lambda: add_plane(2), lambda: add_diag(DB_)],
            }
            for jb in range(seq // BLK):
                at = jb * BLK
                ni = seq - at
                keys = pl.ds(at, BLK)
                cols = pl.ds(at, ni)
                ki = lax.broadcasted_iota(jnp.int32, (BLK, ni), 0)
                qi = lax.broadcasted_iota(jnp.int32, (BLK, ni), 1)
                same = jnp.logical_and(ki < qi, cols_ref[keys, 1:] == rows_ref[:1, cols])
                mt[:, :ni] = jnp.where(jnp.logical_or(ki == qi, same), 1.0, 0.0).astype(F32)

                @pl.loop(0, 4)
                def _(g):
                    kb = k[g, keys, :]
                    qb = q[g, :, cols, :].reshape(2 * ni, 128)
                    db = dos[g, :, cols, :].reshape(2 * ni, 128)
                    m = mt[:, :ni]
                    e = jnp.exp(mm_nt(kb, qb)) * jnp.concatenate([m, m], axis=1)
                    dv[g, keys, :] = mm(e.astype(BF16), db)
                    dp = mm_nt(v[g, keys, :], db)
                    dr = jnp.concatenate([drow[g, 0, :1, cols], drow[g, 1, :1, cols]], axis=1)
                    ds = (e * (dp - dr)).astype(BF16)
                    dk[g, keys, :] = mm(ds, qb)
                    dqs = mm_tn(ds, kb)
                    left = lax.broadcasted_iota(jnp.int32, (ni, 128), 1) < 64
                    lanes = pl.ds(pl.multiple_of(g * 128, 128), 128)
                    dq[cols, lanes] += jnp.where(left, dqs[:ni], dqs[ni:])

                for f in todo[jb]:
                    f()
            for cp in later:
                cp.wait()
            weight_load(0, wqkv, False)
            fetch_load(0, x_ref, hx, x, False)

            @pl.loop(0, seq // BLK)
            def _(r):
                rows = rows_at(r * BLK, BLK)
                cos, sin = cos_ref[rows, :], sin_ref[rows, :]
                left = lax.broadcasted_iota(jnp.int32, (BLK, 128), 1) < 64

                def fold(ref, p):
                    a, b = ref[2 * p, rows, :], ref[2 * p + 1, rows, :]
                    return jnp.where(left, a + pltpu.roll(a, 64, 1), b + pltpu.roll(b, 64, 1))

                for p in range(2):
                    raw = qk[p, rows, :]
                    sc = lax.rsqrt(head_mean(raw * raw, ones_ref, 384) + EPS)
                    unit = raw * sc
                    parts = []
                    for s in range(3):
                        if s < 2:
                            v_ = dq[rows, (2 * p + s) * 128 : (2 * p + s + 1) * 128] * 0.125
                        else:
                            v_ = fold(dk, p)
                        v_ = v_.astype(BF16).astype(F32)
                        parts.append(v_ * cos - lane_swap(v_) * sin)
                    ng = jnp.concatenate(parts, axis=1)
                    gsum = jnp.sum(ng * unit, axis=0, keepdims=True)
                    qsum = gsum[:, :128] + gsum[:, 128:256]
                    ksum = gsum[:, 256:]
                    gain_out[16:17, :] += qsum
                    gain_out[17:18, :] += ksum
                    e = ng * gainqk_ref[...]
                    back = sc * (e - unit * head_mean(e * unit, ones_ref, 384))
                    rows_[p, rows, :384] = back.astype(BF16)
                    rows_[p, rows, 384:] = fold(dv, p).astype(BF16)

            def back_rows(start):
                at = rows_at(start, BLK)
                return mm_nt(rows_[0, at, :], wqkv[0]) + mm_nt(rows_[1, at, :], wqkv[1])

            trade(0).wait_send()

            @pl.loop(0, half // BLK)
            def _(r):
                give[0, rows_at(r * BLK, BLK), :] = back_rows(other_at + r * BLK).astype(BF16)

            trade(2).start()
            load_plane(DA_)
            add_diag(O_)
            trade(2).wait_recv()
            token_copies(0, obuf, oo, False)

            @pl.loop(0, half // BLK)
            def _(r):
                rows = rows_at(r * BLK, BLK)
                ng = back_rows(own_at + r * BLK) + take[0, rows, :].astype(F32)
                xs = x[rows, :].astype(F32)
                sc = lax.rsqrt(jnp.mean(xs * xs, axis=-1, keepdims=True) + EPS)
                unit = xs * sc
                acc_gain(0, ng * unit)
                e = ng * gain1_ref[...]
                ig = hgrad[rows, :] + sc * (e - unit * jnp.mean(e * unit, axis=-1, keepdims=True))
                obuf[rows, :] = ig.astype(BF16)

            token_copies(1, obuf, io, True)
            gain_copy(0).start()
            for p in range(2):
                @pl.loop(0, width // BLK)
                def _(r):
                    cols = pl.ds(pl.multiple_of(r * BLK, BLK), BLK)
                    grads[QKV_][p, cols, :] = mm_tn(normed[:, cols], rows_[p]).astype(BF16)

            begin(QKV_)
            add_plane(DA_)
            load_column(1)
            load_outer(2)

        pl.run_scoped(
            rest, V(h_q.shape, BF16), V(h_k.shape, BF16), V(h_v.shape, BF16), V((BLK, seq), F32), V(h_qk.shape, F32),
            V((2, seq, 512), BF16), V(gqkv.shape, BF16),
        )

    pl.run_scoped(
        attention, pltpu.VMEM(h_q.shape, BF16), pltpu.VMEM((seq, 512), F32), pltpu.VMEM((4, seq, 128), F32),
        pltpu.VMEM((4, seq, 128), F32), pltpu.VMEM((4, 2, 8, seq), F32),
    )
    def gain_step(i, go=True):
        gain_copy(i).wait()
        gain_out[...] += gain_in[i]
        if go:
            gain_copy(i + 1).start()

    add_column(1)
    gain_step(0)
    add_outer(2)
    load_plane(DB_)
    gain_step(1)
    load_outer(DA_)
    load_column(2)
    gain_step(2, False)
    add_plane(DB_)
    load_plane(O_)
    add_outer(DA_)
    add_column(2)
    add_diag(QKV_)
    gain_copy(3).start()
    add_plane(O_)
    load_outer(DB_)
    load_column(DA_)
    add_outer(DB_)
    add_column(DA_)
    load_outer(O_)
    load_plane(QKV_)
    gain_step(3)
    add_plane(QKV_)
    add_outer(O_)
    load_column(DB_)
    load_outer(QKV_)
    gain_step(4, False)
    add_column(DB_)
    add_outer(QKV_)
    load_column(O_)
    add_column(O_)
    load_column(QKV_)
    add_column(QKV_)
    release_last(O_)
    release_last(QKV_)
    for w in range(nw):
        finish(w)
    for n in range(len(pieces)):
        sent(n)
    fetch_copies(0, x_ref, hx, False)
    fetch_copies(1, ct_ref, hc, False)
    trade(2).wait_send()
    attn_swap().wait_send()
    token_copies(1, obuf, io, False)
    token_arrivals(0, obuf, oo)
    token_arrivals(1, obuf, io)


def layer(x, ct, shards, vectors):
    anywhere = pl.BlockSpec(memory_space=pl.ANY)
    vmem = pl.BlockSpec(memory_space=pltpu.VMEM)
    dma = pltpu.SemaphoreType.DMA
    SDS, V = jax.ShapeDtypeStruct, pltpu.VMEM
    seg, width = x.shape[1], x.shape[2]
    half, seq = 2 * seg, 4 * seg
    wqkv, wo, wg, wu, wd = shards
    sizes = [(width, 2 * TILE)] * 3 + [(wd.shape[0], width // 2)] * 2 + [(wo.shape[0], width), (width, wqkv.shape[1])]
    nw, pieces = 7, 2 + 3 * PIECES
    gains = (24, 128)
    results = [(width // 8, 256), (width // 8, 128), (width // 8, 128), (wo.shape[0] // 8, width)]
    results += [(width // 8, wg.shape[1])] * 2 + [(wd.shape[0] // 8, width)]
    held = [((half, width), BF16), ((half, width), BF16), ((seq, width), BF16), ((2, seq, 384), F32), ((4, 2, seq, 128), BF16),
            ((4, seq, 128), BF16), ((4, seq, 128), BF16), ((seq, 512), BF16), ((seq, 512), F32)]
    out_shape = (
        [SDS((2, seg, width), BF16)] * 2
        + [SDS(gains, F32)]
        + [SDS(r, F32) for r in results]
        + [SDS((2,) + s.shape, BF16) for s in shards]
        + [SDS(*h) for h in held]
        + [SDS((2, 2, 2, r // 8, n), BF16) for r, n in sizes]
        + [SDS((2, 2, r // 8, n), BF16) for r, n in sizes]
    )
    e_max, n_max = max(r // 8 for r, _ in sizes), max(n for _, n in sizes)
    out = pl.pallas_call(
        layer_kernel,
        out_shape=out_shape,
        in_specs=[anywhere] * 7 + [vmem] * len(vectors),
        out_specs=[anywhere] * 2 + [vmem] + [anywhere] * (len(out_shape) - 3),
        scratch_shapes=[V((2, r, n), BF16) for r, n in sizes]
        + [V((2, 2, r // 8, n), BF16) for r, n in sizes]
        + [
            V((2, 2, e_max, n_max), F32), V((2, half, width), BF16), V((2, half, width), BF16), V((half, width), BF16),
            V((half, width), F32), V((5,) + gains, F32), V((seq, width), BF16), V((seq, width), BF16),
        ]
        + [
            dma((2, 2)), dma((2, 2)), dma((2, 2)), dma((2, 2)), dma((2, 2)), dma((pieces, 2)), dma((pieces, 2)),
            dma((pieces, 2, 4)), dma((pieces, 2, 4)), dma((nw, 6)), dma((nw, 6)), dma((nw, 2)), dma((nw, 2)), dma((nw, 3)),
            dma((nw, 3)), dma((nw, 3)), dma((5,)), dma((5,)), dma((8,)), dma((8,)), dma((13,)), dma((5, 2)), dma((nw, 2, 2)),
            dma((nw, 2)), dma((9,)),
        ],
        compiler_params=pltpu.CompilerParams(collective_id=0, has_side_effects=True, vmem_limit_bytes=60 * 1024 * 1024),
        name="layer",
    )(x, ct, *shards, *vectors)
    return out[0], out[1], out[2], out[3:10]


def rope_tables(length, width):
    k = np.arange(width // 2)
    angles = np.arange(length)[:, None] * (THETA ** (-2.0 * k / width))[None]
    cos, sin = np.cos(angles), np.sin(angles)
    return (
        jnp.asarray(np.concatenate([cos] * 4, axis=1), F32),
        jnp.asarray(np.concatenate([-sin, sin] * 2, axis=1), F32),
    )


def per_device(n_dp, inputs, query_weight, key_weight, value_weight, out_weight, gate_weight, up_weight, down_weight,
               attn_gain, ffn_gain, query_gain, key_gain, cotangent, segment_ids, padding, row_count):
    slots, _, width = inputs.shape
    seq_len = segment_ids.shape[1]
    head_dim = query_gain.shape[0]
    nq, nk = query_weight.shape[1], key_weight.shape[1]
    z = lax.axis_index("tensor")
    c = lax.axis_index("dp") % 2
    groups = n_dp // 8

    alive_all = padding * (jnp.arange(slots)[:, None] < row_count[0]).astype(jnp.int32)
    code = (segment_ids + ALIVE * alive_all)[z % 2]
    code = jnp.where(c == z // 2, code, lax.ppermute(code, "dp", [(i, i ^ 1) for i in range(n_dp)]))
    segment, alive_row = code % ALIVE, code // ALIVE
    key_code = jnp.where(alive_row > 0, segment, -1)
    codes = jnp.stack([segment, key_code])

    qkv_shard = jnp.concatenate([query_weight, key_weight, value_weight], axis=1)
    cos, sin = rope_tables(seq_len, head_dim)
    gain_qk = jnp.concatenate([query_gain] * (nq // head_dim) + [key_gain] * (nk // head_dim))[None]
    lanes = np.arange(nq + nk) // head_dim
    ones = jnp.asarray(np.where(lanes[:, None] == lanes[None], 1.0 / head_dim, 0.0), BF16)
    gain1, gain2 = attn_gain[None], ffn_gain[None]
    outs, in_grad, gains, sums = layer(
        inputs, cotangent, (qkv_shard, out_weight, gate_weight, up_weight, down_weight),
        (codes.T, codes, gain1, gain2, gain_qk, cos, sin,
         ones),
    )
    if groups > 1:
        same = [[g * 8 + k for g in range(groups)] for k in range(8)]
        sums = [lax.psum_scatter(s, "dp", scatter_dimension=0, axis_index_groups=same, tiled=True) for s in sums]
        gains = lax.psum(gains, "dp", axis_index_groups=same)
    pair = gains[16:18, :head_dim] + gains[16:18, head_dim:]
    return (
        outs,
        in_grad.astype(F32),
        *sums,
        gains[:8].reshape(-1),
        gains[8:16].reshape(-1),
        pair[0],
        pair[1],
    )


def solution(mesh):
    return jax.shard_map(
        functools.partial(per_device, mesh.shape["dp"]),
        mesh=mesh,
        in_specs=(
            P("dp", "tensor", None),
            P(None, "tensor"),
            P(None, "tensor"),
            P(None, "tensor"),
            P("tensor", None),
            P(None, "tensor"),
            P(None, "tensor"),
            P("tensor", None),
            P(),
            P(),
            P(),
            P(),
            P("dp", "tensor", None),
            P("dp", None),
            P("dp", None),
            P("dp"),
        ),
        out_specs=(
            P("dp", "tensor", None),
            P("dp", "tensor", None),
            P("dp", "tensor"),
            P("dp", "tensor"),
            P("dp", "tensor"),
            P(("tensor", "dp"), None),
            P("dp", "tensor"),
            P("dp", "tensor"),
            P(("tensor", "dp"), None),
            P(),
            P(),
            P(),
            P(),
        ),
        check_vma=False,
    )
```

```python
import functools

import jax
import jax.numpy as jnp
import numpy as np
from jax import lax
from jax.experimental import pallas as pl
from jax.experimental.pallas import tpu as pltpu
from jax.sharding import PartitionSpec as P

EPS = 1e-05
THETA = 1000000.0
ALIVE = 4096
MESH = pl.DeviceIdType.MESH
BF16 = jnp.bfloat16
F32 = jnp.float32


class Place:
    def __init__(self):
        self.dp = lax.axis_index("dp")
        self.z = lax.axis_index("tensor")
        self.c = lax.rem(self.dp, 2)
        self.j = lax.rem(self.dp // 2, 4)
        self.half = self.z // 2
        self.par = lax.rem(self.z, 2)
        self.near = self.half == self.c

    def plane(self, k):
        j = self.j
        bit = lax.rem(j // k, 2)
        return (self.dp + (1 - 2 * bit) * 2 * k, self.z)

    def column(self, c, z):
        return (self.dp - self.c + c, z)

    def quarter(self, k):
        j = self.j
        low, high = lax.rem(j, 2), j // 2
        if k & 1:
            low = 1 - low
        if k & 2:
            high = 1 - high
        return 2 * high + low


def greet(place):
    barrier = pltpu.get_barrier_semaphore()
    for k in (1, 2):
        pl.semaphore_signal(barrier, inc=1, device_id=place.plane(k), device_id_type=MESH)
    for dc in range(2):
        for dz in range(4):
            if dc or dz:
                c = lax.rem(place.c + dc, 2)
                z = lax.rem(place.z + dz, 4)
                pl.semaphore_signal(barrier, inc=1, device_id=place.column(c, z), device_id_type=MESH)
    pl.semaphore_wait(barrier, 9)


def remote(src, dst, send, recv, device):
    return pltpu.make_async_remote_copy(
        src_ref=src, dst_ref=dst, send_sem=send, recv_sem=recv, device_id=device, device_id_type=MESH
    )


def lane_swap(v):
    lane = lax.broadcasted_iota(jnp.int32, v.shape, 1)
    return jnp.where(lane % 64 < 32, pltpu.roll(v, 96, 1), pltpu.roll(v, 32, 1))


def head_mean(v, ones_ref, n):
    high = v.astype(BF16)
    low = (v - high.astype(F32)).astype(BF16)
    ones = ones_ref[:n, :n]
    return jnp.dot(high, ones, preferred_element_type=F32) + jnp.dot(low, ones, preferred_element_type=F32)


def mm(a, b):
    return jnp.dot(a, b, preferred_element_type=F32)


def mm_nt(a, b):
    return lax.dot_general(a, b, (((1,), (1,)), ((), ())), preferred_element_type=F32)


def mm_tn(a, b):
    return lax.dot_general(a, b, (((0,), (0,)), ((), ())), preferred_element_type=F32)


BLK = 256


def rows_at(start, size):
    return pl.ds(pl.multiple_of(start, size), size)


TILE = 384
PIECES = 3


def layer_kernel(x_ref, ct_ref, wqkv_ref, wo_ref, wg_ref, wu_ref, wd_ref, cols_ref, rows_ref,
                 gain1_ref, gain2_ref, gainqk_ref, cos_ref, sin_ref, ones_ref,
                 oo, io, gain_out, s_q, s_k, s_v, s_o, s_gate, s_up, s_down,
                 gqkv, go, gg, gu, gd, hx, hc, h_normed, h_qk, h_q, h_k, h_v, h_att, h_linv,
                 p_gu0, p_gu1, p_gu2, p_d0, p_d1, p_o, p_qkv, c_gu0, c_gu1, c_gu2, c_d0, c_d1, c_o, c_qkv,
                 g_a, g_b, g_c, g_d0, g_d1, g_o, g_qkv, d_gu0, d_gu1, d_gu2, d_d0, d_d1, d_o, d_qkv, last, give, take, obuf, hgrad,
                 gain_in, attn_in, din,
                 in_s, in_r, tok_s, tok_r, tok_l, zs, zr, fs, fr, ps, pr, cs, cr, ls, lr, ll, gs, gr, ms, mr, ld, wl, pls, cls,
                 outs):
    shards = (wqkv_ref, wo_ref, wg_ref, wu_ref, wd_ref)
    full = (gqkv, go, gg, gu, gd)
    grads = (g_a, g_b, g_c, g_d0, g_d1, g_o, g_qkv)
    diag = (d_gu0, d_gu1, d_gu2, d_d0, d_d1, d_o, d_qkv)
    plane_in = (p_gu0, p_gu1, p_gu2, p_d0, p_d1, p_o, p_qkv)
    col_in = (c_gu0, c_gu1, c_gu2, c_d0, c_d1, c_o, c_qkv)
    nw = 7
    DA_, DB_, O_, QKV_ = 3, 4, 5, 6
    turn = (0, 1, 2, 3, 4, 5, 6)
    place = Place()
    z, c, par, near, j = place.z, place.c, place.par, place.near, place.j
    inner = jnp.where(c == 0, z == 2, z == 1)
    outer = jnp.where(c == 0, z == 3, z == 0)
    half = obuf.shape[0]
    seq = 2 * half
    seg = half // 2
    width = obuf.shape[1]
    mate = place.column(1 - c, z)
    own_at = c * half
    other_at = (1 - c) * half
    step = 128
    n2 = attn_in
    normed_buf = din
    greet(place)

    def fetch_copies(a, src, dst, go):
        for b in range(2):
            slot = par if b == 0 else 1 - par
            target = place.column(place.half, 2 * c + slot)

            def far_copy():
                cp = remote(src.at[slot], dst.at[rows_at(par * seg, seg)], in_s.at[a, b], in_r.at[a, par], target)
                cp.start() if go else cp.wait_send()

            if b == 0:
                pl.when(jnp.logical_not(near))(far_copy)
            else:
                far_copy()

    def fetch_arrivals(a, src, dst):
        for h in range(2):
            @pl.when(jnp.logical_not(near & (par == h)))
            def _():
                remote(src.at[0], dst.at[pl.ds(h * seg, seg)], in_s.at[a, 0], in_r.at[a, h], place.plane(1)).wait_recv()

    def fetch_load(a, src, landed, dst, go):
        for h in range(2):
            here = dst.at[pl.ds(h * seg, seg)]
            came = pltpu.make_async_copy(landed.at[pl.ds(h * seg, seg)], here, tok_l.at[a, h])
            if go:
                mine = near & (par == h)
                pl.when(mine)(lambda: pltpu.make_async_copy(src.at[h], here, tok_l.at[a, h]).start())
                pl.when(jnp.logical_not(mine))(came.start)
            else:
                came.wait()

    pieces = [(0, 256, 0, None), (1, 64, 0, None)]
    for t in range(PIECES):
        pieces += [(2, 256, 0, t), (3, 256, 0, t), (4, TILE // 4, t * TILE, None)]
    WQKV, WO = 0, 1

    def tile_pieces(t):
        return (2 + 3 * t, 3 + 3 * t, 4 + 3 * t)

    def piece_at(ref, n, k, side=None, p=None):
        w, q, at, t = pieces[n]
        start, size = pl.multiple_of(at + place.quarter(k) * q, 16), q
        if side is not None:
            size = q // 2
            start = pl.multiple_of(start + side * size, 16)
        index = (pl.ds(start, size),) + (() if t is None else (pl.ds(t * TILE, TILE),))
        return ref.at[index if p is None else (p,) + index]

    def part(n, p, k, side=None):
        return piece_at(full[pieces[n][0]], n, k, side, p)

    def z_copies(n, go):
        @pl.when(near)
        def _():
            for i, to in enumerate((2 - c, 2 * place.half + 1 - par)):
                cp = remote(piece_at(shards[pieces[n][0]], n, 0), part(n, par, 0), zs.at[n, i], zr.at[n, par], place.column(c, to))
                cp.start() if go else cp.wait_send()

    def z_onward(n, p):
        return remote(part(n, p, 0), part(n, p, 0), zs.at[n, p], zr.at[n, p], place.column(c, 3 - 3 * c))

    def missing(p, body):
        pl.when(jnp.logical_or(jnp.logical_not(near), par != p))(body)

    def step_copy(n, p, i):
        k, side, to = ((0, None, 1), (0, None, 2), (1, 0, 2), (2, 1, 1))[i]
        return remote(part(n, p, k, side), part(n, p, k, side), fs.at[n, p, i], fr.at[n, p, i], place.plane(to))

    def first(n):
        for p in range(2):
            @functools.partial(missing, p)
            def _():
                z_onward(n, p).wait_recv()
                pl.when(inner)(lambda: z_onward(n, p).start())
                step_copy(n, p, 0).start()
                step_copy(n, p, 1).start()

    def second(n):
        for p in range(2):
            @functools.partial(missing, p)
            def _():
                step_copy(n, p, 0).wait_recv()
                step_copy(n, p, 2).start()
                step_copy(n, p, 1).wait_recv()
                step_copy(n, p, 3).start()

    def third(n):
        for p in range(2):
            @functools.partial(missing, p)
            def _():
                step_copy(n, p, 2).wait_recv()
                step_copy(n, p, 3).wait_recv()

    def sent(n):
        z_copies(n, False)
        for p in range(2):
            @functools.partial(missing, p)
            def _():
                pl.when(inner)(lambda: z_onward(n, p).wait_send())
                for i in range(4):
                    step_copy(n, p, i).wait_send()

    def weight_load(w, dst, go):
        for p in range(2):
            came = pltpu.make_async_copy(full[w].at[p], dst.at[p], wl.at[w, p])
            if go:
                mine = near & (par == p)
                pl.when(mine)(lambda: pltpu.make_async_copy(shards[w], dst.at[p], wl.at[w, p]).start())
                pl.when(jnp.logical_not(mine))(came.start)
            else:
                came.wait()

    def token_copies(a, src, dst, go):
        for b in range(2):
            h = par if b == 0 else 1 - par
            piece = src.at[rows_at(h * seg, seg)]
            target = place.column(place.half, 2 * c + h)
            there = dst.at[par]

            def far_copy():
                cp = remote(piece, there, tok_s.at[a, b], tok_r.at[a, par], target)
                cp.start() if go else cp.wait_send()

            if b == 0:
                @pl.when(near)
                def _():
                    cp = pltpu.make_async_copy(piece, there, tok_l.at[a, 0])
                    cp.start() if go else cp.wait()

                pl.when(jnp.logical_not(near))(far_copy)
            else:
                far_copy()

    def token_arrivals(a, src, dst):
        for s in range(2):
            @pl.when(jnp.logical_not(near & (par == s)))
            def _():
                remote(src.at[pl.ds(0, seg)], dst.at[s], tok_s.at[a, 0], tok_r.at[a, s], place.plane(1)).wait_recv()

    def rows_of(w, k, side=None):
        q = grads[w].shape[1] // 4
        start, size = pl.multiple_of(place.quarter(k) * q, q), q
        if side is not None:
            size = q // 2
            start = pl.multiple_of(start + side * size, size)
        return pl.ds(start, size)

    def diag_copy(w, side):
        return remote(grads[w].at[:, rows_of(w, 3, side)], diag[w].at[side], ps.at[w, side], pr.at[w, side], place.plane(1 + side))

    def plane_copy(w, i, side):
        src = grads[w].at[:, rows_of(w, 1 + i, side)] if side == i else diag[w].at[side]
        n = 2 + 2 * i + side
        return remote(src, plane_in[w].at[i, side], ps.at[w, n], pr.at[w, n], place.plane(1 + i))

    def begin(w):
        diag_copy(w, 0).start()
        diag_copy(w, 1).start()
        plane_copy(w, 0, 0).start()
        plane_copy(w, 1, 1).start()

    def add_diag(w):
        for side in (0, 1):
            diag_copy(w, side).wait()
            rows = rows_of(w, 2 - side, side)
            for p in range(2):
                diag[w][side, p] = (grads[w][p, rows, :].astype(F32) + diag[w][side, p].astype(F32)).astype(BF16)
            plane_copy(w, 1 - side, side).start()

    def outer_copy(w):
        return remote(diag[w], col_in[w], cs.at[w, 0], cr.at[w, 0], place.column(c, z - 1 + 2 * c))

    def inner_copy(w, p):
        return remote(diag[w].at[:, p], col_in[w].at[:, 1], cs.at[w, p], cr.at[w, 1], place.column(c, 2 * c + p))

    def near_copy(w):
        to = place.column(c, 2 * place.half + 1 - par)
        return remote(diag[w].at[:, 1 - par], col_in[w].at[:, 0], cs.at[w, 0], cr.at[w, 0], to)

    def plane_local(w, i, side):
        return pltpu.make_async_copy(plane_in[w].at[i, side], grads[w].at[:, rows_of(w, 1 + i, side)], pls.at[w, i, side])

    def col_local(w, side):
        return pltpu.make_async_copy(col_in[w].at[side], grads[w].at[:, rows_of(w, 3, side)], cls.at[w, side])

    def load_plane(w):
        for i in range(2):
            for side in range(2):
                plane_copy(w, i, side).wait()
        for i in range(2):
            for side in range(2):
                plane_local(w, i, side).start()

    def add_plane(w):
        for side in range(2):
            for i in range(2):
                plane_local(w, i, side).wait()
            mine, one, two = rows_of(w, 0, side), rows_of(w, 1, side), rows_of(w, 2, side)
            for p in range(2):
                total = grads[w][p, mine, :].astype(F32) + grads[w][p, one, :].astype(F32) + grads[w][p, two, :].astype(F32)
                diag[w][side, p] = total.astype(BF16)
        pl.when(outer)(lambda: outer_copy(w).start())
        pl.when(near)(lambda: near_copy(w).start())

    def load_outer(w):
        @pl.when(inner)
        def _():
            outer_copy(w).wait_recv()
            for side in range(2):
                col_local(w, side).start()

    def add_outer(w):
        @pl.when(inner)
        def _():
            for side in range(2):
                col_local(w, side).wait()
            for p in range(2):
                for side in range(2):
                    came = grads[w][p, rows_of(w, 3, side), :].astype(F32)
                    diag[w][side, p] = (diag[w][side, p].astype(F32) + came).astype(BF16)
                inner_copy(w, p).start()

    def last_copies(w, k):
        e = grads[w].shape[1] // 8
        if w < PIECES:
            cut = ((0, TILE, s_gate, w * TILE), (TILE, TILE, s_up, w * TILE))
        elif w == QKV_:
            cut = ((0, 256, s_q, 0), (256, 128, s_k, 0), (384, 128, s_v, 0))
        else:
            n = grads[w].shape[2]
            cut = ((0, n, s_o, 0),) if w == O_ else ((0, n, s_down, (w - DA_) * n),)
        return [(last.at[turn[w] % 2, k, pl.ds(0, e), pl.ds(at, n)], ref.at[:, pl.ds(to, n)]) for at, n, ref, to in cut]

    def last_remote(w):
        return [remote(src, dst, ls.at[w, i], lr.at[w, i], mate) for i, (src, dst) in enumerate(last_copies(w, 1))]

    def last_local(w):
        return [pltpu.make_async_copy(src, dst, ll.at[w, i]) for i, (src, dst) in enumerate(last_copies(w, 0))]

    def release_last(w):
        @pl.when(near)
        def _():
            for cp in last_remote(w):
                cp.wait_send()
            for cp in last_local(w):
                cp.wait()

    def load_column(w):
        @pl.when(near)
        def _():
            near_copy(w).wait_recv()
            inner_copy(w, 0).wait_recv()
            for side in range(2):
                col_local(w, side).start()

    def add_column(w):
        if turn[w] >= 2:
            release_last(turn.index(turn[w] - 2))

        @pl.when(near)
        def _():
            e, n = grads[w].shape[1] // 8, grads[w].shape[2]
            for hc in range(2):
                col_local(w, hc).wait()
                came = rows_of(w, 3, hc)
                total = diag[w][hc, par].astype(F32) + grads[w][0, came, :].astype(F32) + grads[w][1, came, :].astype(F32)

                @pl.when(c == hc)
                def _():
                    last[turn[w] % 2, 0, :e, :n] = total

                @pl.when(c != hc)
                def _():
                    last[turn[w] % 2, 1, :e, :n] = total

            for cp in last_remote(w) + last_local(w):
                cp.start()

    def finish(w):
        pl.when(near)(lambda: near_copy(w).wait_send())

        @pl.when(jnp.logical_not(near))
        def _():
            for cp in last_remote(w):
                cp.wait_recv()

        pl.when(outer)(lambda: outer_copy(w).wait_send())

        @pl.when(inner)
        def _():
            inner_copy(w, 0).wait_send()
            inner_copy(w, 1).wait_send()

    def trade(n):
        return remote(give.at[n % 2], take.at[n % 2], ms.at[n], mr.at[n], mate)

    def load(n, src, dst):
        return pltpu.make_async_copy(src, dst, ld.at[n])

    for n in range(len(pieces)):
        z_copies(n, True)
        if n == 3:
            fetch_copies(0, x_ref, hx, True)
        if n == 8:
            fetch_copies(1, ct_ref, hc, True)

    def swap_rows(buf, n):
        own = rows_at(own_at, half)
        return remote(buf.at[own], buf.at[own], ms.at[n], mr.at[n], mate)

    def swap_wait(buf, n):
        other = rows_at(other_at, half)
        remote(buf.at[other], buf.at[other], ms.at[n], mr.at[n], mate).wait_recv()

    def phase_one(wqkv, wo, xbuf, cbuf, qk, qs, k2, v2, mask, att, linv):
        saves = []

        def save(n, src, dst):
            cp = pltpu.make_async_copy(src, dst, outs.at[n])
            saves.append(cp)
            cp.start()

        for i in range(seq // BLK):
            for jb in range(i + 1):
                same = cols_ref[i * BLK : (i + 1) * BLK, :1] == rows_ref[1:, jb * BLK : (jb + 1) * BLK]
                if i == jb:
                    ri = lax.broadcasted_iota(jnp.int32, (BLK, BLK), 0)
                    ci = lax.broadcasted_iota(jnp.int32, (BLK, BLK), 1)
                    same = jnp.logical_or(ri == ci, jnp.logical_and(ci < ri, same))
                mask[i * BLK : (i + 1) * BLK, jb * BLK : (jb + 1) * BLK] = jnp.where(same, 1.0, 0.0).astype(F32)
        v2[:, :, 128:] = jnp.ones((v2.shape[0], v2.shape[1], 128), BF16)
        first(WQKV)
        first(WO)
        second(WQKV)
        second(WO)
        for n in tile_pieces(0):
            first(n)
        third(WQKV)
        weight_load(0, wqkv, True)
        for n in tile_pieces(0):
            second(n)
        third(WO)
        weight_load(1, wo, True)

        fetch_arrivals(0, x_ref, hx)
        fetch_load(0, x_ref, hx, xbuf, True)
        fetch_load(0, x_ref, hx, xbuf, False)

        @pl.loop(0, half // step)
        def _(r):
            xs = xbuf[rows_at(r * step, step), :].astype(F32)
            sc = lax.rsqrt(jnp.mean(xs * xs, axis=-1, keepdims=True) + EPS)
            normed_buf[rows_at(own_at + r * step, step), :] = (xs * sc * gain1_ref[...]).astype(BF16)

        swap_rows(normed_buf, 4).start()
        first(tile_pieces(1)[0])
        weight_load(0, wqkv, False)
        swap_wait(normed_buf, 4)
        normed = normed_buf
        save(1, normed, h_normed)

        @pl.loop(0, seq // BLK)
        def _(r):
            rows = rows_at(r * BLK, BLK)
            cos, sin = cos_ref[rows, :], sin_ref[rows, :]
            lane = lax.broadcasted_iota(jnp.int32, (BLK, 128), 1)
            left = lane < 64
            for p in range(2):
                proj = mm(normed[rows, :], wqkv[p])
                pq = proj[:, :384]
                qk[p, rows, :] = pq
                sc = lax.rsqrt(head_mean(pq * pq, ones_ref, 384) + EPS)
                n = pq * sc * gainqk_ref[...]
                for s in range(3):
                    v = n[:, s * 128 : (s + 1) * 128]
                    rot = v * cos + lane_swap(v) * sin
                    if s < 2:
                        qr = rot.astype(BF16).astype(F32) * 0.125
                        qs[2 * p + s, 0, rows, :] = jnp.where(left, qr, 0.0).astype(BF16)
                        qs[2 * p + s, 1, rows, :] = jnp.where(left, 0.0, qr).astype(BF16)
                    else:
                        kr = pltpu.roll(rot, 64, 1)
                        k2[2 * p, rows, :] = jnp.where(left, rot, kr).astype(BF16)
                        k2[2 * p + 1, rows, :] = jnp.where(left, kr, rot).astype(BF16)
                v = proj[:, 384:]
                vr = pltpu.roll(v, 64, 1)
                v2[2 * p, rows, :128] = jnp.where(left, v, vr).astype(BF16)
                v2[2 * p + 1, rows, :128] = jnp.where(left, vr, v).astype(BF16)

        save(3, qk, h_qk)
        save(4, qs, h_q)
        save(5, k2, h_k)
        save(6, v2.at[:, :, pl.ds(0, 128)], h_v)
        first(tile_pieces(1)[1])
        first(tile_pieces(1)[2])
        second(tile_pieces(1)[0])
        for i in range(seq // BLK):
            n = (i + 1) * BLK
            rows = pl.ds(i * BLK, BLK)

            @pl.loop(0, k2.shape[0])
            def _(g):
                s = mm_nt(qs[g, :, rows, :].reshape(2 * BLK, 128), k2[g, :n, :])
                e = jnp.exp(s).reshape(2, BLK, n) * mask[rows, :n][None]
                acc = mm(e.astype(BF16).reshape(2 * BLK, n), v2[g, :n, :])
                inv = 1.0 / acc[:, 128:]
                o = acc[:, :128] * inv
                left = lax.broadcasted_iota(jnp.int32, (BLK, 128), 1) < 64
                cols = pl.ds(pl.multiple_of(g * 128, 128), 128)
                att[rows, cols] = jnp.where(left, o[:BLK], o[BLK:]).astype(BF16)
                linv[rows, cols] = jnp.where(left, inv[:BLK], inv[BLK:])

        save(7, att, h_att)
        save(8, linv, h_linv)
        second(tile_pieces(1)[1])
        second(tile_pieces(1)[2])
        weight_load(1, wo, False)

        def out_rows(start):
            return mm(att[rows_at(start, BLK), :], wo[...].reshape(2 * wo.shape[1], wo.shape[2]))

        @pl.loop(0, half // BLK)
        def _(r):
            give[0, rows_at(r * BLK, BLK), :] = out_rows(other_at + r * BLK).astype(BF16)

        saves[0].wait()
        swap_rows(normed_buf, 4).wait_send()
        swap_give = remote(give.at[0], take.at[0], ms.at[5], mr.at[5], mate)
        swap_give.start()

        @pl.loop(0, half // BLK)
        def _(r):
            hgrad[rows_at(r * BLK, BLK), :] = out_rows(own_at + r * BLK) + xbuf[rows_at(r * BLK, BLK), :].astype(F32)

        fetch_arrivals(1, ct_ref, hc)
        fetch_load(1, ct_ref, hc, cbuf, True)
        swap_give.wait_recv()

        @pl.loop(0, half // step)
        def _(r):
            h = hgrad[rows_at(r * step, step), :] + take[0, rows_at(r * step, step), :].astype(F32)
            hgrad[rows_at(r * step, step), :] = h
            sc = lax.rsqrt(jnp.mean(h * h, axis=-1, keepdims=True) + EPS)
            n2[rows_at(own_at + r * step, step), :] = (h * sc * gain2_ref[...]).astype(BF16)

        swap_rows(n2, 6).start()
        fetch_load(1, ct_ref, hc, cbuf, False)

        @pl.loop(0, half // step)
        def _(r):
            own = rows_at(own_at + r * step, step)
            v = cbuf[rows_at(r * step, step), :].astype(F32) * jnp.where(cols_ref[own, 1:] >= 0, 1.0, 0.0)
            din[own, :] = v.astype(BF16)

        swap_rows(din, 7).start()
        for n in tile_pieces(0):
            third(n)
        swap_wait(n2, 6)
        swap_wait(din, 7)
        swap_rows(n2, 6).wait_send()
        swap_rows(din, 7).wait_send()
        swap_give.wait_send()
        for cp in saves[1:]:
            cp.wait()

    V = pltpu.VMEM
    gain_out[...] = jnp.zeros(gain_out.shape, F32)
    pl.run_scoped(
        phase_one, V(gqkv.shape, BF16), V(go.shape, BF16), V((half, width), BF16), V((half, width), BF16), V(h_qk.shape, F32),
        V(h_q.shape, BF16), V(h_k.shape, BF16), V((4, seq, 256), BF16), V((seq, seq), F32), V(h_att.shape, BF16),
        V(h_linv.shape, F32),
    )

    def ffn(wg, wu, wd, acc_o, acc_n, act, gu_rows):
        def tile_loads(t, go):
            cols = pl.ds(t * TILE, TILE)
            for p in range(2):
                here = pl.ds(p * TILE, TILE)

                def run(g, u, d):
                    pairs = ((g.at[:, cols], wg.at[:, here]), (u.at[:, cols], wu.at[:, here]), (d.at[cols], wd.at[here]))
                    for k, (src, dst) in enumerate(pairs):
                        cp = pltpu.make_async_copy(src, dst, wl.at[2 + k, p])
                        cp.start() if go else cp.wait()

                if go:
                    mine = near & (par == p)
                    pl.when(mine)(lambda: run(wg_ref, wu_ref, wd_ref))
                    pl.when(jnp.logical_not(mine))(lambda: run(gg.at[p], gu.at[p], gd.at[p]))
                else:
                    run(gg.at[p], gu.at[p], gd.at[p])

        ones_, twos = tile_pieces(1), tile_pieces(2)
        tile_loads(0, True)
        for t in range(PIECES):
            tile_loads(t, False)

            @pl.loop(0, seq // BLK)
            def _(r):
                rows = rows_at(r * BLK, BLK)
                a = n2[rows, :]
                g = mm(a, wg[...])
                u = mm(a, wu[...])
                ag = mm_nt(din[rows, :], wd[...])
                sig = jax.nn.sigmoid(g)
                gs_ = g * sig
                av = (gs_ * u).astype(BF16)
                act[t, rows, :] = av
                gv = (ag * u * (sig + gs_ * (1.0 - sig))).astype(BF16)
                uv = (ag * gs_).astype(BF16)
                for p in range(2):
                    gu_rows[rows, 2 * p * TILE : (2 * p + 1) * TILE] = gv[:, p * TILE : (p + 1) * TILE]
                    gu_rows[rows, (2 * p + 1) * TILE : (2 * p + 2) * TILE] = uv[:, p * TILE : (p + 1) * TILE]
                dn = mm_nt(gv, wg[...]) + mm_nt(uv, wu[...])
                do = mm(av, wd[...])
                if t == 0:
                    acc_n[rows, :] = dn
                    acc_o[rows, :] = do
                else:
                    acc_n[rows, :] += dn
                    acc_o[rows, :] += do

            if t == 0:
                for n in twos:
                    first(n)
                second(twos[0])
            if t == 2:
                load_plane(0)
            if t == 1:
                for n in twos:
                    third(n)
                tile_loads(2, True)

            @pl.loop(0, width // BLK)
            def _(r):
                cols = pl.ds(pl.multiple_of(r * BLK, BLK), BLK)
                o = mm_tn(n2[:, cols], gu_rows[...]).astype(BF16)
                for p in range(2):
                    grads[t][p, cols, :] = o[:, 2 * p * TILE : 2 * (p + 1) * TILE]

            if t == 1:
                add_diag(0)
            begin(t)
            if t == 2:
                add_plane(0)
            if t == 0:
                second(twos[1])
                second(twos[2])
                for n in ones_:
                    third(n)
                tile_loads(1, True)

        @pl.loop(0, half // BLK)
        def _(r):
            rows = rows_at(r * BLK, BLK)
            give[0, rows, :] = acc_n[rows_at(other_at + r * BLK, BLK), :].astype(BF16)
            give[1, rows, :] = acc_o[rows_at(other_at + r * BLK, BLK), :].astype(BF16)

        trade(0).start()
        trade(1).start()
        for w in (DA_, DB_):
            n = width // 2
            for p in range(2):
                @pl.loop(0, n // BLK)
                def _(r):
                    cols = pl.ds(pl.multiple_of(r * BLK, BLK), BLK)
                    come = pl.ds(pl.multiple_of((w - DA_) * n + r * BLK, BLK), BLK)
                    for k in range(PIECES):
                        rows = pl.ds(k * TILE, TILE)
                        grads[w][p, rows, cols] = mm_tn(act[k, :, p * TILE : (p + 1) * TILE], din[:, come]).astype(BF16)

            if w == DA_:
                add_diag(1)
            begin(w)
            if w == DB_:
                load_plane(1)
                load_outer(0)

        trade(0).wait_recv()
        trade(1).wait_recv()

        @pl.loop(0, half // step)
        def _(r):
            rows = rows_at(r * step, step)
            own = rows_at(own_at + r * step, step)
            h = hgrad[rows, :]
            obuf[rows, :] = (h + acc_o[own, :] + take[1, rows, :].astype(F32)).astype(BF16)
            ng = acc_n[own, :] + take[0, rows, :].astype(F32)
            sc = lax.rsqrt(jnp.mean(h * h, axis=-1, keepdims=True) + EPS)
            unit = h * sc
            acc_gain(8, ng * unit)
            e = ng * gain2_ref[...]
            hg = din[own, :].astype(F32) + sc * (e - unit * jnp.mean(e * unit, axis=-1, keepdims=True))
            hgrad[rows, :] = hg
            attn_in[own, :] = hg.astype(BF16)

        add_plane(1)
        add_outer(0)
        token_copies(0, obuf, oo, True)

    def acc_gain(at, v):
        s = jnp.sum(v, axis=0, keepdims=True)
        for k in range(width // 128):
            gain_out[at + k : at + k + 1, :] += s[:, k * 128 : (k + 1) * 128]

    pl.run_scoped(
        ffn,
        pltpu.VMEM((width, 2 * TILE), BF16), pltpu.VMEM((width, 2 * TILE), BF16), pltpu.VMEM((2 * TILE, width), BF16),
        pltpu.VMEM((seq, width), F32), pltpu.VMEM((seq, width), F32), pltpu.VMEM((PIECES, seq, 2 * TILE), BF16),
        pltpu.VMEM((seq, 4 * TILE), BF16),
    )

    def gain_copy(i):
        to = (mate, place.column(c, 2 * place.half + 1 - par), place.column(c, 2 - 2 * place.half + par), place.plane(1),
              place.plane(2))[i]
        return remote(gain_out, gain_in.at[i], gs.at[i], gr.at[i], to)

    def attn_swap():
        own = rows_at(own_at, half)
        return remote(attn_in.at[own], attn_in.at[own], ms.at[3], mr.at[3], mate)

    attn_swap().start()

    def attention(dos, dq, dk, dv, drow):
        def front(wo, att, linv):
            loads = [load(4, h_att, att), load(5, h_linv, linv)]
            for cp in loads:
                cp.start()
            weight_load(1, wo, True)
            for cp in loads:
                cp.wait()
            weight_load(1, wo, False)
            other = rows_at(other_at, half)
            remote(attn_in.at[other], attn_in.at[other], ms.at[3], mr.at[3], mate).wait_recv()

            @pl.loop(0, seq // BLK)
            def _(r):
                rows = rows_at(r * BLK, BLK)
                left = lax.broadcasted_iota(jnp.int32, (BLK, 128), 1) < 64
                for p in range(2):
                    ag = mm_nt(attn_in[rows, :], wo[p]).astype(BF16).astype(F32)
                    for s in range(2):
                        g = 2 * p + s
                        cols = slice(g * 128, (g + 1) * 128)
                        d = ag[:, s * 128 : (s + 1) * 128] * linv[rows, cols]
                        d0, d1 = jnp.where(left, d, 0.0).astype(BF16), jnp.where(left, 0.0, d).astype(BF16)
                        dos[g, 0, rows, :] = d0
                        dos[g, 1, rows, :] = d1
                        o = att[rows, cols].astype(F32)
                        one = jnp.ones((8, 128), BF16)
                        for k, dd in enumerate((d0, d1)):
                            prod = dd.astype(F32) * o
                            high = prod.astype(BF16)
                            low = (prod - high.astype(F32)).astype(BF16)
                            drow[g, k, :, rows] = mm_nt(one, high) + mm_nt(one, low)

            @pl.loop(0, width // BLK)
            def _(r):
                cols = pl.ds(pl.multiple_of(r * BLK, BLK), BLK)
                for p in range(2):
                    grads[O_][p, :, cols] = mm_tn(att[:, p * 256 : (p + 1) * 256], attn_in[:, cols]).astype(BF16)

            add_diag(2)
            begin(O_)
            load_column(0)
            load_outer(1)

        pl.run_scoped(
            front, pltpu.VMEM(go.shape, BF16), pltpu.VMEM(h_att.shape, BF16), pltpu.VMEM(h_linv.shape, F32),
        )
        def rest(q, k, v, mt, qk, rows_, wqkv):
            normed = din
            trade(1).wait_send()
            x = give.at[1]
            loads = [load(6, h_q, q), load(7, h_k, k), load(8, h_v, v)]
            later = [load(9, h_qk, qk), load(11, h_normed, normed)]
            for cp in loads + later:
                cp.start()
            weight_load(0, wqkv, True)
            fetch_load(0, x_ref, hx, x, True)
            for cp in loads:
                cp.wait()
            dq[...] = jnp.zeros(dq.shape, F32)
            todo = {
                0: [lambda: add_column(0), lambda: add_outer(1)],
                1: [lambda: add_diag(DA_)],
                2: [lambda: load_plane(2)],
                3: [lambda: add_plane(2), lambda: add_diag(DB_)],
            }
            for jb in range(seq // BLK):
                at = jb * BLK
                ni = seq - at
                keys = pl.ds(at, BLK)
                cols = pl.ds(at, ni)
                ki = lax.broadcasted_iota(jnp.int32, (BLK, ni), 0)
                qi = lax.broadcasted_iota(jnp.int32, (BLK, ni), 1)
                same = jnp.logical_and(ki < qi, cols_ref[keys, 1:] == rows_ref[:1, cols])
                mt[:, :ni] = jnp.where(jnp.logical_or(ki == qi, same), 1.0, 0.0).astype(F32)

                @pl.loop(0, 4)
                def _(g):
                    kb = k[g, keys, :]
                    qb = q[g, :, cols, :].reshape(2 * ni, 128)
                    db = dos[g, :, cols, :].reshape(2 * ni, 128)
                    m = mt[:, :ni]
                    e = jnp.exp(mm_nt(kb, qb)) * jnp.concatenate([m, m], axis=1)
                    dv[g, keys, :] = mm(e.astype(BF16), db)
                    dp = mm_nt(v[g, keys, :], db)
                    dr = jnp.concatenate([drow[g, 0, :1, cols], drow[g, 1, :1, cols]], axis=1)
                    ds = (e * (dp - dr)).astype(BF16)
                    dk[g, keys, :] = mm(ds, qb)
                    dqs = mm_tn(ds, kb)
                    left = lax.broadcasted_iota(jnp.int32, (ni, 128), 1) < 64
                    lanes = pl.ds(pl.multiple_of(g * 128, 128), 128)
                    dq[cols, lanes] += jnp.where(left, dqs[:ni], dqs[ni:])

                for f in todo[jb]:
                    f()
            for cp in later:
                cp.wait()
            weight_load(0, wqkv, False)
            fetch_load(0, x_ref, hx, x, False)

            @pl.loop(0, seq // BLK)
            def _(r):
                rows = rows_at(r * BLK, BLK)
                cos, sin = cos_ref[rows, :], sin_ref[rows, :]
                left = lax.broadcasted_iota(jnp.int32, (BLK, 128), 1) < 64

                def fold(ref, p):
                    a, b = ref[2 * p, rows, :], ref[2 * p + 1, rows, :]
                    return jnp.where(left, a + pltpu.roll(a, 64, 1), b + pltpu.roll(b, 64, 1))

                for p in range(2):
                    raw = qk[p, rows, :]
                    sc = lax.rsqrt(head_mean(raw * raw, ones_ref, 384) + EPS)
                    unit = raw * sc
                    parts = []
                    for s in range(3):
                        if s < 2:
                            v_ = dq[rows, (2 * p + s) * 128 : (2 * p + s + 1) * 128] * 0.125
                        else:
                            v_ = fold(dk, p)
                        v_ = v_.astype(BF16).astype(F32)
                        parts.append(v_ * cos - lane_swap(v_) * sin)
                    ng = jnp.concatenate(parts, axis=1)
                    gsum = jnp.sum(ng * unit, axis=0, keepdims=True)
                    qsum = gsum[:, :128] + gsum[:, 128:256]
                    ksum = gsum[:, 256:]
                    gain_out[16:17, :] += qsum
                    gain_out[17:18, :] += ksum
                    e = ng * gainqk_ref[...]
                    back = sc * (e - unit * head_mean(e * unit, ones_ref, 384))
                    rows_[p, rows, :384] = back.astype(BF16)
                    rows_[p, rows, 384:] = fold(dv, p).astype(BF16)

            def back_rows(start):
                at = rows_at(start, BLK)
                return mm_nt(rows_[0, at, :], wqkv[0]) + mm_nt(rows_[1, at, :], wqkv[1])

            trade(0).wait_send()

            @pl.loop(0, half // BLK)
            def _(r):
                give[0, rows_at(r * BLK, BLK), :] = back_rows(other_at + r * BLK).astype(BF16)

            trade(2).start()
            load_plane(DA_)
            add_diag(O_)
            trade(2).wait_recv()
            token_copies(0, obuf, oo, False)

            @pl.loop(0, half // BLK)
            def _(r):
                rows = rows_at(r * BLK, BLK)
                ng = back_rows(own_at + r * BLK) + take[0, rows, :].astype(F32)
                xs = x[rows, :].astype(F32)
                sc = lax.rsqrt(jnp.mean(xs * xs, axis=-1, keepdims=True) + EPS)
                unit = xs * sc
                acc_gain(0, ng * unit)
                e = ng * gain1_ref[...]
                ig = hgrad[rows, :] + sc * (e - unit * jnp.mean(e * unit, axis=-1, keepdims=True))
                obuf[rows, :] = ig.astype(BF16)

            token_copies(1, obuf, io, True)
            gain_copy(0).start()
            for p in range(2):
                @pl.loop(0, width // BLK)
                def _(r):
                    cols = pl.ds(pl.multiple_of(r * BLK, BLK), BLK)
                    grads[QKV_][p, cols, :] = mm_tn(normed[:, cols], rows_[p]).astype(BF16)

            begin(QKV_)
            add_plane(DA_)
            load_column(1)
            load_outer(2)

        pl.run_scoped(
            rest, V(h_q.shape, BF16), V(h_k.shape, BF16), V(h_v.shape, BF16), V((BLK, seq), F32), V(h_qk.shape, F32),
            V((2, seq, 512), BF16), V(gqkv.shape, BF16),
        )

    pl.run_scoped(
        attention, pltpu.VMEM(h_q.shape, BF16), pltpu.VMEM((seq, 512), F32), pltpu.VMEM((4, seq, 128), F32),
        pltpu.VMEM((4, seq, 128), F32), pltpu.VMEM((4, 2, 8, seq), F32),
    )
    def gain_step(i, go=True):
        gain_copy(i).wait()
        gain_out[...] += gain_in[i]
        if go:
            gain_copy(i + 1).start()

    add_column(1)
    gain_step(0)
    add_outer(2)
    load_plane(DB_)
    gain_step(1)
    load_outer(DA_)
    load_column(2)
    gain_step(2, False)
    add_plane(DB_)
    load_plane(O_)
    add_outer(DA_)
    add_column(2)
    add_diag(QKV_)
    gain_copy(3).start()
    add_plane(O_)
    load_outer(DB_)
    load_column(DA_)
    add_outer(DB_)
    add_column(DA_)
    load_outer(O_)
    load_plane(QKV_)
    gain_step(3)
    add_plane(QKV_)
    add_outer(O_)
    load_column(DB_)
    load_outer(QKV_)
    gain_step(4, False)
    add_column(DB_)
    add_outer(QKV_)
    load_column(O_)
    add_column(O_)
    load_column(QKV_)
    add_column(QKV_)
    release_last(O_)
    release_last(QKV_)
    for w in range(nw):
        finish(w)
    for n in range(len(pieces)):
        sent(n)
    fetch_copies(0, x_ref, hx, False)
    fetch_copies(1, ct_ref, hc, False)
    trade(2).wait_send()
    attn_swap().wait_send()
    token_copies(1, obuf, io, False)
    token_arrivals(0, obuf, oo)
    token_arrivals(1, obuf, io)


def layer(x, ct, shards, vectors):
    anywhere = pl.BlockSpec(memory_space=pl.ANY)
    vmem = pl.BlockSpec(memory_space=pltpu.VMEM)
    dma = pltpu.SemaphoreType.DMA
    SDS, V = jax.ShapeDtypeStruct, pltpu.VMEM
    seg, width = x.shape[1], x.shape[2]
    half, seq = 2 * seg, 4 * seg
    wqkv, wo, wg, wu, wd = shards
    sizes = [(width, 2 * TILE)] * 3 + [(wd.shape[0], width // 2)] * 2 + [(wo.shape[0], width), (width, wqkv.shape[1])]
    nw, pieces = 7, 2 + 3 * PIECES
    gains = (24, 128)
    results = [(width // 8, 256), (width // 8, 128), (width // 8, 128), (wo.shape[0] // 8, width)]
    results += [(width // 8, wg.shape[1])] * 2 + [(wd.shape[0] // 8, width)]
    held = [((half, width), BF16), ((half, width), BF16), ((seq, width), BF16), ((2, seq, 384), F32), ((4, 2, seq, 128), BF16),
            ((4, seq, 128), BF16), ((4, seq, 128), BF16), ((seq, 512), BF16), ((seq, 512), F32)]
    out_shape = (
        [SDS((2, seg, width), BF16)] * 2
        + [SDS(gains, F32)]
        + [SDS(r, F32) for r in results]
        + [SDS((2,) + s.shape, BF16) for s in shards]
        + [SDS(*h) for h in held]
        + [SDS((2, 2, 2, r // 8, n), BF16) for r, n in sizes]
        + [SDS((2, 2, r // 8, n), BF16) for r, n in sizes]
    )
    e_max, n_max = max(r // 8 for r, _ in sizes), max(n for _, n in sizes)
    out = pl.pallas_call(
        layer_kernel,
        out_shape=out_shape,
        in_specs=[anywhere] * 7 + [vmem] * len(vectors),
        out_specs=[anywhere] * 2 + [vmem] + [anywhere] * (len(out_shape) - 3),
        scratch_shapes=[V((2, r, n), BF16) for r, n in sizes]
        + [V((2, 2, r // 8, n), BF16) for r, n in sizes]
        + [
            V((2, 2, e_max, n_max), F32), V((2, half, width), BF16), V((2, half, width), BF16), V((half, width), BF16),
            V((half, width), F32), V((5,) + gains, F32), V((seq, width), BF16), V((seq, width), BF16),
        ]
        + [
            dma((2, 2)), dma((2, 2)), dma((2, 2)), dma((2, 2)), dma((2, 2)), dma((pieces, 2)), dma((pieces, 2)),
            dma((pieces, 2, 4)), dma((pieces, 2, 4)), dma((nw, 6)), dma((nw, 6)), dma((nw, 2)), dma((nw, 2)), dma((nw, 3)),
            dma((nw, 3)), dma((nw, 3)), dma((5,)), dma((5,)), dma((8,)), dma((8,)), dma((13,)), dma((5, 2)), dma((nw, 2, 2)),
            dma((nw, 2)), dma((9,)),
        ],
        compiler_params=pltpu.CompilerParams(collective_id=0, has_side_effects=True, vmem_limit_bytes=60 * 1024 * 1024),
        name="layer",
    )(x, ct, *shards, *vectors)
    return out[0], out[1], out[2], out[3:10]


def rope_tables(length, width):
    k = np.arange(width // 2)
    angles = np.arange(length)[:, None] * (THETA ** (-2.0 * k / width))[None]
    cos, sin = np.cos(angles), np.sin(angles)
    return (
        jnp.asarray(np.concatenate([cos] * 4, axis=1), F32),
        jnp.asarray(np.concatenate([-sin, sin] * 2, axis=1), F32),
    )


def per_device(n_dp, inputs, query_weight, key_weight, value_weight, out_weight, gate_weight, up_weight, down_weight,
               attn_gain, ffn_gain, query_gain, key_gain, cotangent, segment_ids, padding, row_count):
    slots, _, width = inputs.shape
    seq_len = segment_ids.shape[1]
    head_dim = query_gain.shape[0]
    nq, nk = query_weight.shape[1], key_weight.shape[1]
    z = lax.axis_index("tensor")
    c = lax.axis_index("dp") % 2
    groups = n_dp // 8

    alive_all = padding * (jnp.arange(slots)[:, None] < row_count[0]).astype(jnp.int32)
    code = (segment_ids + ALIVE * alive_all)[z % 2]
    code = jnp.where(c == z // 2, code, lax.ppermute(code, "dp", [(i, i ^ 1) for i in range(n_dp)]))
    segment, alive_row = code % ALIVE, code // ALIVE
    key_code = jnp.where(alive_row > 0, segment, -1)
    codes = jnp.stack([segment, key_code])

    qkv_shard = jnp.concatenate([query_weight, key_weight, value_weight], axis=1)
    cos, sin = rope_tables(seq_len, head_dim)
    gain_qk = jnp.concatenate([query_gain] * (nq // head_dim) + [key_gain] * (nk // head_dim))[None]
    lanes = np.arange(nq + nk) // head_dim
    ones = jnp.asarray(np.where(lanes[:, None] == lanes[None], 1.0 / head_dim, 0.0), BF16)
    gain1, gain2 = attn_gain[None], ffn_gain[None]
    outs, in_grad, gains, sums = layer(
        inputs, cotangent, (qkv_shard, out_weight, gate_weight, up_weight, down_weight),
        (codes.T, codes, gain1, gain2, gain_qk, cos, sin,
         ones),
    )
    if groups > 1:
        same = [[g * 8 + k for g in range(groups)] for k in range(8)]
        sums = [lax.psum_scatter(s, "dp", scatter_dimension=0, axis_index_groups=same, tiled=True) for s in sums]
        gains = lax.psum(gains, "dp", axis_index_groups=same)
    pair = gains[16:18, :head_dim] + gains[16:18, head_dim:]
    return (
        outs,
        in_grad.astype(F32),
        *sums,
        gains[:8].reshape(-1),
        gains[8:16].reshape(-1),
        pair[0],
        pair[1],
    )


def solution(mesh):
    return jax.shard_map(
        functools.partial(per_device, mesh.shape["dp"]),
        mesh=mesh,
        in_specs=(
            P("dp", "tensor", None),
            P(None, "tensor"),
            P(None, "tensor"),
            P(None, "tensor"),
            P("tensor", None),
            P(None, "tensor"),
            P(None, "tensor"),
            P("tensor", None),
            P(),
            P(),
            P(),
            P(),
            P("dp", "tensor", None),
            P("dp", None),
            P("dp", None),
            P("dp"),
        ),
        out_specs=(
            P("dp", "tensor", None),
            P("dp", "tensor", None),
            P("dp", "tensor"),
            P("dp", "tensor"),
            P("dp", "tensor"),
            P(("tensor", "dp"), None),
            P("dp", "tensor"),
            P("dp", "tensor"),
            P(("tensor", "dp"), None),
            P(),
            P(),
            P(),
            P(),
        ),
        check_vma=False,
    )
```
